512 devices in a mesh: gx: 16 (over z), gy: 4 (over x_hi, core), gz: 8 (over y, x_lo).
Axes of the slice: x: 4 (x_hi: 2, x_lo: 2; x = x_hi * 2 + x_lo), y: 4, z: 16, core: 2. Of those that a mesh axis runs over, the one named last changes fastest.
Arguments:
- populations_in: float32 [19, 64, 32, 1024], P(None, 'gx', 'gy', 'gz'), as said below
- relax_rates: float32 [15], replicated, may hold values from 0.8 to 1.9
- solid_mask: int32 [64, 32, 1024], P('gx', 'gy', 'gz'), may hold values 0 or 1
- noise_slabs: float32 [4, 3, 32, 1024], P(None, None, 'gy', 'gz'), may hold values from -6 to 6
- half_widths: int32 [3, 2], replicated, may hold values from 2 to 4
Outputs:
- populations: float32 [19, 64, 32, 1024], P(None, 'gx', 'gy', 'gz')
The draws below stay inside these ranges and needn't reach their ends.
Inputs may be any that keep to these rules, and one draw needn't show every extreme that they name: `solid_mask`: 1 marks a solid node. `populations_in`: each population lies between 0.75 and 1.25 times its lattice weight.
All inputs are finite; a program needn't handle non-finite values. No bound on the sum of `solid_mask` on one device may be relied on, other than what follows from the above.
Results may differ from the reference program's by a relative error of at most 0.0001.
Values sent between devices are 32-bit elements; how exact they have to be, the bound alone decides.
A program may use at most 128 MiB of HBM per device.

```python
import math
import jax
import jax.numpy as jnp
import numpy as np
from jax import lax

NONCONS = 15
FILT = 8
STEPS = 4
NX = 64
NY = 32
NZ = 1024


def draw_populations_in(key, part):
    weights = jnp.array([1.0 / 3.0] + [1.0 / 18.0] * 6 + [1.0 / 36.0] * 12, jnp.float32)
    factor = 1.0 + 0.1 * jnp.clip(jax.random.normal(key, (19, NX, NY, NZ), jnp.float32), -2.5, 2.5)
    return weights[:, None, None, None] * factor


def plant(values, stream_key, least, top_value):
    spot = [jax.random.randint(jax.random.fold_in(stream_key, axis), (), 0, length) for axis, length in enumerate(values.shape)]
    main_axis = values.shape.index(max(values.shape))
    next_to = spot[:main_axis] + [(spot[main_axis] + 1) % values.shape[main_axis]] + spot[main_axis + 1:]
    return values.at[tuple(spot)].set(least).at[tuple(next_to)].set(top_value)


def block_levels(key, shape, shards, smallest, high):
    def one(dim, shards_of):
        draws = jax.random.uniform(jax.random.fold_in(jax.random.fold_in(key, 6), dim), (shards_of,), jnp.float32, smallest / len(shards), high / len(shards))
        return jnp.repeat(jnp.exp(draws), shape[dim] // shards_of).reshape((-1,) + (1,) * (len(shape) - dim - 1))

    factor_of = one(*shards[0])
    for cut in shards[1:]:
        factor_of = factor_of * one(*cut)
    return factor_of


def bell_draw(stream_key, extent, width, reach, split=(), dtype=jnp.bfloat16):
    entries = width * jax.random.normal(stream_key, extent, jnp.float32)
    if split:
        entries = entries * block_levels(stream_key, extent, split, -0.22, 0.18)
    return jnp.clip(entries, -reach, reach).astype(dtype)


def setup_inputs(seed: int = 0) -> dict:
    seeds = jax.random.split(jax.random.key(seed), 6)
    populations_in = draw_populations_in(jax.random.fold_in(seeds[5], 71), 0)
    relax_rates = jnp.clip(jnp.exp(jax.random.uniform(seeds[1], (NONCONS,), jnp.float32, math.log(0.8), math.log(1.9))), 0.8, 1.9)
    solid_mask = plant((jax.random.randint(seeds[2], (NX, NY, NZ), 0, 10) < 1).astype(jnp.int32), jax.random.fold_in(seeds[2], 1), 0, 1)
    noise_slabs = bell_draw(seeds[3], (STEPS, 3, NY, NZ), 1.0, 6.0, ((2, 4), (3, 8)), jnp.float32)
    half_widths = plant(jax.random.randint(seeds[4], (3, 2), 2, 5), jax.random.fold_in(seeds[4], 1), 2, 4).astype(jnp.int32)
    return {"populations_in": populations_in, "relax_rates": relax_rates, "solid_mask": solid_mask, "noise_slabs": noise_slabs, "half_widths": half_widths}


def lattice():
    velocity = [(0, 0, 0), (1, 0, 0), (-1, 0, 0), (0, 1, 0), (0, -1, 0), (0, 0, 1), (0, 0, -1), (1, 1, 0), (-1, -1, 0), (1, -1, 0), (-1, 1, 0), (1, 0, 1), (-1, 0, -1), (1, 0, -1), (-1, 0, 1), (0, 1, 1), (0, -1, -1), (0, 1, -1), (0, -1, 1)]
    return np.array(velocity) * 1.0

def lattice_weights():
    return np.array([1.0 / 3.0] + [1.0 / 18.0] * 6 + [1.0 / 36.0] * 12)

def opposite():
    return np.array([0] + [number + 1 if number % 2 == 1 else number - 1 for number in range(1, 19)])

def moment_basis():
    speeds = lattice()
    vel_x, vel_y, vel_z = (speeds[:, 0], speeds[:, 1], speeds[:, 2])
    square = vel_x * vel_x + vel_y * vel_y + vel_z * vel_z
    candidates = [np.ones(19), vel_x, vel_y, vel_z, square, vel_x * vel_x - vel_y * vel_y, vel_y * vel_y - vel_z * vel_z, vel_x * vel_y, vel_y * vel_z, vel_x * vel_z, vel_x * square, vel_y * square, vel_z * square, vel_x * (vel_y * vel_y - vel_z * vel_z), vel_y * (vel_z * vel_z - vel_x * vel_x), vel_z * (vel_x * vel_x - vel_y * vel_y), square * square, (vel_x * vel_x - vel_y * vel_y) * square, (vel_y * vel_y - vel_z * vel_z) * square]
    candidates = candidates + list(np.eye(19))
    basis_rows = []
    for vector in candidates:
        remain = np.array(vector) * 1.0
        for earlier in basis_rows:
            remain = remain - np.dot(earlier, remain) * earlier
        length = np.sqrt(np.dot(remain, remain))
        if length > 1e-08 and len(basis_rows) < 19:
            basis_rows.append(remain / length)
    return np.stack(basis_rows)

def collision_kernel(relax_rates):
    moment_rows = jnp.asarray(moment_basis(), jnp.float32)
    relax_full = jnp.concatenate([jnp.zeros((4,), jnp.float32), relax_rates])
    return jnp.einsum('ki,k,kj->ij', moment_rows, relax_full, moment_rows, precision=lax.Precision.HIGHEST)

def filter_taps(half_widths):
    offsets = jnp.arange(-FILT, FILT + 1).astype(jnp.float32)
    spread = half_widths.astype(jnp.float32)[..., None]
    weights_yz = jnp.exp(-jnp.pi * offsets * offsets / (2.0 * spread * spread))
    weights_yz = jnp.where(jnp.abs(offsets) <= 2.0 * spread, weights_yz, 0.0)
    return weights_yz / jnp.sqrt(lax.optimization_barrier(jnp.sum(weights_yz * weights_yz, -1, keepdims=True)))

def apply_filter(padded, weights_yz, span_len, height):
    along_span = jnp.zeros(padded.shape[:2] + (span_len, padded.shape[3]), jnp.float32)
    for offset in range(2 * FILT + 1):
        along_span = along_span + weights_yz[:, 0, offset][None, :, None, None] * padded[:, :, offset:offset + span_len, :]
    result = jnp.zeros(padded.shape[:2] + (span_len, height), jnp.float32)
    for offset in range(2 * FILT + 1):
        result = result + weights_yz[:, 1, offset][None, :, None, None] * along_span[:, :, :, offset:offset + height]
    return result

def equilibrium(density, vel_field):
    speeds = jnp.asarray(lattice(), jnp.float32)
    weights = jnp.asarray(lattice_weights(), jnp.float32)
    projection = jnp.einsum('qa,a...->q...', speeds, vel_field, precision=lax.Precision.HIGHEST)
    speed_sq = lax.optimization_barrier(jnp.sum(vel_field * vel_field, 0))
    shape = (19,) + (1,) * density.ndim
    return weights.reshape(shape) * density[None] * (1.0 + 3.0 * projection + 4.5 * projection * projection - 1.5 * speed_sq[None])

def collide(populations, solid_mask, kernel):
    speeds = jnp.asarray(lattice(), jnp.float32)
    density = lax.optimization_barrier(jnp.sum(populations, 0))
    momentum = jnp.einsum('qa,q...->a...', speeds, populations, precision=lax.Precision.HIGHEST)
    vel_field = momentum / density[None]
    balance = equilibrium(density, vel_field)
    relaxed = populations - jnp.einsum('ij,j...->i...', kernel, populations - balance, precision=lax.Precision.HIGHEST)
    bounced = jnp.stack([populations[int(which)] for which in opposite()])
    return jnp.where(solid_mask[None] > 0, bounced, relaxed)

def inlet_velocity(turbulence_step):
    return jnp.stack([0.05 + 0.05 * turbulence_step[0], 0.05 * turbulence_step[1], 0.05 * turbulence_step[2]])

def reference(populations_in, relax_rates, solid_mask, noise_slabs, half_widths):
    kernel = collision_kernel(relax_rates)
    weights_yz = filter_taps(half_widths)
    padded = jnp.pad(noise_slabs, ((0, 0), (0, 0), (FILT, FILT), (FILT, FILT)), mode='wrap')
    turbulence = apply_filter(padded, weights_yz, NY, NZ)
    speeds = lattice()
    populations = populations_in
    for turn in range(STEPS):
        post = collide(populations, solid_mask, kernel)
        layers = []
        for which in range(19):
            layers.append(jnp.roll(post[which], (int(speeds[which, 0]), int(speeds[which, 1]), int(speeds[which, 2])), axis=(0, 1, 2)))
        populations = jnp.stack(layers)
        inflow = equilibrium(jnp.ones((NY, NZ), jnp.float32), inlet_velocity(turbulence[turn]))
        populations = populations.at[:, 0].set(inflow)
    return populations
```

```python
import functools
import itertools

import jax
import jax.numpy as jnp
from jax import lax
from jax.experimental import pallas as pl
from jax.experimental.pallas import tpu as pltpu
from jax.sharding import PartitionSpec as P

MESH = pl.DeviceIdType.MESH
AXES = ("gx", "gy", "gz")
FILT = 8
STEPS = 4
NX, NY, NZ = 4, 8, 128
VELOCITY = [
    (0, 0, 0),
    (1, 0, 0),
    (-1, 0, 0),
    (0, 1, 0),
    (0, -1, 0),
    (0, 0, 1),
    (0, 0, -1),
    (1, 1, 0),
    (-1, -1, 0),
    (1, -1, 0),
    (-1, 1, 0),
    (1, 0, 1),
    (-1, 0, -1),
    (1, 0, -1),
    (-1, 0, 1),
    (0, 1, 1),
    (0, -1, -1),
    (0, 1, -1),
    (0, -1, 1),
]
OPPOSITE = [0] + [q + 1 if q % 2 == 1 else q - 1 for q in range(1, 19)]
ORDER = sorted(range(19), key=lambda q: -VELOCITY[q][0])
PLACE = [ORDER.index(q) for q in range(19)]
RANK_Y = {
    q: [p for p in range(19) if VELOCITY[p][1] == VELOCITY[q][1]].index(q) for q in range(19)
}
RANK_Z = {
    q: [p for p in range(19) if VELOCITY[p][2] == VELOCITY[q][2]].index(q) for q in range(19)
}
NEIGHBOURS = sorted(
    (d for d in itertools.product((-1, 0, 1), repeat=3) if 1 <= sum(map(abs, d)) <= 2),
    key=lambda d: -sum(map(abs, d)),
)
ACROSS = [d for d in itertools.product((0,), (-1, 0, 1), (-1, 0, 1)) if any(d)]


def way(step):
    return 0 if step > 0 else 1


def neighbour(here, counts, offset):
    return tuple(
        lax.rem(place + step + count, count) if step else place
        for place, step, count in zip(here, offset, counts)
    )


def collide(f, solid, rate):
    total = {q: f[q] + f[q + 1] for q in range(1, 19, 2)}
    apart = {q: f[q] - f[q + 1] for q in range(1, 19, 2)}
    p_xy, p_xz, p_yz = total[7] + total[9], total[11] + total[13], total[15] + total[17]
    q_xy, q_xz, q_yz = total[7] - total[9], total[11] - total[13], total[15] - total[17]
    a_xy, b_xy = apart[7] + apart[9], apart[7] - apart[9]
    a_xz, b_xz = apart[11] + apart[13], apart[11] - apart[13]
    a_yz, b_yz = apart[15] + apart[17], apart[15] - apart[17]
    axis_sum = total[1] + total[3] + total[5]
    edge_sum = p_xy + p_xz + p_yz
    rho = f[0] + axis_sum + edge_sum
    far_x, far_y, far_z = a_xy + a_xz, b_xy + a_yz, b_xz + b_yz
    j_x, j_y, j_z = apart[1] + far_x, apart[3] + far_y, apart[5] + far_z
    inverse = 1.0 / rho
    u_x, u_y, u_z = j_x * inverse, j_y * inverse, j_z * inverse
    xx, yy, zz = j_x * u_x, j_y * u_y, j_z * u_z
    square = xx + yy + zz
    normal_xy, normal_z = xx - yy, 2.0 * zz - xx - yy

    def relax(which, norm, value):
        return (rate[which] * (1.0 / norm)) * value

    axis_xy, edge_xy = total[1] - total[3], p_xz - p_yz
    axis_z = 2.0 * total[5] - total[1] - total[3]
    edge_z = p_xz + p_yz - 2.0 * p_xy
    m4 = relax(0, 2394.0, 8.0 * edge_sum - 11.0 * axis_sum - 30.0 * f[0] + 11.0 * rho - 19.0 * square)
    m5 = relax(1, 12.0, axis_xy + edge_xy - normal_xy)
    m6 = relax(2, 36.0, axis_z + edge_z - normal_z)
    m7 = relax(3, 4.0, q_xy - j_x * u_y)
    m8 = relax(4, 4.0, q_yz - j_y * u_z)
    m9 = relax(5, 4.0, q_xz - j_x * u_z)
    m10 = relax(6, 40.0, far_x - 4.0 * apart[1] + (2.0 / 3.0) * j_x)
    m11 = relax(7, 40.0, far_y - 4.0 * apart[3] + (2.0 / 3.0) * j_y)
    m12 = relax(8, 40.0, far_z - 4.0 * apart[5] + (2.0 / 3.0) * j_z)
    m13 = relax(9, 8.0, a_xy - a_xz)
    m14 = relax(10, 8.0, a_yz - b_xy)
    m15 = relax(11, 8.0, b_xz - b_yz)
    m16 = relax(12, 252.0, 12.0 * f[0] - 4.0 * axis_sum + edge_sum - 3.0 * rho + 5.5 * square)
    m17 = relax(13, 24.0, edge_xy - 2.0 * axis_xy + 0.5 * normal_xy)
    m18 = relax(14, 72.0, edge_z - 2.0 * axis_z + 0.5 * normal_z)

    axis_base = -11.0 * m4 - 4.0 * m16
    edge_base = 8.0 * m4 + m16
    v5, v6 = m5 - 2.0 * m17, m6 - 2.0 * m18
    w5, w6 = m5 + m17, m6 + m18
    e_xy, e_xz, e_yz = edge_base - 2.0 * w6, edge_base + w5 + w6, edge_base - w5 + w6
    even = {
        1: axis_base + v5 - v6,
        3: axis_base - v5 - v6,
        5: axis_base + 2.0 * v6,
        7: e_xy + m7,
        9: e_xy - m7,
        11: e_xz + m9,
        13: e_xz - m9,
        15: e_yz + m8,
        17: e_yz - m8,
    }
    s_xy, t_xy = m10 + m13, m11 - m14
    s_xz, t_xz = m10 - m13, m12 + m15
    s_yz, t_yz = m11 + m14, m12 - m15
    odd = {
        1: -4.0 * m10,
        3: -4.0 * m11,
        5: -4.0 * m12,
        7: s_xy + t_xy,
        9: s_xy - t_xy,
        11: s_xz + t_xz,
        13: s_xz - t_xz,
        15: s_yz + t_yz,
        17: s_yz - t_yz,
    }
    post = [f[0] + 30.0 * m4 - 12.0 * m16]
    for q in range(1, 19, 2):
        post.append(f[q] - even[q] - odd[q])
        post.append(f[q + 1] - even[q] + odd[q])
    return [jnp.where(solid, f[OPPOSITE[q]], post[q]) for q in range(19)]


def inflow(turbulence):
    u = [0.05 + 0.05 * turbulence[0], 0.05 * turbulence[1], 0.05 * turbulence[2]]
    speed = 1.0 - 1.5 * (u[0] * u[0] + u[1] * u[1] + u[2] * u[2])
    result = []
    for q in range(19):
        weight = (1.0 / 3.0, 1.0 / 18.0, 1.0 / 36.0)[sum(map(abs, VELOCITY[q]))]
        along = None
        for step, part in zip(VELOCITY[q], u):
            if step:
                part = part if step > 0 else -part
                along = part if along is None else along + part
        result.append(weight * (speed if along is None else speed + along * (3.0 + 4.5 * along)))
    return result


def tap(offset, half_width):
    spread = half_width.astype(jnp.float32)
    reach = offset.astype(jnp.float32)
    value = jnp.exp(reach * reach * (-jnp.pi / (2.0 * (spread * spread))))
    return jnp.where(jnp.abs(reach) <= 2.0 * spread, value, 0.0)


def tap_norm(half_width):
    offset = lax.broadcasted_iota(jnp.int32, (8, 128), 1) - FILT
    value = jnp.where(offset <= FILT, tap(offset, half_width), 0.0)
    return 1.0 / jnp.sqrt(jnp.sum(value * value, axis=1, keepdims=True))[0:1]


def kernel(
    counts,
    f_hbm,
    rate_hbm,
    solid_hbm,
    noise_hbm,
    width_hbm,
    out,
    f_in,
    rate,
    solid,
    noise,
    width,
    post,
    send_y,
    send_z,
    from_y,
    from_z,
    from_yz,
    filter_y,
    filter_z,
    turbulence,
    load_sem,
    send_sem,
    recv_sem,
    noise_send,
    noise_recv,
):
    here = tuple(lax.axis_index(axis) for axis in AXES)
    at_inlet = here[0] == 0

    barrier = pltpu.get_barrier_semaphore()
    for offset in NEIGHBOURS:
        pl.semaphore_signal(
            barrier, inc=1, device_id=neighbour(here, counts, offset), device_id_type=MESH
        )

    loads = [
        pltpu.make_async_copy(f_hbm, f_in, load_sem.at[0]),
        pltpu.make_async_copy(rate_hbm, rate, load_sem.at[1]),
        pltpu.make_async_copy(solid_hbm, solid, load_sem.at[2]),
        pltpu.make_async_copy(noise_hbm, noise.at[1, 1], load_sem.at[3]),
        pltpu.make_async_copy(width_hbm, width, load_sem.at[4]),
    ]
    for load in loads:
        load.start()

    row = lax.broadcasted_iota(jnp.int32, (NY, NZ), 0)
    lane = lax.broadcasted_iota(jnp.int32, (NY, NZ), 1)

    def face_copies(slot):
        copies = []
        for number, offset in enumerate(NEIGHBOURS):
            dx, dy, dz = offset
            side = 0 if dx > 0 else 2 if dx < 0 else 1
            edge = NX - 1 if dx > 0 else 0
            if dx and not dy and not dz:
                group = pl.ds(0, 5) if dx > 0 else pl.ds(14, 5)
                source = post.at[slot, 1 + edge, group]
                target = post.at[slot, 0 if dx > 0 else NX + 1, group]
            elif dy and not dx and not dz:
                source = send_y.at[slot, way(dy)]
                target = from_y.at[slot, 1, way(dy)]
            elif dz and not dy:
                source = send_z.at[slot, way(dz)]
                target = from_z.at[slot, side, way(dz)]
            elif dx and dy:
                rank = RANK_Y[VELOCITY.index(offset)]
                source = send_y.at[slot, way(dy), edge, pl.ds(rank, 1)]
                target = from_y.at[slot, side, way(dy), edge, pl.ds(rank, 1)]
            else:
                source = send_z.at[slot, way(dz), pl.ds(NY - 1 if dy > 0 else 0, 1)]
                target = from_yz.at[slot, way(dy), way(dz), pl.ds(0, 1)]
            copies.append(
                pltpu.make_async_remote_copy(
                    src_ref=source,
                    dst_ref=target,
                    send_sem=send_sem.at[slot, number],
                    recv_sem=recv_sem.at[slot, number],
                    device_id=neighbour(here, counts, offset),
                    device_id_type=MESH,
                )
            )
        return copies

    def noise_copies(step):
        copies = []
        for number, offset in enumerate(ACROSS):
            block = pl.ds(step, 1)
            copies.append(
                pltpu.make_async_remote_copy(
                    src_ref=noise.at[1, 1, block],
                    dst_ref=noise.at[1 - offset[1], 1 - offset[2], block],
                    send_sem=noise_send.at[step, number],
                    recv_sem=noise_recv.at[step, number],
                    device_id=neighbour(here, counts, offset),
                    device_id_type=MESH,
                )
            )
        return copies

    def collide_plane(f, x, slot):
        result = collide(f, solid[x] > 0, [rate[k] for k in range(15)])
        for q in range(19):
            post[slot, x + 1, PLACE[q]] = result[q]
            step_y, step_z = VELOCITY[q][1:]
            if step_y:
                edge = NY - 1 if step_y > 0 else 0
                send_y[slot, way(step_y), x, RANK_Y[q] : RANK_Y[q] + 1] = result[q][edge : edge + 1]
        for step_z in (1, -1):
            packed = send_z[slot, way(step_z)]
            for q in range(19):
                if VELOCITY[q][2] == step_z:
                    mine = x * 8 + RANK_Z[q]
                    moved = pltpu.roll(result[q], mine + 1 if step_z > 0 else mine, 1)
                    packed = jnp.where(lane == mine, moved, packed)
            send_z[slot, way(step_z)] = packed

    def stream_plane(x, slot):
        result = []
        for q in range(19):
            step_x, step_y, step_z = VELOCITY[q]
            source = x - step_x
            value = post[slot, source + 1, PLACE[q]]
            if step_x:
                side = (source + 4) // 4
                source = source + 4 - 4 * side
            else:
                side = 1
            edge_y = 0 if step_y > 0 else NY - 1
            edge_z = 0 if step_z > 0 else NZ - 1
            line = None
            if step_y:
                line = from_y[slot, side, way(step_y), source, RANK_Y[q] : RANK_Y[q] + 1]
                line = jnp.broadcast_to(line, (NY, NZ))
            if step_z:
                turn = edge_z + 128 - (source * 8 + RANK_Z[q])
                turn = jnp.where(turn >= 128, turn - 128, turn)
                spin = 1 if step_z > 0 else NZ - 1
                value = jnp.where(
                    lane == edge_z,
                    pltpu.roll(from_z[slot, side, way(step_z)], turn, 1),
                    pltpu.roll(value, spin, 1),
                )
                if step_y:
                    point = from_yz[slot, way(step_y), way(step_z), 0:1]
                    point = jnp.broadcast_to(point, (NY, NZ))
                    line = jnp.where(
                        lane == edge_z, pltpu.roll(point, turn, 1), pltpu.roll(line, spin, 1)
                    )
            if step_y:
                spin = 1 if step_y > 0 else NY - 1
                value = jnp.where(row == edge_y, line, pltpu.roll(value, spin, 0))
            result.append(value)
        return result

    def inlet_plane(step, x, f):
        flow = inflow([turbulence[step, a] for a in range(3)])
        here_too = jnp.logical_and(at_inlet, x == 0)
        return [jnp.where(here_too, flow[q], f[q]) for q in range(19)]

    def filter_step(step):
        for copy in noise_copies(step):
            copy.wait_recv()

        def component(a, carry):
            across = jnp.concatenate(
                [
                    jnp.dot(
                        filter_y[a],
                        jnp.concatenate([noise[b, c, step, a] for b in range(3)], 0),
                        precision=lax.Precision.HIGHEST,
                        preferred_element_type=jnp.float32,
                    )
                    for c in range(3)
                ],
                1,
            )
            turbulence[step, a] = jnp.dot(
                across,
                filter_z[a],
                precision=lax.Precision.HIGHEST,
                preferred_element_type=jnp.float32,
            )
            return carry

        lax.fori_loop(0, 3, component, 0)

    turbulence[...] = jnp.zeros_like(turbulence)
    send_z[...] = jnp.zeros_like(send_z)

    loads[0].wait()
    loads[1].wait()
    loads[2].wait()

    def first(x, carry):
        collide_plane([f_in[q, x] for q in range(19)], x, 0)
        return carry

    lax.fori_loop(0, NX, first, 0)
    loads[3].wait()
    loads[4].wait()

    @pl.when(at_inlet)
    def _():
        def component(a, carry):
            reach_y = lax.broadcasted_iota(jnp.int32, (NY, 3 * NY), 1) - lax.broadcasted_iota(
                jnp.int32, (NY, 3 * NY), 0
            )
            filter_y[a] = tap(reach_y - NY, width[a, 0]) * tap_norm(width[a, 0])
            reach_z = lax.broadcasted_iota(jnp.int32, (3 * NZ, NZ), 0) - lax.broadcasted_iota(
                jnp.int32, (3 * NZ, NZ), 1
            )
            filter_z[a] = tap(reach_z - NZ, width[a, 1]) * tap_norm(width[a, 1])
            return carry

        lax.fori_loop(0, 3, component, 0)

    pl.semaphore_wait(barrier, len(NEIGHBOURS))

    for copy in face_copies(0):
        copy.start()

    @pl.when(at_inlet)
    def _():
        for step in range(STEPS):
            for copy in noise_copies(step):
                copy.start()

    def middle(step, carry):
        @pl.when(at_inlet)
        def _():
            filter_step(step)

        for copy in face_copies(step):
            copy.wait_recv()

        def plane(x, carry):
            collide_plane(inlet_plane(step, x, stream_plane(x, step)), x, step + 1)
            return carry

        lax.fori_loop(0, NX, plane, 0)
        for copy in face_copies(step + 1):
            copy.start()
        return carry

    lax.fori_loop(0, STEPS - 1, middle, 0)

    @pl.when(at_inlet)
    def _():
        filter_step(STEPS - 1)

    for copy in face_copies(STEPS - 1):
        copy.wait_recv()

    def last(x, carry):
        f = inlet_plane(STEPS - 1, x, stream_plane(x, STEPS - 1))
        for q in range(19):
            out[q, x] = f[q]
        return carry

    lax.fori_loop(0, NX, last, 0)

    for step in range(STEPS):
        for copy in face_copies(step):
            copy.wait_send()

    @pl.when(at_inlet)
    def _():
        for step in range(STEPS):
            for copy in noise_copies(step):
                copy.wait_send()


def solution(mesh):
    counts = tuple(mesh.shape[axis] for axis in AXES)
    number = len(NEIGHBOURS)
    tile = (NY, NZ)

    def local(populations_in, relax_rates, solid_mask, noise_slabs, half_widths):
        return pl.pallas_call(
            functools.partial(kernel, counts),
            name="lattice_steps",
            out_shape=jax.ShapeDtypeStruct(populations_in.shape, jnp.float32),
            in_specs=[pl.BlockSpec(memory_space=pltpu.HBM)] * 5,
            out_specs=pl.BlockSpec(memory_space=pltpu.VMEM),
            scratch_shapes=[
                pltpu.VMEM((19, NX) + tile, jnp.float32),
                pltpu.SMEM((15,), jnp.float32),
                pltpu.VMEM((NX,) + tile, jnp.int32),
                pltpu.VMEM((3, 3, STEPS, 3) + tile, jnp.float32),
                pltpu.SMEM((3, 2), jnp.int32),
                pltpu.VMEM((STEPS, NX + 2, 19) + tile, jnp.float32),
                pltpu.VMEM((STEPS, 2, NX) + tile, jnp.float32),
                pltpu.VMEM((STEPS, 2) + tile, jnp.float32),
                pltpu.VMEM((STEPS, 3, 2, NX) + tile, jnp.float32),
                pltpu.VMEM((STEPS, 3, 2) + tile, jnp.float32),
                pltpu.VMEM((STEPS, 2, 2) + tile, jnp.float32),
                pltpu.VMEM((3, NY, 3 * NY), jnp.float32),
                pltpu.VMEM((3, 3 * NZ, NZ), jnp.float32),
                pltpu.VMEM((STEPS, 3) + tile, jnp.float32),
                pltpu.SemaphoreType.DMA((5,)),
                pltpu.SemaphoreType.DMA((STEPS, number)),
                pltpu.SemaphoreType.DMA((STEPS, number)),
                pltpu.SemaphoreType.DMA((STEPS, len(ACROSS))),
                pltpu.SemaphoreType.DMA((STEPS, len(ACROSS))),
            ],
            compiler_params=pltpu.CompilerParams(
                collective_id=0, has_side_effects=True, vmem_limit_bytes=24 << 20
            ),
        )(populations_in, relax_rates, solid_mask, noise_slabs, half_widths)

    return jax.shard_map(
        local,
        mesh=mesh,
        in_specs=(
            P(None, "gx", "gy", "gz"),
            P(),
            P("gx", "gy", "gz"),
            P(None, None, "gy", "gz"),
            P(),
        ),
        out_specs=P(None, "gx", "gy", "gz"),
        check_vma=False,
    )
```

```python
import functools
import itertools

import jax
import jax.numpy as jnp
from jax import lax
from jax.experimental import pallas as pl
from jax.experimental.pallas import tpu as pltpu
from jax.sharding import PartitionSpec as P

MESH = pl.DeviceIdType.MESH
AXES = ("gx", "gy", "gz")
FILT = 8
UNROLL = (4, 4, 4, 3)
STEPS = 4
NX, NY, NZ = 4, 8, 128
VELOCITY = [
    (0, 0, 0),
    (1, 0, 0),
    (-1, 0, 0),
    (0, 1, 0),
    (0, -1, 0),
    (0, 0, 1),
    (0, 0, -1),
    (1, 1, 0),
    (-1, -1, 0),
    (1, -1, 0),
    (-1, 1, 0),
    (1, 0, 1),
    (-1, 0, -1),
    (1, 0, -1),
    (-1, 0, 1),
    (0, 1, 1),
    (0, -1, -1),
    (0, 1, -1),
    (0, -1, 1),
]
OPPOSITE = [0] + [q + 1 if q % 2 == 1 else q - 1 for q in range(1, 19)]
ORDER = sorted(range(19), key=lambda q: -VELOCITY[q][0])
PLACE = [ORDER.index(q) for q in range(19)]
RANK_Y = {
    q: [p for p in range(19) if VELOCITY[p][1] == VELOCITY[q][1]].index(q) for q in range(19)
}
RANK_Z = {
    q: [p for p in range(19) if VELOCITY[p][2] == VELOCITY[q][2]].index(q) for q in range(19)
}
NEIGHBOURS = sorted(
    (d for d in itertools.product((-1, 0, 1), repeat=3) if 1 <= sum(map(abs, d)) <= 2),
    key=lambda d: -sum(map(abs, d)),
)
FACE_TILES = 2 * 5 + 2 * NX + 2 + 4 + 1
NOISE_TILES = 8 * 3
ACROSS = [d for d in itertools.product((0,), (-1, 0, 1), (-1, 0, 1)) if any(d)]


def way(step):
    return 0 if step > 0 else 1


def neighbour(here, counts, offset):
    return tuple(
        lax.rem(place + step + count, count) if step else place
        for place, step, count in zip(here, offset, counts)
    )


def collide(f, solid, rate):
    total = {q: f[q] + f[q + 1] for q in range(1, 19, 2)}
    apart = {q: f[q] - f[q + 1] for q in range(1, 19, 2)}
    p_xy, p_xz, p_yz = total[7] + total[9], total[11] + total[13], total[15] + total[17]
    q_xy, q_xz, q_yz = total[7] - total[9], total[11] - total[13], total[15] - total[17]
    a_xy, b_xy = apart[7] + apart[9], apart[7] - apart[9]
    a_xz, b_xz = apart[11] + apart[13], apart[11] - apart[13]
    a_yz, b_yz = apart[15] + apart[17], apart[15] - apart[17]
    axis_sum = total[1] + total[3] + total[5]
    edge_sum = p_xy + p_xz + p_yz
    rho = f[0] + axis_sum + edge_sum
    far_x, far_y, far_z = a_xy + a_xz, b_xy + a_yz, b_xz + b_yz
    j_x, j_y, j_z = apart[1] + far_x, apart[3] + far_y, apart[5] + far_z
    inverse = 1.0 / rho
    u_x, u_y, u_z = j_x * inverse, j_y * inverse, j_z * inverse
    xx, yy, zz = j_x * u_x, j_y * u_y, j_z * u_z
    square = xx + yy + zz
    normal_xy, normal_z = xx - yy, 2.0 * zz - xx - yy

    def relax(which, norm, value):
        return (rate[which] * (1.0 / norm)) * value

    axis_xy, edge_xy = total[1] - total[3], p_xz - p_yz
    axis_z = 2.0 * total[5] - total[1] - total[3]
    edge_z = p_xz + p_yz - 2.0 * p_xy
    m4 = relax(0, 2394.0, 8.0 * edge_sum - 11.0 * axis_sum - 30.0 * f[0] + 11.0 * rho - 19.0 * square)
    m5 = relax(1, 12.0, axis_xy + edge_xy - normal_xy)
    m6 = relax(2, 36.0, axis_z + edge_z - normal_z)
    m7 = relax(3, 4.0, q_xy - j_x * u_y)
    m8 = relax(4, 4.0, q_yz - j_y * u_z)
    m9 = relax(5, 4.0, q_xz - j_x * u_z)
    m10 = relax(6, 40.0, far_x - 4.0 * apart[1] + (2.0 / 3.0) * j_x)
    m11 = relax(7, 40.0, far_y - 4.0 * apart[3] + (2.0 / 3.0) * j_y)
    m12 = relax(8, 40.0, far_z - 4.0 * apart[5] + (2.0 / 3.0) * j_z)
    m13 = relax(9, 8.0, a_xy - a_xz)
    m14 = relax(10, 8.0, a_yz - b_xy)
    m15 = relax(11, 8.0, b_xz - b_yz)
    m16 = relax(12, 252.0, 12.0 * f[0] - 4.0 * axis_sum + edge_sum - 3.0 * rho + 5.5 * square)
    m17 = relax(13, 24.0, edge_xy - 2.0 * axis_xy + 0.5 * normal_xy)
    m18 = relax(14, 72.0, edge_z - 2.0 * axis_z + 0.5 * normal_z)

    axis_base = -11.0 * m4 - 4.0 * m16
    edge_base = 8.0 * m4 + m16
    v5, v6 = m5 - 2.0 * m17, m6 - 2.0 * m18
    w5, w6 = m5 + m17, m6 + m18
    e_xy, e_xz, e_yz = edge_base - 2.0 * w6, edge_base + w5 + w6, edge_base - w5 + w6
    even = {
        1: axis_base + v5 - v6,
        3: axis_base - v5 - v6,
        5: axis_base + 2.0 * v6,
        7: e_xy + m7,
        9: e_xy - m7,
        11: e_xz + m9,
        13: e_xz - m9,
        15: e_yz + m8,
        17: e_yz - m8,
    }
    s_xy, t_xy = m10 + m13, m11 - m14
    s_xz, t_xz = m10 - m13, m12 + m15
    s_yz, t_yz = m11 + m14, m12 - m15
    odd = {
        1: -4.0 * m10,
        3: -4.0 * m11,
        5: -4.0 * m12,
        7: s_xy + t_xy,
        9: s_xy - t_xy,
        11: s_xz + t_xz,
        13: s_xz - t_xz,
        15: s_yz + t_yz,
        17: s_yz - t_yz,
    }
    post = [f[0] + 30.0 * m4 - 12.0 * m16]
    for q in range(1, 19, 2):
        post.append(f[q] - even[q] - odd[q])
        post.append(f[q + 1] - even[q] + odd[q])
    return [jnp.where(solid, f[OPPOSITE[q]], post[q]) for q in range(19)]


def inflow(turbulence):
    u = [0.05 + 0.05 * turbulence[0], 0.05 * turbulence[1], 0.05 * turbulence[2]]
    speed = 1.0 - 1.5 * (u[0] * u[0] + u[1] * u[1] + u[2] * u[2])
    result = []
    for q in range(19):
        weight = (1.0 / 3.0, 1.0 / 18.0, 1.0 / 36.0)[sum(map(abs, VELOCITY[q]))]
        along = None
        for step, part in zip(VELOCITY[q], u):
            if step:
                part = part if step > 0 else -part
                along = part if along is None else along + part
        result.append(weight * (speed if along is None else speed + along * (3.0 + 4.5 * along)))
    return result


def tap(offset, half_width):
    spread = half_width.astype(jnp.float32)
    reach = offset.astype(jnp.float32)
    value = jnp.exp(reach * reach * (-jnp.pi / (2.0 * (spread * spread))))
    return jnp.where(jnp.abs(reach) <= 2.0 * spread, value, 0.0)


def tap_norm(half_width):
    offset = lax.broadcasted_iota(jnp.int32, (8, 128), 1) - FILT
    value = jnp.where(offset <= FILT, tap(offset, half_width), 0.0)
    return 1.0 / jnp.sqrt(jnp.sum(value * value, axis=1, keepdims=True))[0:1]


def kernel(
    counts,
    f_hbm,
    rate_hbm,
    solid_hbm,
    noise_hbm,
    width_hbm,
    out,
    f_in,
    rate,
    solid,
    noise,
    width,
    post,
    send_y,
    send_z,
    from_y,
    from_z,
    from_yz,
    filter_y,
    filter_z,
    turbulence,
    load_sem,
    send_sem,
    recv_sem,
    noise_recv,
    ruler,
):
    here = tuple(lax.axis_index(axis) for axis in AXES)
    at_inlet = here[0] == 0

    barrier = pltpu.get_barrier_semaphore()
    for offset in NEIGHBOURS:
        pl.semaphore_signal(
            barrier, inc=1, device_id=neighbour(here, counts, offset), device_id_type=MESH
        )

    loads = [pltpu.make_async_copy(rate_hbm, rate, load_sem.at[NX])]
    loads.append(pltpu.make_async_copy(solid_hbm, solid, load_sem.at[NX + 1]))
    for x in range(NX):
        plane = pl.ds(x, 1)
        loads.append(pltpu.make_async_copy(f_hbm.at[:, plane], f_in.at[:, plane], load_sem.at[x]))
    loads.append(pltpu.make_async_copy(width_hbm, width, load_sem.at[NX + 2]))
    loads.append(pltpu.make_async_copy(noise_hbm, noise.at[1, 1], load_sem.at[NX + 3]))
    for load in loads:
        load.start()

    row = lax.broadcasted_iota(jnp.int32, (NY, NZ), 0)
    lane = lax.broadcasted_iota(jnp.int32, (NY, NZ), 1)

    def await_bytes(tiles, semaphore):
        span = ruler.at[pl.ds(0, tiles)]
        pltpu.make_async_copy(span, span, semaphore).wait()

    def face_copies(slot):
        copies = []
        for offset in NEIGHBOURS:
            dx, dy, dz = offset
            side = 0 if dx > 0 else 2 if dx < 0 else 1
            edge = NX - 1 if dx > 0 else 0
            if dx and not dy and not dz:
                group = pl.ds(0, 5) if dx > 0 else pl.ds(14, 5)
                source = post.at[slot, 1 + edge, group]
                target = post.at[slot, 0 if dx > 0 else NX + 1, group]
            elif dy and not dx and not dz:
                source = send_y.at[slot, way(dy)]
                target = from_y.at[slot, 1, way(dy)]
            elif dz and not dy:
                source = send_z.at[slot, way(dz)]
                target = from_z.at[slot, side, way(dz)]
            elif dx and dy:
                rank = RANK_Y[VELOCITY.index(offset)]
                source = send_y.at[slot, way(dy), edge, pl.ds(rank, 1)]
                target = from_y.at[slot, side, way(dy), edge, pl.ds(rank, 1)]
            else:
                source = send_z.at[slot, way(dz), pl.ds(NY - 1 if dy > 0 else 0, 1)]
                target = from_yz.at[slot, way(dy), way(dz), pl.ds(0, 1)]
            copies.append(
                pltpu.make_async_remote_copy(
                    src_ref=source,
                    dst_ref=target,
                    send_sem=send_sem.at[0],
                    recv_sem=recv_sem.at[slot],
                    device_id=neighbour(here, counts, offset),
                    device_id_type=MESH,
                )
            )
        return copies

    def noise_copies(step):
        copies = []
        for offset in ACROSS:
            block = pl.ds(step, 1)
            copies.append(
                pltpu.make_async_remote_copy(
                    src_ref=noise.at[1, 1, block],
                    dst_ref=noise.at[1 - offset[1], 1 - offset[2], block],
                    send_sem=send_sem.at[1],
                    recv_sem=noise_recv.at[step],
                    device_id=neighbour(here, counts, offset),
                    device_id_type=MESH,
                )
            )
        return copies

    def collide_plane(f, x, slot):
        result = collide(f, solid[x] > 0, [rate[k] for k in range(15)])
        for q in range(19):
            post[slot, x + 1, PLACE[q]] = result[q]
            step_y, step_z = VELOCITY[q][1:]
            if step_y:
                edge = NY - 1 if step_y > 0 else 0
                send_y[slot, way(step_y), x, RANK_Y[q] : RANK_Y[q] + 1] = result[q][edge : edge + 1]
        for step_z in (1, -1):
            packed = send_z[slot, way(step_z)]
            for q in range(19):
                if VELOCITY[q][2] == step_z:
                    mine = x * 8 + RANK_Z[q]
                    moved = pltpu.roll(result[q], mine + 1 if step_z > 0 else mine, 1)
                    packed = jnp.where(lane == mine, moved, packed)
            send_z[slot, way(step_z)] = packed

    def stream_plane(x, slot):
        result = []
        for q in range(19):
            step_x, step_y, step_z = VELOCITY[q]
            source = x - step_x
            value = post[slot, source + 1, PLACE[q]]
            if step_x:
                side = (source + 4) // 4
                source = source + 4 - 4 * side
            else:
                side = 1
            edge_y = 0 if step_y > 0 else NY - 1
            edge_z = 0 if step_z > 0 else NZ - 1
            line = None
            if step_y:
                line = from_y[slot, side, way(step_y), source, RANK_Y[q] : RANK_Y[q] + 1]
                line = jnp.broadcast_to(line, (NY, NZ))
            if step_z:
                turn = edge_z + 128 - (source * 8 + RANK_Z[q])
                turn = jnp.where(turn >= 128, turn - 128, turn)
                spin = 1 if step_z > 0 else NZ - 1
                value = jnp.where(
                    lane == edge_z,
                    pltpu.roll(from_z[slot, side, way(step_z)], turn, 1),
                    pltpu.roll(value, spin, 1),
                )
                if step_y:
                    point = from_yz[slot, way(step_y), way(step_z), 0:1]
                    point = jnp.broadcast_to(point, (NY, NZ))
                    line = jnp.where(
                        lane == edge_z, pltpu.roll(point, turn, 1), pltpu.roll(line, spin, 1)
                    )
            if step_y:
                spin = 1 if step_y > 0 else NY - 1
                value = jnp.where(row == edge_y, line, pltpu.roll(value, spin, 0))
            result.append(value)
        return result

    def inlet_plane(step, x, f):
        flow = inflow([turbulence[step, a] for a in range(3)])
        here_too = jnp.logical_and(at_inlet, x == 0)
        return [jnp.where(here_too, flow[q], f[q]) for q in range(19)]

    def filter_step(step):
        await_bytes(NOISE_TILES, noise_recv.at[step])

        def component(a, carry):
            across = jnp.concatenate(
                [
                    jnp.dot(
                        filter_y[a],
                        jnp.concatenate([noise[b, c, step, a] for b in range(3)], 0),
                        precision=lax.Precision.HIGHEST,
                        preferred_element_type=jnp.float32,
                    )
                    for c in range(3)
                ],
                1,
            )
            turbulence[step, a] = jnp.dot(
                across,
                filter_z[a],
                precision=lax.Precision.HIGHEST,
                preferred_element_type=jnp.float32,
            )
            return carry

        lax.fori_loop(0, 3, component, 0, unroll=UNROLL[3])

    turbulence[...] = jnp.zeros_like(turbulence)
    send_z[...] = jnp.zeros_like(send_z)

    loads[0].wait()
    loads[1].wait()

    def first(x, carry):
        plane = pl.ds(x, 1)
        pltpu.make_async_copy(f_hbm.at[:, plane], f_in.at[:, plane], load_sem.at[x]).wait()
        collide_plane([f_in[q, x] for q in range(19)], x, 0)
        return carry

    lax.fori_loop(0, NX, first, 0, unroll=UNROLL[0])
    loads[NX + 2].wait()
    loads[NX + 3].wait()

    @pl.when(at_inlet)
    def _():
        def component(a, carry):
            reach_y = lax.broadcasted_iota(jnp.int32, (NY, 3 * NY), 1) - lax.broadcasted_iota(
                jnp.int32, (NY, 3 * NY), 0
            )
            filter_y[a] = tap(reach_y - NY, width[0, a]) * tap_norm(width[0, a])
            reach_z = lax.broadcasted_iota(jnp.int32, (3 * NZ, NZ), 0) - lax.broadcasted_iota(
                jnp.int32, (3 * NZ, NZ), 1
            )
            filter_z[a] = tap(reach_z - NZ, width[1, a]) * tap_norm(width[1, a])
            return carry

        lax.fori_loop(0, 3, component, 0)

    pl.semaphore_wait(barrier, len(NEIGHBOURS))

    for copy in face_copies(0):
        copy.start()

    @pl.when(at_inlet)
    def _():
        for step in range(STEPS):
            for copy in noise_copies(step):
                copy.start()

    def middle(step, carry):
        @pl.when(at_inlet)
        def _():
            filter_step(step)

        await_bytes(FACE_TILES, recv_sem.at[step])

        def plane(x, carry):
            collide_plane(inlet_plane(step, x, stream_plane(x, step)), x, step + 1)
            return carry

        lax.fori_loop(0, NX, plane, 0, unroll=UNROLL[1])
        for copy in face_copies(step + 1):
            copy.start()
        return carry

    lax.fori_loop(0, STEPS - 1, middle, 0)

    @pl.when(at_inlet)
    def _():
        filter_step(STEPS - 1)

    await_bytes(FACE_TILES, recv_sem.at[STEPS - 1])

    def last(x, carry):
        f = inlet_plane(STEPS - 1, x, stream_plane(x, STEPS - 1))
        for q in range(19):
            out[q, x] = f[q]
        return carry

    lax.fori_loop(0, NX, last, 0, unroll=UNROLL[2])

    await_bytes(STEPS * FACE_TILES, send_sem.at[0])

    @pl.when(at_inlet)
    def _():
        await_bytes(STEPS * NOISE_TILES, send_sem.at[1])


def solution(mesh):
    counts = tuple(mesh.shape[axis] for axis in AXES)
    tile = (NY, NZ)

    def local(populations_in, relax_rates, solid_mask, noise_slabs, half_widths):
        operands = (populations_in, relax_rates, solid_mask, noise_slabs, half_widths.T)
        return pl.pallas_call(
            functools.partial(kernel, counts),
            name="lattice_steps",
            out_shape=jax.ShapeDtypeStruct(populations_in.shape, jnp.float32),
            in_specs=[pl.BlockSpec(memory_space=pltpu.HBM)] * 5,
            out_specs=pl.BlockSpec(memory_space=pltpu.VMEM),
            scratch_shapes=[
                pltpu.VMEM((19, NX) + tile, jnp.float32),
                pltpu.SMEM((15,), jnp.float32),
                pltpu.VMEM((NX,) + tile, jnp.int32),
                pltpu.VMEM((3, 3, STEPS, 3) + tile, jnp.float32),
                pltpu.SMEM((2, 3), jnp.int32),
                pltpu.VMEM((STEPS, NX + 2, 19) + tile, jnp.float32),
                pltpu.VMEM((STEPS, 2, NX) + tile, jnp.float32),
                pltpu.VMEM((STEPS, 2) + tile, jnp.float32),
                pltpu.VMEM((STEPS, 3, 2, NX) + tile, jnp.float32),
                pltpu.VMEM((STEPS, 3, 2) + tile, jnp.float32),
                pltpu.VMEM((STEPS, 2, 2) + tile, jnp.float32),
                pltpu.VMEM((3, NY, 3 * NY), jnp.float32),
                pltpu.VMEM((3, 3 * NZ, NZ), jnp.float32),
                pltpu.VMEM((STEPS, 3) + tile, jnp.float32),
                pltpu.SemaphoreType.DMA((NX + 4,)),
                pltpu.SemaphoreType.DMA((2,)),
                pltpu.SemaphoreType.DMA((STEPS,)),
                pltpu.SemaphoreType.DMA((STEPS,)),
                pltpu.VMEM((STEPS * FACE_TILES,) + tile, jnp.float32),
            ],
            compiler_params=pltpu.CompilerParams(
                collective_id=0, has_side_effects=True, vmem_limit_bytes=24 << 20
            ),
        )(*[pltpu.with_memory_space_constraint(x, pltpu.HBM) for x in operands])

    return jax.shard_map(
        local,
        mesh=mesh,
        in_specs=(
            P(None, "gx", "gy", "gz"),
            P(),
            P("gx", "gy", "gz"),
            P(None, None, "gy", "gz"),
            P(),
        ),
        out_specs=P(None, "gx", "gy", "gz"),
        check_vma=False,
    )
```

```python
import functools
import itertools

import jax
import jax.numpy as jnp
from jax import lax
from jax.experimental import pallas as pl
from jax.experimental.pallas import tpu as pltpu
from jax.sharding import PartitionSpec as P

MESH = pl.DeviceIdType.MESH
AXES = ("gx", "gy", "gz")
FILT = 8
UNROLL = (4, 4, 4, 3)
STEPS = 4
NX, NY, NZ = 4, 8, 128
VELOCITY = [
    (0, 0, 0),
    (1, 0, 0),
    (-1, 0, 0),
    (0, 1, 0),
    (0, -1, 0),
    (0, 0, 1),
    (0, 0, -1),
    (1, 1, 0),
    (-1, -1, 0),
    (1, -1, 0),
    (-1, 1, 0),
    (1, 0, 1),
    (-1, 0, -1),
    (1, 0, -1),
    (-1, 0, 1),
    (0, 1, 1),
    (0, -1, -1),
    (0, 1, -1),
    (0, -1, 1),
]
OPPOSITE = [0] + [q + 1 if q % 2 == 1 else q - 1 for q in range(1, 19)]
ORDER = sorted(range(19), key=lambda q: -VELOCITY[q][0])
PLACE = [ORDER.index(q) for q in range(19)]
RANK_Y = {
    q: [p for p in range(19) if VELOCITY[p][1] == VELOCITY[q][1]].index(q) for q in range(19)
}
RANK_Z = {
    q: [p for p in range(19) if VELOCITY[p][2] == VELOCITY[q][2]].index(q) for q in range(19)
}
NEIGHBOURS = sorted(
    (d for d in itertools.product((-1, 0, 1), repeat=3) if 1 <= sum(map(abs, d)) <= 2),
    key=lambda d: -sum(map(abs, d)),
)
LEVEL, UP, DOWN = ([d for d in NEIGHBOURS if d[0] == step] for step in (0, 1, -1))
UP_ROWS = 5 * NY + 2 * NY + 2
FACE_ROWS = 2 * UP_ROWS + 2 * NX * NY + 2 * NY + 4
NOISE_ROWS = 8 * 3 * NY
ACROSS = [d for d in itertools.product((0,), (-1, 0, 1), (-1, 0, 1)) if any(d)]


def way(step):
    return 0 if step > 0 else 1


def neighbour(here, counts, offset):
    return tuple(
        lax.rem(place + step + count, count) if step else place
        for place, step, count in zip(here, offset, counts)
    )


def collide(f, solid, rate):
    total = {q: f[q] + f[q + 1] for q in range(1, 19, 2)}
    apart = {q: f[q] - f[q + 1] for q in range(1, 19, 2)}
    p_xy, p_xz, p_yz = total[7] + total[9], total[11] + total[13], total[15] + total[17]
    q_xy, q_xz, q_yz = total[7] - total[9], total[11] - total[13], total[15] - total[17]
    a_xy, b_xy = apart[7] + apart[9], apart[7] - apart[9]
    a_xz, b_xz = apart[11] + apart[13], apart[11] - apart[13]
    a_yz, b_yz = apart[15] + apart[17], apart[15] - apart[17]
    axis_sum = total[1] + total[3] + total[5]
    edge_sum = p_xy + p_xz + p_yz
    rho = f[0] + axis_sum + edge_sum
    far_x, far_y, far_z = a_xy + a_xz, b_xy + a_yz, b_xz + b_yz
    j_x, j_y, j_z = apart[1] + far_x, apart[3] + far_y, apart[5] + far_z
    inverse = 1.0 / rho
    u_x, u_y, u_z = j_x * inverse, j_y * inverse, j_z * inverse
    xx, yy, zz = j_x * u_x, j_y * u_y, j_z * u_z
    square = xx + yy + zz
    normal_xy, normal_z = xx - yy, 2.0 * zz - xx - yy

    def relax(which, norm, value):
        return (rate[which] * (1.0 / norm)) * value

    axis_xy, edge_xy = total[1] - total[3], p_xz - p_yz
    axis_z = 2.0 * total[5] - total[1] - total[3]
    edge_z = p_xz + p_yz - 2.0 * p_xy
    m4 = relax(0, 2394.0, 8.0 * edge_sum - 11.0 * axis_sum - 30.0 * f[0] + 11.0 * rho - 19.0 * square)
    m5 = relax(1, 12.0, axis_xy + edge_xy - normal_xy)
    m6 = relax(2, 36.0, axis_z + edge_z - normal_z)
    m7 = relax(3, 4.0, q_xy - j_x * u_y)
    m8 = relax(4, 4.0, q_yz - j_y * u_z)
    m9 = relax(5, 4.0, q_xz - j_x * u_z)
    m10 = relax(6, 40.0, far_x - 4.0 * apart[1] + (2.0 / 3.0) * j_x)
    m11 = relax(7, 40.0, far_y - 4.0 * apart[3] + (2.0 / 3.0) * j_y)
    m12 = relax(8, 40.0, far_z - 4.0 * apart[5] + (2.0 / 3.0) * j_z)
    m13 = relax(9, 8.0, a_xy - a_xz)
    m14 = relax(10, 8.0, a_yz - b_xy)
    m15 = relax(11, 8.0, b_xz - b_yz)
    m16 = relax(12, 252.0, 12.0 * f[0] - 4.0 * axis_sum + edge_sum - 3.0 * rho + 5.5 * square)
    m17 = relax(13, 24.0, edge_xy - 2.0 * axis_xy + 0.5 * normal_xy)
    m18 = relax(14, 72.0, edge_z - 2.0 * axis_z + 0.5 * normal_z)

    axis_base = -11.0 * m4 - 4.0 * m16
    edge_base = 8.0 * m4 + m16
    v5, v6 = m5 - 2.0 * m17, m6 - 2.0 * m18
    w5, w6 = m5 + m17, m6 + m18
    e_xy, e_xz, e_yz = edge_base - 2.0 * w6, edge_base + w5 + w6, edge_base - w5 + w6
    even = {
        1: axis_base + v5 - v6,
        3: axis_base - v5 - v6,
        5: axis_base + 2.0 * v6,
        7: e_xy + m7,
        9: e_xy - m7,
        11: e_xz + m9,
        13: e_xz - m9,
        15: e_yz + m8,
        17: e_yz - m8,
    }
    s_xy, t_xy = m10 + m13, m11 - m14
    s_xz, t_xz = m10 - m13, m12 + m15
    s_yz, t_yz = m11 + m14, m12 - m15
    odd = {
        1: -4.0 * m10,
        3: -4.0 * m11,
        5: -4.0 * m12,
        7: s_xy + t_xy,
        9: s_xy - t_xy,
        11: s_xz + t_xz,
        13: s_xz - t_xz,
        15: s_yz + t_yz,
        17: s_yz - t_yz,
    }
    post = [f[0] + 30.0 * m4 - 12.0 * m16]
    for q in range(1, 19, 2):
        post.append(f[q] - even[q] - odd[q])
        post.append(f[q + 1] - even[q] + odd[q])
    return [jnp.where(solid, f[OPPOSITE[q]], post[q]) for q in range(19)]


def inflow(turbulence):
    u = [0.05 + 0.05 * turbulence[0], 0.05 * turbulence[1], 0.05 * turbulence[2]]
    speed = 1.0 - 1.5 * (u[0] * u[0] + u[1] * u[1] + u[2] * u[2])
    result = []
    for q in range(19):
        weight = (1.0 / 3.0, 1.0 / 18.0, 1.0 / 36.0)[sum(map(abs, VELOCITY[q]))]
        along = None
        for step, part in zip(VELOCITY[q], u):
            if step:
                part = part if step > 0 else -part
                along = part if along is None else along + part
        result.append(weight * (speed if along is None else speed + along * (3.0 + 4.5 * along)))
    return result


def tap(offset, half_width):
    spread = half_width.astype(jnp.float32)
    reach = offset.astype(jnp.float32)
    value = jnp.exp(reach * reach * (-jnp.pi / (2.0 * (spread * spread))))
    return jnp.where(jnp.abs(reach) <= 2.0 * spread, value, 0.0)


def tap_norm(half_width):
    offset = lax.broadcasted_iota(jnp.int32, (8, 128), 1) - FILT
    value = jnp.where(offset <= FILT, tap(offset, half_width), 0.0)
    return 1.0 / jnp.sqrt(jnp.sum(value * value, axis=1, keepdims=True))[0:1]


def kernel(
    counts,
    f_hbm,
    rate_hbm,
    solid_hbm,
    noise_hbm,
    width_hbm,
    out,
    f_in,
    rate,
    solid,
    noise,
    width,
    post,
    send_y,
    send_z,
    from_y,
    from_z,
    from_yz,
    filter_y,
    filter_z,
    turbulence,
    load_sem,
    send_sem,
    recv_sem,
    recv_up,
    noise_recv,
    ready_sem,
    ruler,
):
    here = tuple(lax.axis_index(axis) for axis in AXES)
    at_inlet = here[0] == 0

    at_outlet = here[0] == counts[0] - 1
    barrier = pltpu.get_barrier_semaphore()

    def greet(offset, semaphore=barrier):
        pl.semaphore_signal(
            semaphore, inc=1, device_id=neighbour(here, counts, offset), device_id_type=MESH
        )

    for offset in LEVEL + DOWN:
        greet(offset)

    @pl.when(jnp.logical_not(at_outlet))
    def _():
        for offset in UP:
            greet(offset)

    loads = [pltpu.make_async_copy(rate_hbm, rate, load_sem.at[NX])]
    loads.append(pltpu.make_async_copy(solid_hbm, solid, load_sem.at[NX + 1]))
    for x in range(NX):
        plane = pl.ds(x, 1)
        loads.append(pltpu.make_async_copy(f_hbm.at[:, plane], f_in.at[:, plane], load_sem.at[x]))
    loads.append(pltpu.make_async_copy(width_hbm, width, load_sem.at[NX + 2]))
    loads.append(pltpu.make_async_copy(noise_hbm, noise.at[1, 1], load_sem.at[NX + 3]))
    for load in loads:
        load.start()

    row = lax.broadcasted_iota(jnp.int32, (NY, NZ), 0)
    lane = lax.broadcasted_iota(jnp.int32, (NY, NZ), 1)

    def await_rows(rows, semaphore):
        span = ruler.at[pl.ds(0, rows)]
        pltpu.make_async_copy(span, span, semaphore).wait()

    def face_copies(slot, offsets):
        copies = []
        for offset in offsets:
            dx, dy, dz = offset
            side = 0 if dx > 0 else 2 if dx < 0 else 1
            edge = NX - 1 if dx > 0 else 0
            if dx and not dy and not dz:
                group = pl.ds(0, 5) if dx > 0 else pl.ds(14, 5)
                source = post.at[slot, 1 + edge, group]
                target = post.at[slot, 0 if dx > 0 else NX + 1, group]
            elif dy and not dx and not dz:
                source = send_y.at[slot, way(dy)]
                target = from_y.at[slot, 1, way(dy)]
            elif dz and not dy:
                source = send_z.at[slot, way(dz)]
                target = from_z.at[slot, side, way(dz)]
            elif dx and dy:
                rank = RANK_Y[VELOCITY.index(offset)]
                source = send_y.at[slot, way(dy), edge, pl.ds(rank, 1)]
                target = from_y.at[slot, side, way(dy), edge, pl.ds(rank, 1)]
            else:
                source = send_z.at[slot, way(dz), pl.ds(NY - 1 if dy > 0 else 0, 1)]
                target = from_yz.at[slot, way(dy), way(dz), pl.ds(0, 1)]
            copies.append(
                pltpu.make_async_remote_copy(
                    src_ref=source,
                    dst_ref=target,
                    send_sem=send_sem.at[2 if dx > 0 else 0],
                    recv_sem=(recv_up if dx > 0 else recv_sem).at[slot],
                    device_id=neighbour(here, counts, offset),
                    device_id_type=MESH,
                )
            )
        return copies

    def send_faces(slot):
        for copy in face_copies(slot, LEVEL):
            copy.start()

        @pl.when(jnp.logical_not(at_outlet))
        def _():
            for copy in face_copies(slot, UP):
                copy.start()

        @pl.when(jnp.logical_not(at_inlet))
        def _():
            for copy in face_copies(slot, DOWN):
                copy.start()

        @pl.when(jnp.logical_and(at_inlet, slot > 0))
        def _():
            @pl.when(slot == 1)
            def _():
                pl.semaphore_wait(ready_sem, len(DOWN))
                for copy in face_copies(0, DOWN):
                    copy.start()

            for copy in face_copies(slot, DOWN):
                copy.start()

    def await_faces(slot):
        await_rows(FACE_ROWS - UP_ROWS, recv_sem.at[slot])

        @pl.when(jnp.logical_not(at_inlet))
        def _():
            await_rows(UP_ROWS, recv_up.at[slot])

    def noise_copies(step):
        copies = []
        for offset in ACROSS:
            block = pl.ds(step, 1)
            copies.append(
                pltpu.make_async_remote_copy(
                    src_ref=noise.at[1, 1, block],
                    dst_ref=noise.at[1 - offset[1], 1 - offset[2], block],
                    send_sem=send_sem.at[1],
                    recv_sem=noise_recv.at[step],
                    device_id=neighbour(here, counts, offset),
                    device_id_type=MESH,
                )
            )
        return copies

    def collide_plane(f, x, slot):
        result = collide(f, solid[x] > 0, [rate[k] for k in range(15)])
        for q in range(19):
            post[slot, x + 1, PLACE[q]] = result[q]
            step_y, step_z = VELOCITY[q][1:]
            if step_y:
                edge = NY - 1 if step_y > 0 else 0
                send_y[slot, way(step_y), x, RANK_Y[q] : RANK_Y[q] + 1] = result[q][edge : edge + 1]
        for step_z in (1, -1):
            packed = send_z[slot, way(step_z)]
            for q in range(19):
                if VELOCITY[q][2] == step_z:
                    mine = x * 8 + RANK_Z[q]
                    moved = pltpu.roll(result[q], mine + 1 if step_z > 0 else mine, 1)
                    packed = jnp.where(lane == mine, moved, packed)
            send_z[slot, way(step_z)] = packed

    def stream_plane(x, slot):
        result = []
        for q in range(19):
            step_x, step_y, step_z = VELOCITY[q]
            source = x - step_x
            value = post[slot, source + 1, PLACE[q]]
            if step_x:
                side = (source + 4) // 4
                source = source + 4 - 4 * side
            else:
                side = 1
            edge_y = 0 if step_y > 0 else NY - 1
            edge_z = 0 if step_z > 0 else NZ - 1
            line = None
            if step_y:
                line = from_y[slot, side, way(step_y), source, RANK_Y[q] : RANK_Y[q] + 1]
                line = jnp.broadcast_to(line, (NY, NZ))
            if step_z:
                turn = edge_z + 128 - (source * 8 + RANK_Z[q])
                turn = jnp.where(turn >= 128, turn - 128, turn)
                spin = 1 if step_z > 0 else NZ - 1
                value = jnp.where(
                    lane == edge_z,
                    pltpu.roll(from_z[slot, side, way(step_z)], turn, 1),
                    pltpu.roll(value, spin, 1),
                )
                if step_y:
                    point = from_yz[slot, way(step_y), way(step_z), 0:1]
                    point = jnp.broadcast_to(point, (NY, NZ))
                    line = jnp.where(
                        lane == edge_z, pltpu.roll(point, turn, 1), pltpu.roll(line, spin, 1)
                    )
            if step_y:
                spin = 1 if step_y > 0 else NY - 1
                value = jnp.where(row == edge_y, line, pltpu.roll(value, spin, 0))
            result.append(value)
        return result

    def inlet_plane(step, x, f):
        flow = inflow([turbulence[step, a] for a in range(3)])
        here_too = jnp.logical_and(at_inlet, x == 0)
        return [jnp.where(here_too, flow[q], f[q]) for q in range(19)]

    def filter_step(step):
        await_rows(NOISE_ROWS, noise_recv.at[step])

        def component(a, carry):
            across = jnp.concatenate(
                [
                    jnp.dot(
                        filter_y[a],
                        jnp.concatenate([noise[b, c, step, a] for b in range(3)], 0),
                        precision=lax.Precision.HIGHEST,
                        preferred_element_type=jnp.float32,
                    )
                    for c in range(3)
                ],
                1,
            )
            turbulence[step, a] = jnp.dot(
                across,
                filter_z[a],
                precision=lax.Precision.HIGHEST,
                preferred_element_type=jnp.float32,
            )
            return carry

        lax.fori_loop(0, 3, component, 0, unroll=UNROLL[3])

    turbulence[...] = jnp.zeros_like(turbulence)
    send_z[...] = jnp.zeros_like(send_z)

    loads[0].wait()
    loads[1].wait()

    def first(x, carry):
        plane = pl.ds(x, 1)
        pltpu.make_async_copy(f_hbm.at[:, plane], f_in.at[:, plane], load_sem.at[x]).wait()
        collide_plane([f_in[q, x] for q in range(19)], x, 0)
        return carry

    lax.fori_loop(0, NX, first, 0, unroll=UNROLL[0])
    loads[NX + 2].wait()
    loads[NX + 3].wait()

    @pl.when(at_inlet)
    def _():
        def component(a, carry):
            reach_y = lax.broadcasted_iota(jnp.int32, (NY, 3 * NY), 1) - lax.broadcasted_iota(
                jnp.int32, (NY, 3 * NY), 0
            )
            filter_y[a] = tap(reach_y - NY, width[0, a]) * tap_norm(width[0, a])
            reach_z = lax.broadcasted_iota(jnp.int32, (3 * NZ, NZ), 0) - lax.broadcasted_iota(
                jnp.int32, (3 * NZ, NZ), 1
            )
            filter_z[a] = tap(reach_z - NZ, width[1, a]) * tap_norm(width[1, a])
            return carry

        lax.fori_loop(0, 3, component, 0)

    pl.semaphore_wait(barrier, jnp.where(at_inlet, len(LEVEL) + len(UP), len(NEIGHBOURS)))

    @pl.when(at_outlet)
    def _():
        for offset in UP:
            greet(offset, ready_sem)

    send_faces(0)

    @pl.when(at_inlet)
    def _():
        for step in range(STEPS):
            for copy in noise_copies(step):
                copy.start()

    def middle(step, carry):
        @pl.when(at_inlet)
        def _():
            filter_step(step)

        await_faces(step)

        def plane(x, carry):
            collide_plane(inlet_plane(step, x, stream_plane(x, step)), x, step + 1)
            return carry

        lax.fori_loop(0, NX, plane, 0, unroll=UNROLL[1])
        send_faces(step + 1)
        return carry

    lax.fori_loop(0, STEPS - 1, middle, 0)

    @pl.when(at_inlet)
    def _():
        filter_step(STEPS - 1)

    await_faces(STEPS - 1)

    def last(x, carry):
        f = inlet_plane(STEPS - 1, x, stream_plane(x, STEPS - 1))
        for q in range(19):
            out[q, x] = f[q]
        return carry

    lax.fori_loop(0, NX, last, 0, unroll=UNROLL[2])

    await_rows(STEPS * (FACE_ROWS - UP_ROWS), send_sem.at[0])

    @pl.when(jnp.logical_not(at_outlet))
    def _():
        await_rows(STEPS * UP_ROWS, send_sem.at[2])

    @pl.when(at_inlet)
    def _():
        await_rows(STEPS * NOISE_ROWS, send_sem.at[1])


def solution(mesh):
    counts = tuple(mesh.shape[axis] for axis in AXES)
    tile = (NY, NZ)

    def local(populations_in, relax_rates, solid_mask, noise_slabs, half_widths):
        operands = (populations_in, relax_rates, solid_mask, noise_slabs, half_widths.T)
        return pl.pallas_call(
            functools.partial(kernel, counts),
            name="lattice_steps",
            out_shape=jax.ShapeDtypeStruct(populations_in.shape, jnp.float32),
            in_specs=[pl.BlockSpec(memory_space=pltpu.HBM)] * 5,
            out_specs=pl.BlockSpec(memory_space=pltpu.VMEM),
            scratch_shapes=[
                pltpu.VMEM((19, NX) + tile, jnp.float32),
                pltpu.SMEM((15,), jnp.float32),
                pltpu.VMEM((NX,) + tile, jnp.int32),
                pltpu.VMEM((3, 3, STEPS, 3) + tile, jnp.float32),
                pltpu.SMEM((2, 3), jnp.int32),
                pltpu.VMEM((STEPS, NX + 2, 19) + tile, jnp.float32),
                pltpu.VMEM((STEPS, 2, NX) + tile, jnp.float32),
                pltpu.VMEM((STEPS, 2) + tile, jnp.float32),
                pltpu.VMEM((STEPS, 3, 2, NX) + tile, jnp.float32),
                pltpu.VMEM((STEPS, 3, 2) + tile, jnp.float32),
                pltpu.VMEM((STEPS, 2, 2) + tile, jnp.float32),
                pltpu.VMEM((3, NY, 3 * NY), jnp.float32),
                pltpu.VMEM((3, 3 * NZ, NZ), jnp.float32),
                pltpu.VMEM((STEPS, 3) + tile, jnp.float32),
                pltpu.SemaphoreType.DMA((NX + 4,)),
                pltpu.SemaphoreType.DMA((3,)),
                pltpu.SemaphoreType.DMA((STEPS,)),
                pltpu.SemaphoreType.DMA((STEPS,)),
                pltpu.SemaphoreType.DMA((STEPS,)),
                pltpu.SemaphoreType.REGULAR,
                pltpu.VMEM((STEPS * FACE_ROWS, NZ), jnp.float32),
            ],
            compiler_params=pltpu.CompilerParams(
                collective_id=0, has_side_effects=True, vmem_limit_bytes=24 << 20
            ),
        )(*[pltpu.with_memory_space_constraint(x, pltpu.HBM) for x in operands])

    return jax.shard_map(
        local,
        mesh=mesh,
        in_specs=(
            P(None, "gx", "gy", "gz"),
            P(),
            P("gx", "gy", "gz"),
            P(None, None, "gy", "gz"),
            P(),
        ),
        out_specs=P(None, "gx", "gy", "gz"),
        check_vma=False,
    )
```

```python
import functools
import itertools

import jax
import jax.numpy as jnp
from jax import lax
from jax.experimental import pallas as pl
from jax.experimental.pallas import tpu as pltpu
from jax.sharding import PartitionSpec as P

MESH = pl.DeviceIdType.MESH
AXES = ("gx", "gy", "gz")
FILT = 8
STEPS = 4
NX, NY, NZ = 4, 8, 128
UNROLL = 6
VELOCITY = [
    (0, 0, 0),
    (1, 0, 0),
    (-1, 0, 0),
    (0, 1, 0),
    (0, -1, 0),
    (0, 0, 1),
    (0, 0, -1),
    (1, 1, 0),
    (-1, -1, 0),
    (1, -1, 0),
    (-1, 1, 0),
    (1, 0, 1),
    (-1, 0, -1),
    (1, 0, -1),
    (-1, 0, 1),
    (0, 1, 1),
    (0, -1, -1),
    (0, 1, -1),
    (0, -1, 1),
]
OPPOSITE = [0] + [q + 1 if q % 2 == 1 else q - 1 for q in range(1, 19)]
SOLID = 19
ORDER = sorted(range(20), key=lambda q: (tuple(-c for c in (VELOCITY + [(0, 0, 0)])[q][:2]), q))
PLACE = [ORDER.index(q) for q in range(20)]
WIDE = 2
HALVES = STEPS // WIDE
PLANES = NX + 2 * WIDE
PACKED = 3
NEIGHBOURS = sorted(
    (d for d in itertools.product((-1, 0, 1), repeat=3) if any(d)),
    key=lambda d: -sum(map(abs, d)),
)
LEVEL, UP, DOWN = ([d for d in NEIGHBOURS if d[0] == step] for step in (0, 1, -1))
ACROSS = [d for d in itertools.product((0,), (-1, 0, 1, 2), (-1, 0, 1)) if any(d)]
BEYOND = [d for d in ACROSS if d[1] == 2]


def pieces(offset):
    dx, dy, dz = offset
    rows = (0, NY) if not dy else (NY - WIDE, WIDE) if dy > 0 else (0, WIDE)
    if dz:
        return [rows]
    if dx > 0:
        return [(5, 1, 0, 15, 1, rows), (4, 1, 0, 5, 0, rows)]
    if dx < 0:
        return [(2, 1, 5, 15, 6, rows), (3, 1, 15, 5, 7, rows)]
    if dy > 0:
        return [(2, NX, 0, 12, 2, rows), (2, NX, 15, 4, 2, rows)]
    return [(2, NX, 1, 4, 2, rows), (2, NX, 8, 12, 2, rows)]


def rows_of(offsets):
    return sum(
        piece[1] * PACKED if len(piece) == 2 else piece[1] * piece[3] * piece[5][1]
        for offset in offsets
        for piece in pieces(offset)
    )


UP_ROWS = rows_of(UP)
OTHER_ROWS = rows_of(LEVEL + DOWN)
NOISE_ROWS = len(ACROSS) * 3 * NY


def neighbour(here, counts, offset):
    return tuple(
        lax.rem(place + step + count, count) if step else place
        for place, step, count in zip(here, offset, counts)
    )


def collide(f, solid, rate):
    total = {q: f[q] + f[q + 1] for q in range(1, 19, 2)}
    apart = {q: f[q] - f[q + 1] for q in range(1, 19, 2)}
    p_xy, p_xz, p_yz = total[7] + total[9], total[11] + total[13], total[15] + total[17]
    q_xy, q_xz, q_yz = total[7] - total[9], total[11] - total[13], total[15] - total[17]
    a_xy, b_xy = apart[7] + apart[9], apart[7] - apart[9]
    a_xz, b_xz = apart[11] + apart[13], apart[11] - apart[13]
    a_yz, b_yz = apart[15] + apart[17], apart[15] - apart[17]
    axis_sum = total[1] + total[3] + total[5]
    edge_sum = p_xy + p_xz + p_yz
    rho = f[0] + axis_sum + edge_sum
    far_x, far_y, far_z = a_xy + a_xz, b_xy + a_yz, b_xz + b_yz
    j_x, j_y, j_z = apart[1] + far_x, apart[3] + far_y, apart[5] + far_z
    inverse = 1.0 / rho
    u_x, u_y, u_z = j_x * inverse, j_y * inverse, j_z * inverse
    xx, yy, zz = j_x * u_x, j_y * u_y, j_z * u_z
    square = xx + yy + zz
    normal_xy, normal_z = xx - yy, 2.0 * zz - xx - yy

    def relax(which, norm, value):
        return (rate[which] * (1.0 / norm)) * value

    axis_xy, edge_xy = total[1] - total[3], p_xz - p_yz
    axis_z = 2.0 * total[5] - total[1] - total[3]
    edge_z = p_xz + p_yz - 2.0 * p_xy
    m4 = relax(0, 2394.0, 8.0 * edge_sum - 11.0 * axis_sum - 30.0 * f[0] + 11.0 * rho - 19.0 * square)
    m5 = relax(1, 12.0, axis_xy + edge_xy - normal_xy)
    m6 = relax(2, 36.0, axis_z + edge_z - normal_z)
    m7 = relax(3, 4.0, q_xy - j_x * u_y)
    m8 = relax(4, 4.0, q_yz - j_y * u_z)
    m9 = relax(5, 4.0, q_xz - j_x * u_z)
    m10 = relax(6, 40.0, far_x - 4.0 * apart[1] + (2.0 / 3.0) * j_x)
    m11 = relax(7, 40.0, far_y - 4.0 * apart[3] + (2.0 / 3.0) * j_y)
    m12 = relax(8, 40.0, far_z - 4.0 * apart[5] + (2.0 / 3.0) * j_z)
    m13 = relax(9, 8.0, a_xy - a_xz)
    m14 = relax(10, 8.0, a_yz - b_xy)
    m15 = relax(11, 8.0, b_xz - b_yz)
    m16 = relax(12, 252.0, 12.0 * f[0] - 4.0 * axis_sum + edge_sum - 3.0 * rho + 5.5 * square)
    m17 = relax(13, 24.0, edge_xy - 2.0 * axis_xy + 0.5 * normal_xy)
    m18 = relax(14, 72.0, edge_z - 2.0 * axis_z + 0.5 * normal_z)

    axis_base = -11.0 * m4 - 4.0 * m16
    edge_base = 8.0 * m4 + m16
    v5, v6 = m5 - 2.0 * m17, m6 - 2.0 * m18
    w5, w6 = m5 + m17, m6 + m18
    e_xy, e_xz, e_yz = edge_base - 2.0 * w6, edge_base + w5 + w6, edge_base - w5 + w6
    even = {
        1: axis_base + v5 - v6,
        3: axis_base - v5 - v6,
        5: axis_base + 2.0 * v6,
        7: e_xy + m7,
        9: e_xy - m7,
        11: e_xz + m9,
        13: e_xz - m9,
        15: e_yz + m8,
        17: e_yz - m8,
    }
    s_xy, t_xy = m10 + m13, m11 - m14
    s_xz, t_xz = m10 - m13, m12 + m15
    s_yz, t_yz = m11 + m14, m12 - m15
    odd = {
        1: -4.0 * m10,
        3: -4.0 * m11,
        5: -4.0 * m12,
        7: s_xy + t_xy,
        9: s_xy - t_xy,
        11: s_xz + t_xz,
        13: s_xz - t_xz,
        15: s_yz + t_yz,
        17: s_yz - t_yz,
    }
    post = [f[0] + 30.0 * m4 - 12.0 * m16]
    for q in range(1, 19, 2):
        post.append(f[q] - even[q] - odd[q])
        post.append(f[q + 1] - even[q] + odd[q])
    return [jnp.where(solid, f[OPPOSITE[q]], post[q]) for q in range(19)]


def inflow(turbulence):
    u = [0.05 + 0.05 * turbulence[0], 0.05 * turbulence[1], 0.05 * turbulence[2]]
    speed = 1.0 - 1.5 * (u[0] * u[0] + u[1] * u[1] + u[2] * u[2])
    result = []
    for q in range(19):
        weight = (1.0 / 3.0, 1.0 / 18.0, 1.0 / 36.0)[sum(map(abs, VELOCITY[q]))]
        along = None
        for step, part in zip(VELOCITY[q], u):
            if step:
                part = part if step > 0 else -part
                along = part if along is None else along + part
        result.append(weight * (speed if along is None else speed + along * (3.0 + 4.5 * along)))
    return result


def tap(offset, half_width):
    spread = half_width.astype(jnp.float32)
    reach = offset.astype(jnp.float32)
    value = jnp.exp(reach * reach * (-jnp.pi / (2.0 * (spread * spread))))
    return jnp.where(jnp.abs(reach) <= 2.0 * spread, value, 0.0)


def tap_norm(half_width):
    offset = lax.broadcasted_iota(jnp.int32, (8, 128), 1) - FILT
    value = jnp.where(offset <= FILT, tap(offset, half_width), 0.0)
    return 1.0 / jnp.sqrt(jnp.sum(value * value, axis=1, keepdims=True))[0:1]


def kernel(
    counts,
    f_hbm,
    rate_hbm,
    solid_hbm,
    noise_hbm,
    width_hbm,
    out,
    f_in,
    rate,
    solid,
    noise,
    width,
    post,
    side,
    later,
    later_side,
    send_z,
    from_z,
    filter_y,
    filter_z,
    turbulence,
    flow,
    load_sem,
    send_sem,
    recv_sem,
    recv_up,
    noise_recv,
    ready_sem,
    ruler,
):
    here = tuple(lax.axis_index(axis) for axis in AXES)
    at_inlet = here[0] == 0
    at_outlet = here[0] == counts[0] - 1
    at_edge = jnp.logical_or(at_inlet, at_outlet)
    barrier = pltpu.get_barrier_semaphore()

    def greet(offset, semaphore=barrier):
        pl.semaphore_signal(
            semaphore, inc=1, device_id=neighbour(here, counts, offset), device_id_type=MESH
        )

    for offset in DOWN + LEVEL:
        greet(offset)

    @pl.when(jnp.logical_not(at_outlet))
    def _():
        for offset in UP:
            greet(offset)

    @pl.when(at_edge)
    def _():
        for offset in BEYOND:
            greet(offset)

    loads = [pltpu.make_async_copy(rate_hbm, rate, load_sem.at[NX])]
    loads.append(pltpu.make_async_copy(solid_hbm, solid, load_sem.at[NX + 1]))
    for x in range(NX):
        plane = pl.ds(x, 1)
        loads.append(pltpu.make_async_copy(f_hbm.at[:, plane], f_in.at[:, plane], load_sem.at[x]))
    loads.append(pltpu.make_async_copy(width_hbm, width, load_sem.at[NX + 2]))
    loads.append(pltpu.make_async_copy(noise_hbm, noise.at[1, 1], load_sem.at[NX + 3]))
    for load in loads:
        load.start()

    row = lax.broadcasted_iota(jnp.int32, (NY, NZ), 0)
    lane = lax.broadcasted_iota(jnp.int32, (NY, NZ), 1)
    quarter = lane & 3

    def spin(value, amount, axis=1):
        amount = amount % value.shape[axis]
        return pltpu.roll(value, amount, axis) if amount else value

    def await_rows(rows, semaphore):
        span = ruler.at[pl.ds(0, rows)]
        pltpu.make_async_copy(span, span, semaphore).wait()

    def face_copies(half, offsets):
        copies = []
        for offset in offsets:
            dx, dy, dz = offset
            form = 1 if dy else 0
            for piece in pieces(offset):
                if dz:
                    rows = pl.ds(*piece)
                    source = send_z.at[half, :, rows]
                    target = from_z.at[half, 1 - dx, 0 if dz > 0 else 1, form, :, rows]
                else:
                    first, number, array, arrays, there, rows = piece
                    array, rows = pl.ds(array, arrays), pl.ds(*rows)
                    source = post.at[half, pl.ds(first, number), array, 0, rows]
                    target = post.at[half, pl.ds(there, number), array, form, rows]
                copies.append(
                    pltpu.make_async_remote_copy(
                        src_ref=source,
                        dst_ref=target,
                        send_sem=send_sem.at[2 if dx > 0 else 0],
                        recv_sem=(recv_up if dx > 0 else recv_sem).at[half],
                        device_id=neighbour(here, counts, offset),
                        device_id_type=MESH,
                    )
                )
        return copies

    def noise_copies(step):
        copies = []
        for offset in ACROSS:
            block = pl.ds(step, 1)
            copies.append(
                pltpu.make_async_remote_copy(
                    src_ref=noise.at[1, 1, block],
                    dst_ref=noise.at[(1 - offset[1]) % 4, 1 - offset[2], block],
                    send_sem=send_sem.at[1],
                    recv_sem=noise_recv.at[step],
                    device_id=neighbour(here, counts, offset),
                    device_id_type=MESH,
                )
            )
        return copies

    def send_faces(half):
        @pl.when(jnp.logical_not(at_outlet))
        def _():
            for copy in face_copies(half, UP):
                copy.start()

        if half == 0:

            @pl.when(jnp.logical_not(at_inlet))
            def _():
                for copy in face_copies(half, DOWN):
                    copy.start()

        else:
            for copy in face_copies(half, DOWN):
                copy.start()
        for copy in face_copies(half, LEVEL):
            copy.start()

    def await_faces(half):
        await_rows(OTHER_ROWS, recv_sem.at[half])

        @pl.when(jnp.logical_not(at_inlet))
        def _():
            await_rows(UP_ROWS, recv_up.at[half])

    def rates():
        return [rate[k] for k in range(15)]

    def collide_plane(f, x, half):
        blocked = solid[x] > 0
        result = collide(f, blocked, rates()) + [jnp.where(blocked, 1.0, 0.0)]
        packed = [send_z[half, k] for k in range(PACKED)]
        for q in range(20):
            post[half, x + WIDE, PLACE[q], 0] = result[q]
            tile, slot = PLACE[q] // 8, PLACE[q] % 8
            first = 16 * slot + 4 * x + 2
            moved = pltpu.roll(result[q], lax.rem(first + 2, NZ), 1)
            packed[tile] = jnp.where(((lane - first) & (NZ - 1)) < 4, moved, packed[tile])
        for k in range(PACKED):
            send_z[half, k] = packed[k]

    def unpack(half):
        for form in range(2):
            merged = [
                [
                    jnp.where(
                        quarter >= 2,
                        from_z[half, block, 0, form, k],
                        spin(from_z[half, block, 1, form, k], -4),
                    )
                    for k in range(PACKED)
                ]
                for block in range(3)
            ]
            for place in range(20):
                tile, slot = place // 8, place % 8
                below, own, above = (
                    spin(merged[block][tile], shift - 16 * slot)
                    for block, shift in enumerate((-8, 8, 24))
                )
                side[place, form] = jnp.where(lane < 8, below, jnp.where(lane < 24, own, above))

    def column(tile, plane, step_z):
        amount = (0 if step_z > 0 else NZ - 1) + 2 * NZ - (4 * plane + (3 if step_z > 0 else 0))
        return pltpu.roll(tile, lax.rem(amount, NZ), 1)

    def exchange_rows(main, edge, step_y):
        main, edge = spin(main, step_y, 0), spin(edge, step_y, 0)
        swap = row == (0 if step_y > 0 else NY - 1)
        return jnp.where(swap, edge, main), jnp.where(swap, main, edge)

    def stream_plane(plane, planes_of, sides_of, both):
        result = [[], []]
        for q in range(19):
            step_x, step_y, step_z = VELOCITY[q]
            source = plane - step_x
            forms = [0, 1] if both or step_y else [0]
            value = [planes_of(source, q, form) for form in forms]
            if step_z:
                enters = lane == (0 if step_z > 0 else NZ - 1)
                value = [
                    jnp.where(enters, column(sides_of(q, form), source, step_z), spin(value[form], step_z))
                    for form in forms
                ]
            if step_y:
                value = exchange_rows(value[0], value[1], step_y)
            result[0].append(value[0])
            if both:
                result[1].append(value[1])
        return result

    def stream_side(half):
        result = [[], []]
        for q in range(19):
            step_x, step_y, step_z = VELOCITY[q]
            value = []
            for form in range(2):
                moved = spin(side[PLACE[q], form], 4 * step_x + step_z)
                if step_z:
                    place, origin = (0, NZ - 1) if step_z > 0 else (3, 0)
                    outer = None
                    for plane in range(1, PLANES - 1):
                        source = plane - step_x
                        taken = spin(post[half, source, PLACE[q], form], 4 * plane + place - origin)
                        outer = taken if outer is None else jnp.where(lane >= 4 * plane, taken, outer)
                    moved = jnp.where(quarter == place, outer, moved)
                value.append(moved)
            if step_y:
                value = exchange_rows(value[0], value[1], step_y)
            for form in range(2):
                result[form].append(value[form])
        return result

    def filter_step(step):
        await_rows(NOISE_ROWS, noise_recv.at[step])

        def component(a, carry):
            across = jnp.concatenate(
                [
                    jnp.dot(
                        filter_y[a],
                        jnp.concatenate([noise[b, c, step, a] for b in range(4)], 0),
                        precision=lax.Precision.HIGHEST,
                        preferred_element_type=jnp.float32,
                    )
                    for c in range(3)
                ],
                1,
            )
            turbulence[step, a] = jnp.dot(
                across,
                filter_z[a],
                precision=lax.Precision.HIGHEST,
                preferred_element_type=jnp.float32,
            )
            return carry

        lax.fori_loop(0, 3, component, 0, unroll=3)
        for q, value in enumerate(inflow([turbulence[step, a] for a in range(3)])):
            flow[step % WIDE, q] = value

    def inflow_at(step, q, form, packed):
        return flow[step % WIDE, q, form * NY : (form + 1) * NY, packed * NZ : (packed + 1) * NZ]

    send_z[...] = jnp.zeros_like(send_z)
    loads[0].wait()
    loads[1].wait()

    def first(x, carry):
        plane = pl.ds(x, 1)
        pltpu.make_async_copy(f_hbm.at[:, plane], f_in.at[:, plane], load_sem.at[x]).wait()
        collide_plane([f_in[q, x] for q in range(19)], x, 0)
        return carry

    lax.fori_loop(0, NX, first, 0, unroll=NX)
    loads[NX + 2].wait()
    loads[NX + 3].wait()

    @pl.when(at_edge)
    def _():
        def component(a, carry):
            index = lax.broadcasted_iota(jnp.int32, (2 * NY, 4 * NY), 0)
            node = jnp.where(index < NY + 4, index, index - 2 * NY)
            node = jnp.where(jnp.logical_and(index >= NY, index < NY + 4), index, node)
            reach_y = lax.broadcasted_iota(jnp.int32, (2 * NY, 4 * NY), 1) - NY - node
            reach_y = jnp.where(reach_y > 2 * NY - 1, reach_y - 4 * NY, reach_y)
            filter_y[a] = tap(reach_y, width[0, a]) * tap_norm(width[0, a])
            index = lax.broadcasted_iota(jnp.int32, (3 * NZ, 2 * NZ), 1)
            part = index & 3
            node = jnp.where(index < NZ, index, jnp.where(part < 2, part + NZ, part - 4))
            reach_z = lax.broadcasted_iota(jnp.int32, (3 * NZ, 2 * NZ), 0) - NZ - node
            filter_z[a] = tap(reach_z, width[1, a]) * tap_norm(width[1, a])
            return carry

        lax.fori_loop(0, 3, component, 0)

    expected = jnp.where(at_inlet, len(LEVEL) + len(UP), len(NEIGHBOURS))
    pl.semaphore_wait(barrier, expected + jnp.where(at_edge, len(BEYOND), 0))

    @pl.when(at_outlet)
    def _():
        for offset in UP:
            greet(offset, ready_sem)

    for half in range(HALVES):
        send_faces(half)

        @pl.when(at_edge)
        def _():
            if half == 0:
                for step in range(STEPS):
                    for copy in noise_copies(step):
                        copy.start()

                @pl.when(at_inlet)
                def _():
                    pl.semaphore_wait(ready_sem, len(DOWN))
                    for copy in face_copies(0, DOWN):
                        copy.start()

            for step in range(WIDE * half, WIDE * half + WIDE):
                filter_step(step)

        await_faces(half)
        unpack(half)

        step = WIDE * half

        def around(index, carry):
            plane = index + 1
            f = stream_plane(
                plane,
                lambda source, q, form: post[half, source, PLACE[q], form],
                lambda q, form: side[PLACE[q], form],
                True,
            )
            set_here = jnp.logical_or(
                jnp.logical_and(at_inlet, plane == WIDE),
                jnp.logical_and(at_outlet, plane == WIDE + NX),
            )
            for form in range(2):
                f_form = [
                    jnp.where(set_here, inflow_at(step, q, form, 0), f[form][q]) for q in range(19)
                ]
                result = collide(f_form, post[half, plane, PLACE[SOLID], form] > 0.5, rates())
                for q in range(19):
                    later[index, q, form] = result[q]
            return carry

        lax.fori_loop(0, PLANES - 2, around, 0, unroll=UNROLL)
        f = stream_side(half)
        edge_plane = jnp.where(at_inlet, WIDE, WIDE + NX)
        set_here = jnp.logical_and(at_edge, (lane >> 2) == edge_plane)
        for form in range(2):
            f_form = [
                jnp.where(set_here, inflow_at(step, q, form, 1), f[form][q]) for q in range(19)
            ]
            result = collide(f_form, side[PLACE[SOLID], form] > 0.5, rates())
            for q in range(19):
                later_side[q, form] = result[q]

        step = WIDE * half + 1

        def own(x, carry):
            f = stream_plane(
                x + WIDE,
                lambda source, q, form: later[source - 1, q, form],
                lambda q, form: later_side[q, form],
                False,
            )[0]
            set_here = jnp.logical_and(at_inlet, x == 0)
            f = [jnp.where(set_here, inflow_at(step, q, 0, 0), f[q]) for q in range(19)]
            if half + 1 < HALVES:
                collide_plane(f, x, half + 1)
            else:
                for q in range(19):
                    out[q, x] = f[q]
            return carry

        lax.fori_loop(0, NX, own, 0, unroll=NX)

    await_rows(HALVES * OTHER_ROWS, send_sem.at[0])

    @pl.when(jnp.logical_not(at_outlet))
    def _():
        await_rows(HALVES * UP_ROWS, send_sem.at[2])

    @pl.when(at_edge)
    def _():
        await_rows(STEPS * NOISE_ROWS, send_sem.at[1])


def solution(mesh):
    counts = tuple(mesh.shape[axis] for axis in AXES)
    tile = (NY, NZ)

    def local(populations_in, relax_rates, solid_mask, noise_slabs, half_widths):
        operands = (populations_in, relax_rates, solid_mask, noise_slabs, half_widths.T)
        return pl.pallas_call(
            functools.partial(kernel, counts),
            name="lattice_steps",
            out_shape=jax.ShapeDtypeStruct(populations_in.shape, jnp.float32),
            in_specs=[pl.BlockSpec(memory_space=pltpu.HBM)] * 5,
            out_specs=pl.BlockSpec(memory_space=pltpu.VMEM),
            scratch_shapes=[
                pltpu.VMEM((19, NX) + tile, jnp.float32),
                pltpu.SMEM((15,), jnp.float32),
                pltpu.VMEM((NX,) + tile, jnp.int32),
                pltpu.VMEM((4, 3, STEPS, 3) + tile, jnp.float32),
                pltpu.SMEM((2, 3), jnp.int32),
                pltpu.VMEM((HALVES, PLANES, 20, 2) + tile, jnp.float32),
                pltpu.VMEM((20, 2) + tile, jnp.float32),
                pltpu.VMEM((PLANES - 2, 19, 2) + tile, jnp.float32),
                pltpu.VMEM((19, 2) + tile, jnp.float32),
                pltpu.VMEM((HALVES, PACKED) + tile, jnp.float32),
                pltpu.VMEM((HALVES, 3, 2, 2, PACKED) + tile, jnp.float32),
                pltpu.VMEM((3, 2 * NY, 4 * NY), jnp.float32),
                pltpu.VMEM((3, 3 * NZ, 2 * NZ), jnp.float32),
                pltpu.VMEM((STEPS, 3, 2 * NY, 2 * NZ), jnp.float32),
                pltpu.VMEM((WIDE, 19, 2 * NY, 2 * NZ), jnp.float32),
                pltpu.SemaphoreType.DMA((NX + 4,)),
                pltpu.SemaphoreType.DMA((3,)),
                pltpu.SemaphoreType.DMA((HALVES,)),
                pltpu.SemaphoreType.DMA((HALVES,)),
                pltpu.SemaphoreType.DMA((STEPS,)),
                pltpu.SemaphoreType.REGULAR,
                pltpu.VMEM((max(HALVES * OTHER_ROWS, STEPS * NOISE_ROWS), NZ), jnp.float32),
            ],
            compiler_params=pltpu.CompilerParams(
                collective_id=0, has_side_effects=True, vmem_limit_bytes=32 << 20
            ),
        )(*[pltpu.with_memory_space_constraint(x, pltpu.HBM) for x in operands])

    return jax.shard_map(
        local,
        mesh=mesh,
        in_specs=(
            P(None, "gx", "gy", "gz"),
            P(),
            P("gx", "gy", "gz"),
            P(None, None, "gy", "gz"),
            P(),
        ),
        out_specs=P(None, "gx", "gy", "gz"),
        check_vma=False,
    )
```

```python
import functools
import itertools

import jax
import jax.numpy as jnp
from jax import lax
from jax.experimental import pallas as pl
from jax.experimental.pallas import tpu as pltpu
from jax.sharding import PartitionSpec as P

MESH = pl.DeviceIdType.MESH
AXES = ("gx", "gy", "gz")
FILT = 8
STEPS = 4
NX, NY, NZ = 4, 8, 128
UNROLL = 6
VELOCITY = [
    (0, 0, 0),
    (1, 0, 0),
    (-1, 0, 0),
    (0, 1, 0),
    (0, -1, 0),
    (0, 0, 1),
    (0, 0, -1),
    (1, 1, 0),
    (-1, -1, 0),
    (1, -1, 0),
    (-1, 1, 0),
    (1, 0, 1),
    (-1, 0, -1),
    (1, 0, -1),
    (-1, 0, 1),
    (0, 1, 1),
    (0, -1, -1),
    (0, 1, -1),
    (0, -1, 1),
]
OPPOSITE = [0] + [q + 1 if q % 2 == 1 else q - 1 for q in range(1, 19)]
SOLID = 19
ORDER = sorted(range(20), key=lambda q: (tuple(-c for c in (VELOCITY + [(0, 0, 0)])[q][:2]), q))
PLACE = [ORDER.index(q) for q in range(20)]
WIDE = 2
HALVES = STEPS // WIDE
PLANES = NX + 2 * WIDE
RISING, SINKING = ([q for q in range(19) if VELOCITY[q][2] == step] for step in (1, -1))
STAYING = [q for q in range(19) if VELOCITY[q][2] == 0] + [SOLID]
NEIGHBOURS = sorted(
    (d for d in itertools.product((-1, 0, 1), repeat=3) if any(d)),
    key=lambda d: -sum(map(abs, d)),
)
LEVEL, UP, DOWN = ([d for d in NEIGHBOURS if d[0] == step] for step in (0, 1, -1))
ACROSS = [d for d in itertools.product((0,), (-1, 0, 1, 2), (-1, 0, 1)) if any(d)]
BEYOND = [d for d in ACROSS if d[1] == 2]


def pieces(offset):
    dx, dy, dz = offset
    if dz:
        return [(0, NY) if not dy else (NY - WIDE, WIDE) if dy > 0 else (0, WIDE)]
    near_row, far_row = ((0, NY), None) if not dy else ((7, 1), (6, 1)) if dy > 0 else ((0, 1), (1, 1))
    if dx > 0:
        whole = [
            [[(0, 15)], []],
            [[(0, 12)], [(0, 1), (5, 3)]],
            [[(1, 4), (8, 7)], [(4, 1), (12, 3)]],
        ][dy]
        half = [[[(0, 5)], []], [[(0, 4)], [(0, 1)]], [[(1, 4)], [(4, 1)]]][dy]
        planes = [(5, 1, 1, whole), (4, 1, 0, half)]
    elif dx < 0:
        whole = [
            [[(5, 15)], []],
            [[(5, 7), (15, 4)], [(5, 3), (15, 1)]],
            [[(8, 12)], [(12, 3), (19, 1)]],
        ][dy]
        half = [[[(15, 5)], []], [[(15, 4)], [(15, 1)]], [[(16, 4)], [(19, 1)]]][dy]
        planes = [(2, 1, 6, whole), (3, 1, 7, half)]
    elif dy > 0:
        planes = [(2, NX, 2, [[(0, 12), (15, 4)], [(0, 1), (5, 3), (15, 1)]])]
    else:
        planes = [(2, NX, 2, [[(1, 4), (8, 12)], [(4, 1), (12, 3), (19, 1)]])]
    return [
        (first, number, array, arrays, there, rows)
        for first, number, there, ranges in planes
        for rows, parts in zip((near_row, far_row), ranges)
        for array, arrays in parts
    ]


def rows_of(offsets):
    return sum(
        piece[1] if len(piece) == 2 else piece[1] * piece[3] * piece[5][1]
        for offset in offsets
        for piece in pieces(offset)
    )


SHORT, LONG = ([d for d in NEIGHBOURS if (d[2] != 0) == short] for short in (True, False))
UP_ROWS = rows_of(UP)
OTHER_ROWS = rows_of(LEVEL + DOWN)


def received(offsets, kind):
    return rows_of([d for d in offsets if d in kind])


REACH = 10
NOISE_Y_ROWS = WIDE * 3 * (2 * NY + 2)
NOISE_ROWS = [6 * NY + 2 * 2 + NOISE_Y_ROWS, NOISE_Y_ROWS]


def neighbour(here, counts, offset):
    return tuple(
        lax.rem(place + step + count, count) if step else place
        for place, step, count in zip(here, offset, counts)
    )


def collide(f, solid, rate):
    total = {q: f[q] + f[q + 1] for q in range(1, 19, 2)}
    apart = {q: f[q] - f[q + 1] for q in range(1, 19, 2)}
    p_xy, p_xz, p_yz = total[7] + total[9], total[11] + total[13], total[15] + total[17]
    q_xy, q_xz, q_yz = total[7] - total[9], total[11] - total[13], total[15] - total[17]
    a_xy, b_xy = apart[7] + apart[9], apart[7] - apart[9]
    a_xz, b_xz = apart[11] + apart[13], apart[11] - apart[13]
    a_yz, b_yz = apart[15] + apart[17], apart[15] - apart[17]
    axis_sum = total[1] + total[3] + total[5]
    edge_sum = p_xy + p_xz + p_yz
    rho = f[0] + axis_sum + edge_sum
    far_x, far_y, far_z = a_xy + a_xz, b_xy + a_yz, b_xz + b_yz
    j_x, j_y, j_z = apart[1] + far_x, apart[3] + far_y, apart[5] + far_z
    inverse = 1.0 / rho
    u_x, u_y, u_z = j_x * inverse, j_y * inverse, j_z * inverse
    xx, yy, zz = j_x * u_x, j_y * u_y, j_z * u_z
    square = xx + yy + zz
    normal_xy, normal_z = xx - yy, 2.0 * zz - xx - yy

    def relax(which, norm, value):
        return (rate[which] * (1.0 / norm)) * value

    axis_xy, edge_xy = total[1] - total[3], p_xz - p_yz
    axis_z = 2.0 * total[5] - total[1] - total[3]
    edge_z = p_xz + p_yz - 2.0 * p_xy
    m4 = relax(0, 2394.0, 8.0 * edge_sum - 11.0 * axis_sum - 30.0 * f[0] + 11.0 * rho - 19.0 * square)
    m5 = relax(1, 12.0, axis_xy + edge_xy - normal_xy)
    m6 = relax(2, 36.0, axis_z + edge_z - normal_z)
    m7 = relax(3, 4.0, q_xy - j_x * u_y)
    m8 = relax(4, 4.0, q_yz - j_y * u_z)
    m9 = relax(5, 4.0, q_xz - j_x * u_z)
    m10 = relax(6, 40.0, far_x - 4.0 * apart[1] + (2.0 / 3.0) * j_x)
    m11 = relax(7, 40.0, far_y - 4.0 * apart[3] + (2.0 / 3.0) * j_y)
    m12 = relax(8, 40.0, far_z - 4.0 * apart[5] + (2.0 / 3.0) * j_z)
    m13 = relax(9, 8.0, a_xy - a_xz)
    m14 = relax(10, 8.0, a_yz - b_xy)
    m15 = relax(11, 8.0, b_xz - b_yz)
    m16 = relax(12, 252.0, 12.0 * f[0] - 4.0 * axis_sum + edge_sum - 3.0 * rho + 5.5 * square)
    m17 = relax(13, 24.0, edge_xy - 2.0 * axis_xy + 0.5 * normal_xy)
    m18 = relax(14, 72.0, edge_z - 2.0 * axis_z + 0.5 * normal_z)

    axis_base = -11.0 * m4 - 4.0 * m16
    edge_base = 8.0 * m4 + m16
    v5, v6 = m5 - 2.0 * m17, m6 - 2.0 * m18
    w5, w6 = m5 + m17, m6 + m18
    e_xy, e_xz, e_yz = edge_base - 2.0 * w6, edge_base + w5 + w6, edge_base - w5 + w6
    even = {
        1: axis_base + v5 - v6,
        3: axis_base - v5 - v6,
        5: axis_base + 2.0 * v6,
        7: e_xy + m7,
        9: e_xy - m7,
        11: e_xz + m9,
        13: e_xz - m9,
        15: e_yz + m8,
        17: e_yz - m8,
    }
    s_xy, t_xy = m10 + m13, m11 - m14
    s_xz, t_xz = m10 - m13, m12 + m15
    s_yz, t_yz = m11 + m14, m12 - m15
    odd = {
        1: -4.0 * m10,
        3: -4.0 * m11,
        5: -4.0 * m12,
        7: s_xy + t_xy,
        9: s_xy - t_xy,
        11: s_xz + t_xz,
        13: s_xz - t_xz,
        15: s_yz + t_yz,
        17: s_yz - t_yz,
    }
    post = [f[0] + 30.0 * m4 - 12.0 * m16]
    for q in range(1, 19, 2):
        post.append(f[q] - even[q] - odd[q])
        post.append(f[q + 1] - even[q] + odd[q])
    return [jnp.where(solid, f[OPPOSITE[q]], post[q]) for q in range(19)]


def inflow(turbulence):
    u = [0.05 + 0.05 * turbulence[0], 0.05 * turbulence[1], 0.05 * turbulence[2]]
    speed = 1.0 - 1.5 * (u[0] * u[0] + u[1] * u[1] + u[2] * u[2])
    result = []
    for q in range(19):
        weight = (1.0 / 3.0, 1.0 / 18.0, 1.0 / 36.0)[sum(map(abs, VELOCITY[q]))]
        along = None
        for step, part in zip(VELOCITY[q], u):
            if step:
                part = part if step > 0 else -part
                along = part if along is None else along + part
        result.append(weight * (speed if along is None else speed + along * (3.0 + 4.5 * along)))
    return result


def tap(offset, half_width):
    spread = half_width.astype(jnp.float32)
    reach = offset.astype(jnp.float32)
    value = jnp.exp(reach * reach * (-jnp.pi / (2.0 * (spread * spread))))
    return jnp.where(jnp.abs(reach) <= 2.0 * spread, value, 0.0)


def tap_norm(half_width):
    offset = lax.broadcasted_iota(jnp.int32, (8, 128), 1) - FILT
    value = jnp.where(offset <= FILT, tap(offset, half_width), 0.0)
    return 1.0 / jnp.sqrt(jnp.sum(value * value, axis=1, keepdims=True))[0:1]


def kernel(
    counts,
    f_hbm,
    rate_hbm,
    solid_hbm,
    noise_hbm,
    width_hbm,
    out,
    f_in,
    rate,
    solid,
    noise,
    noise_z,
    noise_side,
    width,
    post,
    side,
    later,
    later_side,
    send_z,
    from_z,
    filter_y,
    filter_z,
    turbulence,
    flow,
    load_sem,
    send_sem,
    recv_sem,
    recv_up,
    noise_recv,
    ready_sem,
    ruler,
):
    here = tuple(lax.axis_index(axis) for axis in AXES)
    at_inlet = here[0] == 0
    at_outlet = here[0] == counts[0] - 1
    at_edge = jnp.logical_or(at_inlet, at_outlet)
    barrier = pltpu.get_barrier_semaphore()

    def greet(offset, semaphore=barrier):
        pl.semaphore_signal(
            semaphore, inc=1, device_id=neighbour(here, counts, offset), device_id_type=MESH
        )

    for offset in DOWN + LEVEL:
        greet(offset)

    @pl.when(jnp.logical_not(at_outlet))
    def _():
        for offset in UP:
            greet(offset)

    @pl.when(at_edge)
    def _():
        for offset in BEYOND:
            greet(offset)

    loads = [pltpu.make_async_copy(rate_hbm, rate, load_sem.at[NX])]
    loads.append(pltpu.make_async_copy(solid_hbm, solid, load_sem.at[NX + 1]))
    for x in range(NX):
        plane = pl.ds(x, 1)
        loads.append(pltpu.make_async_copy(f_hbm.at[:, plane], f_in.at[:, plane], load_sem.at[x]))
    loads.append(pltpu.make_async_copy(width_hbm, width, load_sem.at[NX + 2]))
    loads.append(pltpu.make_async_copy(noise_hbm, noise.at[1], load_sem.at[NX + 3]))
    for load in loads:
        load.start()

    row = lax.broadcasted_iota(jnp.int32, (NY, NZ), 0)
    lane = lax.broadcasted_iota(jnp.int32, (NY, NZ), 1)
    quarter = lane & 3

    def spin(value, amount, axis=1):
        amount = amount % value.shape[axis]
        return pltpu.roll(value, amount, axis) if amount else value

    def await_rows(rows, semaphore):
        span = ruler.at[pl.ds(0, rows)]
        pltpu.make_async_copy(span, span, semaphore).wait()

    def face_copies(half, offsets):
        copies = []
        for offset in offsets:
            dx, dy, dz = offset
            form = 1 if dy else 0
            for piece in pieces(offset):
                if dz:
                    rows = pl.ds(*piece)
                    source = send_z.at[half, 0 if dz > 0 else 1, rows]
                    target = from_z.at[half, 1 - dx, 0 if dz > 0 else 1, form, rows]
                else:
                    first, number, array, arrays, there, rows = piece
                    array, rows = pl.ds(array, arrays), pl.ds(*rows)
                    source = post.at[half, pl.ds(first, number), array, 0, rows]
                    target = post.at[half, pl.ds(there, number), array, form, rows]
                copies.append(
                    pltpu.make_async_remote_copy(
                        src_ref=source,
                        dst_ref=target,
                        send_sem=send_sem.at[2 if dx > 0 else 0],
                        recv_sem=(recv_up if dx > 0 else recv_sem).at[half, 0 if dz else 1],
                        device_id=neighbour(here, counts, offset),
                        device_id_type=MESH,
                    )
                )
        return copies

    def noise_copies(half):
        copies = []
        for offset in ACROSS:
            dy, dz = offset[1:]
            block, direction = (1 - dy) % 4, 0 if dz > 0 else 1
            steps = pl.ds(WIDE * half, WIDE)
            if dz and half:
                continue
            for rows in [(0, 1), (NY - 1, 1)] if offset in BEYOND else [(0, NY)]:
                rows = pl.ds(*rows)
                copies.append(
                    pltpu.make_async_remote_copy(
                        src_ref=noise_z.at[direction, rows] if dz else noise.at[1, steps, :, rows],
                        dst_ref=noise_side.at[block, direction, rows]
                        if dz
                        else noise.at[block, steps, :, rows],
                        send_sem=send_sem.at[1],
                        recv_sem=noise_recv.at[half],
                        device_id=neighbour(here, counts, offset),
                        device_id_type=MESH,
                    )
                )
        return copies

    def pack_noise():
        above, below = jnp.zeros((NY, NZ), jnp.float32), jnp.zeros((NY, NZ), jnp.float32)
        for k in range(3 * STEPS):
            place = REACH * k
            mine = jnp.logical_and(lane >= place, lane < place + REACH)
            tile = noise[1, k // 3, k % 3]
            above = jnp.where(mine, spin(tile, place + REACH), above)
            below = jnp.where(mine, spin(tile, place), below)
        noise_z[0], noise_z[1] = above, below

    def send_faces(half):
        @pl.when(jnp.logical_not(at_outlet))
        def _():
            for copy in face_copies(half, UP):
                copy.start()

        @pl.when(jnp.logical_not(at_inlet))
        def _():
            for copy in face_copies(half, DOWN):
                copy.start()

        for copy in face_copies(half, LEVEL):
            copy.start()
        if half == 1:

            @pl.when(at_inlet)
            def _():
                pl.semaphore_wait(ready_sem, len(DOWN))
                for late in range(2):
                    for copy in face_copies(late, DOWN):
                        copy.start()

    def await_faces(half, kind):
        place = 0 if kind is SHORT else 1
        await_rows(received(LEVEL + DOWN, kind), recv_sem.at[half, place])

        @pl.when(jnp.logical_not(at_inlet))
        def _():
            await_rows(received(UP, kind), recv_up.at[half, place])

    def rates():
        return [rate[k] for k in range(15)]

    def collide_plane(f, x, half):
        blocked = solid[x] > 0
        result = collide(f, blocked, rates()) + [jnp.where(blocked, 1.0, 0.0)]
        for q in range(20):
            post[half, x + WIDE, PLACE[q], 0] = result[q]
        above, below = send_z[half, 0], send_z[half, 1]
        for k in range(5):
            place = 16 * k + 4 * x
            moved = pltpu.roll(result[RISING[k]], place + 4, 1)
            above = jnp.where(jnp.logical_or(lane == place + 2, lane == place + 3), moved, above)
            moved = pltpu.roll(result[SINKING[k]], place, 1)
            below = jnp.where(jnp.logical_or(lane == place, lane == place + 1), moved, below)
        for k in range(10):
            place = 16 * (k // 2) + 4 * x + k % 2
            above = jnp.where(lane == place, pltpu.roll(result[STAYING[k]], place + 1, 1), above)
            place = place + 2
            below = jnp.where(lane == place, pltpu.roll(result[STAYING[k]], place, 1), below)
        send_z[half, 0], send_z[half, 1] = above, below

    def unpack(half):
        for form in range(2):
            pairs, lone = [], ([], [])
            for block in range(3):
                low, high = from_z[half, block, 0, form], from_z[half, block, 1, form]
                pairs.append(jnp.where(quarter >= 2, low, high))
                for k in range(2):
                    lone[k].append(jnp.where(quarter == 3, spin(low, 3 - k), spin(high, -2 - k)))

            def spread(tiles, slot):
                below, own, above = (
                    spin(tile, shift - 16 * slot) for tile, shift in zip(tiles, (-8, 8, 24))
                )
                return jnp.where(lane < 8, below, jnp.where(lane < 24, own, above))

            for k in range(5):
                tile = spread(pairs, k)
                side[PLACE[RISING[k]], form] = tile
                side[PLACE[SINKING[k]], form] = tile
            for k in range(10):
                side[PLACE[STAYING[k]], form] = spread(lone[k % 2], k // 2)

    def column(tile, plane, step_z):
        amount = (0 if step_z > 0 else NZ - 1) + 2 * NZ - (4 * plane + (3 if step_z > 0 else 0))
        return pltpu.roll(tile, lax.rem(amount, NZ), 1)

    def exchange_rows(main, edge, step_y):
        main, edge = spin(main, step_y, 0), spin(edge, step_y, 0)
        swap = row == (0 if step_y > 0 else NY - 1)
        return jnp.where(swap, edge, main), jnp.where(swap, main, edge)

    def stream_plane(plane, planes_of, sides_of, both):
        result = [[], []]
        for q in range(19):
            step_x, step_y, step_z = VELOCITY[q]
            source = plane - step_x
            forms = [0, 1] if both or step_y else [0]
            value = [planes_of(source, q, form) for form in forms]
            if step_z:
                enters = lane == (0 if step_z > 0 else NZ - 1)
                value = [
                    jnp.where(enters, column(sides_of(q, form), source, step_z), spin(value[form], step_z))
                    for form in forms
                ]
            if step_y:
                value = exchange_rows(value[0], value[1], step_y)
            result[0].append(value[0])
            if both:
                result[1].append(value[1])
        return result

    def stream_side(half):
        result = [[], []]
        for q in range(19):
            step_x, step_y, step_z = VELOCITY[q]
            value = []
            for form in range(2):
                moved = spin(side[PLACE[q], form], 4 * step_x + step_z)
                if step_z:
                    place, origin = (0, NZ - 1) if step_z > 0 else (3, 0)
                    outer = None
                    for plane in range(1, PLANES - 1):
                        source = plane - step_x
                        taken = spin(post[half, source, PLACE[q], form], 4 * plane + place - origin)
                        outer = taken if outer is None else jnp.where(lane >= 4 * plane, taken, outer)
                    moved = jnp.where(quarter == place, outer, moved)
                value.append(moved)
            if step_y:
                value = exchange_rows(value[0], value[1], step_y)
            for form in range(2):
                result[form].append(value[form])
        return result

    def make_filters():
        def component(a, carry):
            index = lax.broadcasted_iota(jnp.int32, (2 * NY, 4 * NY), 0)
            node = jnp.where(index < NY + 4, index, index - 2 * NY)
            node = jnp.where(jnp.logical_and(index >= NY, index < NY + 4), index, node)
            reach_y = lax.broadcasted_iota(jnp.int32, (2 * NY, 4 * NY), 1) - NY - node
            reach_y = jnp.where(reach_y > 2 * NY - 1, reach_y - 4 * NY, reach_y)
            filter_y[a] = tap(reach_y, width[0, a]) * tap_norm(width[0, a])
            index = lax.broadcasted_iota(jnp.int32, (2 * NZ, 2 * NZ), 1)
            part = index & 3
            node = jnp.where(index < NZ, index, jnp.where(part < 2, part + NZ, part - 4))
            index = lax.broadcasted_iota(jnp.int32, (2 * NZ, 2 * NZ), 0)
            part = index - NZ
            origin = jnp.where(part < 2 * REACH, part + NZ - REACH, 8 * NZ)
            origin = jnp.where(part < REACH, part - REACH, origin)
            reach_z = jnp.where(part < 0, index, origin) - node
            filter_z[a] = tap(reach_z, width[1, a]) * tap_norm(width[1, a])
            return carry

        lax.fori_loop(0, 3, component, 0)

    def filter_steps(half):
        await_rows(NOISE_ROWS[half], noise_recv.at[half])
        outer = jnp.logical_or(row == 0, row == NY - 1)
        for a in range(3):
            across = []
            for step in range(WIDE * half, WIDE * half + WIDE):
                place = REACH * (3 * step + a)
                blocks = []
                for b in range(4):
                    main = noise[b, step, a]
                    sides = jnp.where(
                        lane < REACH,
                        spin(noise_side[b, 0], -place),
                        spin(noise_side[b, 1], REACH - place),
                    )
                    if b == 3:
                        main, sides = jnp.where(outer, main, 0.0), jnp.where(outer, sides, 0.0)
                    blocks.append(jnp.concatenate([main, sides], 1))
                across.append(
                    jnp.dot(
                        filter_y[a],
                        jnp.concatenate(blocks, 0),
                        precision=lax.Precision.HIGHEST,
                        preferred_element_type=jnp.float32,
                    )
                )
            turbulence[a] = jnp.dot(
                jnp.concatenate(across, 0),
                filter_z[a],
                precision=lax.Precision.HIGHEST,
                preferred_element_type=jnp.float32,
            )
        for k in range(WIDE):
            rows = pl.ds(2 * NY * k, 2 * NY)
            for q, value in enumerate(inflow([turbulence[a, rows] for a in range(3)])):
                flow[k, q] = value

    def inflow_at(step, q, form, packed):
        return flow[step % WIDE, q, form * NY : (form + 1) * NY, packed * NZ : (packed + 1) * NZ]

    send_z[...] = jnp.zeros_like(send_z)
    loads[0].wait()
    loads[1].wait()

    def first(x, carry):
        plane = pl.ds(x, 1)
        pltpu.make_async_copy(f_hbm.at[:, plane], f_in.at[:, plane], load_sem.at[x]).wait()
        collide_plane([f_in[q, x] for q in range(19)], x, 0)
        return carry

    lax.fori_loop(0, NX, first, 0, unroll=NX)
    loads[NX + 2].wait()
    loads[NX + 3].wait()
    pl.when(at_edge)(pack_noise)

    expected = jnp.where(at_inlet, len(LEVEL) + len(UP), len(NEIGHBOURS))
    pl.semaphore_wait(barrier, expected + jnp.where(at_edge, len(BEYOND), 0))

    @pl.when(at_outlet)
    def _():
        for offset in UP:
            greet(offset, ready_sem)

    for half in range(HALVES):
        send_faces(half)

        @pl.when(at_edge)
        def _():
            if half == 0:
                for part in range(HALVES):
                    for copy in noise_copies(part):
                        copy.start()
                make_filters()
            filter_steps(half)

        await_faces(half, SHORT)
        unpack(half)
        await_faces(half, LONG)

        step = WIDE * half

        def around(index, carry):
            plane = index + 1
            f = stream_plane(
                plane,
                lambda source, q, form: post[half, source, PLACE[q], form],
                lambda q, form: side[PLACE[q], form],
                True,
            )
            set_here = jnp.logical_or(
                jnp.logical_and(at_inlet, plane == WIDE),
                jnp.logical_and(at_outlet, plane == WIDE + NX),
            )
            for form in range(2):
                f_form = [
                    jnp.where(set_here, inflow_at(step, q, form, 0), f[form][q]) for q in range(19)
                ]
                result = collide(f_form, post[half, plane, PLACE[SOLID], form] > 0.5, rates())
                for q in range(19):
                    later[index, q, form] = result[q]
            return carry

        lax.fori_loop(0, PLANES - 2, around, 0, unroll=UNROLL)
        f = stream_side(half)
        edge_plane = jnp.where(at_inlet, WIDE, WIDE + NX)
        set_here = jnp.logical_and(at_edge, (lane >> 2) == edge_plane)
        for form in range(2):
            f_form = [
                jnp.where(set_here, inflow_at(step, q, form, 1), f[form][q]) for q in range(19)
            ]
            result = collide(f_form, side[PLACE[SOLID], form] > 0.5, rates())
            for q in range(19):
                later_side[q, form] = result[q]

        step = WIDE * half + 1

        def own(x, carry):
            f = stream_plane(
                x + WIDE,
                lambda source, q, form: later[source - 1, q, form],
                lambda q, form: later_side[q, form],
                False,
            )[0]
            set_here = jnp.logical_and(at_inlet, x == 0)
            f = [jnp.where(set_here, inflow_at(step, q, 0, 0), f[q]) for q in range(19)]
            if half + 1 < HALVES:
                collide_plane(f, x, half + 1)
            else:
                for q in range(19):
                    out[q, x] = f[q]
            return carry

        lax.fori_loop(0, NX, own, 0, unroll=NX)

    await_rows(HALVES * OTHER_ROWS, send_sem.at[0])

    @pl.when(jnp.logical_not(at_outlet))
    def _():
        await_rows(HALVES * UP_ROWS, send_sem.at[2])

    @pl.when(at_edge)
    def _():
        await_rows(sum(NOISE_ROWS), send_sem.at[1])


def solution(mesh):
    counts = tuple(mesh.shape[axis] for axis in AXES)
    tile = (NY, NZ)

    def local(populations_in, relax_rates, solid_mask, noise_slabs, half_widths):
        operands = (populations_in, relax_rates, solid_mask, noise_slabs, half_widths.T)
        return pl.pallas_call(
            functools.partial(kernel, counts),
            name="lattice_steps",
            out_shape=jax.ShapeDtypeStruct(populations_in.shape, jnp.float32),
            in_specs=[pl.BlockSpec(memory_space=pltpu.HBM)] * 5,
            out_specs=pl.BlockSpec(memory_space=pltpu.VMEM),
            scratch_shapes=[
                pltpu.VMEM((19, NX) + tile, jnp.float32),
                pltpu.SMEM((15,), jnp.float32),
                pltpu.VMEM((NX,) + tile, jnp.int32),
                pltpu.VMEM((4, STEPS, 3) + tile, jnp.float32),
                pltpu.VMEM((2,) + tile, jnp.float32),
                pltpu.VMEM((4, 2) + tile, jnp.float32),
                pltpu.SMEM((2, 3), jnp.int32),
                pltpu.VMEM((HALVES, PLANES, 20, 2) + tile, jnp.float32),
                pltpu.VMEM((20, 2) + tile, jnp.float32),
                pltpu.VMEM((PLANES - 2, 19, 2) + tile, jnp.float32),
                pltpu.VMEM((19, 2) + tile, jnp.float32),
                pltpu.VMEM((HALVES, 2) + tile, jnp.float32),
                pltpu.VMEM((HALVES, 3, 2, 2) + tile, jnp.float32),
                pltpu.VMEM((3, 2 * NY, 4 * NY), jnp.float32),
                pltpu.VMEM((3, 2 * NZ, 2 * NZ), jnp.float32),
                pltpu.VMEM((3, WIDE * 2 * NY, 2 * NZ), jnp.float32),
                pltpu.VMEM((WIDE, 19, 2 * NY, 2 * NZ), jnp.float32),
                pltpu.SemaphoreType.DMA((NX + 4,)),
                pltpu.SemaphoreType.DMA((3,)),
                pltpu.SemaphoreType.DMA((HALVES, 2)),
                pltpu.SemaphoreType.DMA((HALVES, 2)),
                pltpu.SemaphoreType.DMA((HALVES,)),
                pltpu.SemaphoreType.REGULAR,
                pltpu.VMEM((HALVES * OTHER_ROWS, NZ), jnp.float32),
            ],
            compiler_params=pltpu.CompilerParams(
                collective_id=0, has_side_effects=True, vmem_limit_bytes=32 << 20
            ),
        )(*[pltpu.with_memory_space_constraint(x, pltpu.HBM) for x in operands])

    return jax.shard_map(
        local,
        mesh=mesh,
        in_specs=(
            P(None, "gx", "gy", "gz"),
            P(),
            P("gx", "gy", "gz"),
            P(None, None, "gy", "gz"),
            P(),
        ),
        out_specs=P(None, "gx", "gy", "gz"),
        check_vma=False,
    )
```

```python
import functools
import itertools

import jax
import jax.numpy as jnp
from jax import lax
from jax.experimental import pallas as pl
from jax.experimental.pallas import tpu as pltpu
from jax.sharding import PartitionSpec as P

MESH = pl.DeviceIdType.MESH
AXES = ("gx", "gy", "gz")
FILT = 8
STEPS = 4
NX, NY, NZ = 4, 8, 128
UNROLL = 6
VELOCITY = [
    (0, 0, 0),
    (1, 0, 0),
    (-1, 0, 0),
    (0, 1, 0),
    (0, -1, 0),
    (0, 0, 1),
    (0, 0, -1),
    (1, 1, 0),
    (-1, -1, 0),
    (1, -1, 0),
    (-1, 1, 0),
    (1, 0, 1),
    (-1, 0, -1),
    (1, 0, -1),
    (-1, 0, 1),
    (0, 1, 1),
    (0, -1, -1),
    (0, 1, -1),
    (0, -1, 1),
]
OPPOSITE = [0] + [q + 1 if q % 2 == 1 else q - 1 for q in range(1, 19)]
SOLID = 19
ORDER = sorted(range(20), key=lambda q: (tuple(-c for c in (VELOCITY + [(0, 0, 0)])[q][:2]), q))
PLACE = [ORDER.index(q) for q in range(20)]
WIDE = 2
HALVES = STEPS // WIDE
PLANES = NX + 2 * WIDE
RISING, SINKING = ([q for q in range(19) if VELOCITY[q][2] == step] for step in (1, -1))
STAYING = [q for q in range(19) if VELOCITY[q][2] == 0] + [SOLID]
NEIGHBOURS = sorted(
    (d for d in itertools.product((-1, 0, 1), repeat=3) if any(d)),
    key=lambda d: -sum(map(abs, d)),
)
LEVEL, UP, DOWN = ([d for d in NEIGHBOURS if d[0] == step] for step in (0, 1, -1))
STRAIGHT = (-1, 0, 0)
ACROSS = [d for d in itertools.product((0,), (-1, 0, 1, 2), (-1, 0, 1)) if any(d)]
BEYOND = [d for d in ACROSS if d[1] == 2]


def pieces(offset):
    dx, dy, dz = offset
    if dz:
        return [(0, NY) if not dy else (NY - WIDE, WIDE) if dy > 0 else (0, WIDE)]
    near_row, far_row = ((0, NY), None) if not dy else ((7, 1), (6, 1)) if dy > 0 else ((0, 1), (1, 1))
    if dx > 0:
        whole = [
            [[(0, 15)], []],
            [[(0, 12)], [(0, 1), (5, 3)]],
            [[(1, 4), (8, 7)], [(4, 1), (12, 3)]],
        ][dy]
        half = [[[(0, 5)], []], [[(0, 4)], [(0, 1)]], [[(1, 4)], [(4, 1)]]][dy]
        planes = [(5, 1, 1, whole), (4, 1, 0, half)]
    elif dx < 0:
        whole = [
            [[(5, 15)], []],
            [[(5, 7), (15, 4)], [(5, 3), (15, 1)]],
            [[(8, 12)], [(12, 3), (19, 1)]],
        ][dy]
        half = [[[(15, 5)], []], [[(15, 4)], [(15, 1)]], [[(16, 4)], [(19, 1)]]][dy]
        planes = [(2, 1, 6, whole), (3, 1, 7, half)]
    elif dy > 0:
        planes = [(2, NX, 2, [[(0, 12), (15, 4)], [(0, 1), (5, 3), (15, 1)]])]
    else:
        planes = [(2, NX, 2, [[(1, 4), (8, 12)], [(4, 1), (12, 3), (19, 1)]])]
    return [
        (first, number, array, arrays, there, rows)
        for first, number, there, ranges in planes
        for rows, parts in zip((near_row, far_row), ranges)
        for array, arrays in parts
    ]


def rows_of(offsets):
    return sum(
        piece[1] if len(piece) == 2 else piece[1] * piece[3] * piece[5][1]
        for offset in offsets
        for piece in pieces(offset)
    )


SHORT, LONG = ([d for d in NEIGHBOURS if (d[2] != 0) == short] for short in (True, False))
UP_ROWS = rows_of(UP)
OTHER_ROWS = rows_of(LEVEL + DOWN)


def received(offsets, kind):
    return rows_of([d for d in offsets if d in kind])


REACH = 10
KNOWN_ROWS = 15 * NY
NOISE_Y_ROWS = WIDE * 3 * (2 * NY + 2)
NOISE_ROWS = [6 * NY + 2 * 2 + NOISE_Y_ROWS, NOISE_Y_ROWS]


def neighbour(here, counts, offset):
    return tuple(
        lax.rem(place + step + count, count) if step else place
        for place, step, count in zip(here, offset, counts)
    )


def collide(f, solid, rate):
    total = {q: f[q] + f[q + 1] for q in range(1, 19, 2)}
    apart = {q: f[q] - f[q + 1] for q in range(1, 19, 2)}
    p_xy, p_xz, p_yz = total[7] + total[9], total[11] + total[13], total[15] + total[17]
    q_xy, q_xz, q_yz = total[7] - total[9], total[11] - total[13], total[15] - total[17]
    a_xy, b_xy = apart[7] + apart[9], apart[7] - apart[9]
    a_xz, b_xz = apart[11] + apart[13], apart[11] - apart[13]
    a_yz, b_yz = apart[15] + apart[17], apart[15] - apart[17]
    axis_sum = total[1] + total[3] + total[5]
    edge_sum = p_xy + p_xz + p_yz
    rho = f[0] + axis_sum + edge_sum
    far_x, far_y, far_z = a_xy + a_xz, b_xy + a_yz, b_xz + b_yz
    j_x, j_y, j_z = apart[1] + far_x, apart[3] + far_y, apart[5] + far_z
    inverse = 1.0 / rho
    u_x, u_y, u_z = j_x * inverse, j_y * inverse, j_z * inverse
    xx, yy, zz = j_x * u_x, j_y * u_y, j_z * u_z
    square = xx + yy + zz
    normal_xy, normal_z = xx - yy, 2.0 * zz - xx - yy

    def relax(which, norm, value):
        return (rate[which] * (1.0 / norm)) * value

    axis_xy, edge_xy = total[1] - total[3], p_xz - p_yz
    axis_z = 2.0 * total[5] - total[1] - total[3]
    edge_z = p_xz + p_yz - 2.0 * p_xy
    m4 = relax(0, 2394.0, 8.0 * edge_sum - 11.0 * axis_sum - 30.0 * f[0] + 11.0 * rho - 19.0 * square)
    m5 = relax(1, 12.0, axis_xy + edge_xy - normal_xy)
    m6 = relax(2, 36.0, axis_z + edge_z - normal_z)
    m7 = relax(3, 4.0, q_xy - j_x * u_y)
    m8 = relax(4, 4.0, q_yz - j_y * u_z)
    m9 = relax(5, 4.0, q_xz - j_x * u_z)
    m10 = relax(6, 40.0, far_x - 4.0 * apart[1] + (2.0 / 3.0) * j_x)
    m11 = relax(7, 40.0, far_y - 4.0 * apart[3] + (2.0 / 3.0) * j_y)
    m12 = relax(8, 40.0, far_z - 4.0 * apart[5] + (2.0 / 3.0) * j_z)
    m13 = relax(9, 8.0, a_xy - a_xz)
    m14 = relax(10, 8.0, a_yz - b_xy)
    m15 = relax(11, 8.0, b_xz - b_yz)
    m16 = relax(12, 252.0, 12.0 * f[0] - 4.0 * axis_sum + edge_sum - 3.0 * rho + 5.5 * square)
    m17 = relax(13, 24.0, edge_xy - 2.0 * axis_xy + 0.5 * normal_xy)
    m18 = relax(14, 72.0, edge_z - 2.0 * axis_z + 0.5 * normal_z)

    axis_base = -11.0 * m4 - 4.0 * m16
    edge_base = 8.0 * m4 + m16
    v5, v6 = m5 - 2.0 * m17, m6 - 2.0 * m18
    w5, w6 = m5 + m17, m6 + m18
    e_xy, e_xz, e_yz = edge_base - 2.0 * w6, edge_base + w5 + w6, edge_base - w5 + w6
    even = {
        1: axis_base + v5 - v6,
        3: axis_base - v5 - v6,
        5: axis_base + 2.0 * v6,
        7: e_xy + m7,
        9: e_xy - m7,
        11: e_xz + m9,
        13: e_xz - m9,
        15: e_yz + m8,
        17: e_yz - m8,
    }
    s_xy, t_xy = m10 + m13, m11 - m14
    s_xz, t_xz = m10 - m13, m12 + m15
    s_yz, t_yz = m11 + m14, m12 - m15
    odd = {
        1: -4.0 * m10,
        3: -4.0 * m11,
        5: -4.0 * m12,
        7: s_xy + t_xy,
        9: s_xy - t_xy,
        11: s_xz + t_xz,
        13: s_xz - t_xz,
        15: s_yz + t_yz,
        17: s_yz - t_yz,
    }
    post = [f[0] + 30.0 * m4 - 12.0 * m16]
    for q in range(1, 19, 2):
        post.append(f[q] - even[q] - odd[q])
        post.append(f[q + 1] - even[q] + odd[q])
    return [jnp.where(solid, f[OPPOSITE[q]], post[q]) for q in range(19)]


def inflow(turbulence):
    u = [0.05 + 0.05 * turbulence[0], 0.05 * turbulence[1], 0.05 * turbulence[2]]
    speed = 1.0 - 1.5 * (u[0] * u[0] + u[1] * u[1] + u[2] * u[2])
    result = []
    for q in range(19):
        weight = (1.0 / 3.0, 1.0 / 18.0, 1.0 / 36.0)[sum(map(abs, VELOCITY[q]))]
        along = None
        for step, part in zip(VELOCITY[q], u):
            if step:
                part = part if step > 0 else -part
                along = part if along is None else along + part
        result.append(weight * (speed if along is None else speed + along * (3.0 + 4.5 * along)))
    return result


def tap(offset, half_width):
    spread = half_width.astype(jnp.float32)
    reach = offset.astype(jnp.float32)
    value = jnp.exp(reach * reach * (-jnp.pi / (2.0 * (spread * spread))))
    return jnp.where(jnp.abs(reach) <= 2.0 * spread, value, 0.0)


def tap_norm(half_width):
    offset = lax.broadcasted_iota(jnp.int32, (8, 128), 1) - FILT
    value = jnp.where(offset <= FILT, tap(offset, half_width), 0.0)
    return 1.0 / jnp.sqrt(jnp.sum(value * value, axis=1, keepdims=True))[0:1]


def kernel(
    counts,
    f_hbm,
    rate_hbm,
    solid_hbm,
    noise_hbm,
    width_hbm,
    out,
    f_in,
    rate,
    solid,
    noise,
    noise_z,
    noise_side,
    width,
    post,
    side,
    later,
    later_side,
    send_z,
    from_z,
    filter_y,
    filter_z,
    turbulence,
    flow,
    load_sem,
    send_sem,
    recv_sem,
    recv_up,
    noise_recv,
    ready_sem,
    ruler,
):
    here = tuple(lax.axis_index(axis) for axis in AXES)
    at_inlet = here[0] == 0
    at_outlet = here[0] == counts[0] - 1
    at_edge = jnp.logical_or(at_inlet, at_outlet)
    barrier = pltpu.get_barrier_semaphore()

    def greet(offset, semaphore=barrier):
        pl.semaphore_signal(
            semaphore, inc=1, device_id=neighbour(here, counts, offset), device_id_type=MESH
        )

    for offset in DOWN + LEVEL:
        greet(offset)

    @pl.when(jnp.logical_not(at_outlet))
    def _():
        for offset in UP:
            greet(offset)

    @pl.when(at_edge)
    def _():
        for offset in BEYOND:
            greet(offset)

    loads = [pltpu.make_async_copy(rate_hbm, rate, load_sem.at[NX])]
    loads.append(pltpu.make_async_copy(solid_hbm, solid, load_sem.at[NX + 1]))
    for x in range(NX):
        plane = pl.ds(x, 1)
        loads.append(pltpu.make_async_copy(f_hbm.at[:, plane], f_in.at[:, plane], load_sem.at[x]))
    loads.append(pltpu.make_async_copy(width_hbm, width, load_sem.at[NX + 2]))
    loads.append(pltpu.make_async_copy(noise_hbm, noise.at[1], load_sem.at[NX + 3]))
    for load in loads:
        load.start()

    row = lax.broadcasted_iota(jnp.int32, (NY, NZ), 0)
    lane = lax.broadcasted_iota(jnp.int32, (NY, NZ), 1)
    quarter = lane & 3

    def spin(value, amount, axis=1):
        amount = amount % value.shape[axis]
        return pltpu.roll(value, amount, axis) if amount else value

    def await_rows(rows, semaphore):
        span = ruler.at[pl.ds(0, rows)]
        pltpu.make_async_copy(span, span, semaphore).wait()

    def face_copies(half, offsets, known=0):
        copies = []
        for offset in offsets:
            dx, dy, dz = offset
            form = 1 if dy else 0
            for piece in pieces(offset)[known:]:
                if dz:
                    rows = pl.ds(*piece)
                    source = send_z.at[half, 0 if dz > 0 else 1, rows]
                    target = from_z.at[half, 1 - dx, 0 if dz > 0 else 1, form, rows]
                else:
                    first, number, array, arrays, there, rows = piece
                    array, rows = pl.ds(array, arrays), pl.ds(*rows)
                    source = post.at[half, pl.ds(first, number), array, 0, rows]
                    target = post.at[half, pl.ds(there, number), array, form, rows]
                copies.append(
                    pltpu.make_async_remote_copy(
                        src_ref=source,
                        dst_ref=target,
                        send_sem=send_sem.at[2 if dx > 0 else 0],
                        recv_sem=(recv_up if dx > 0 else recv_sem).at[half, 0 if dz else 1],
                        device_id=neighbour(here, counts, offset),
                        device_id_type=MESH,
                    )
                )
        return copies

    def noise_copies(half):
        copies = []
        for offset in ACROSS:
            dy, dz = offset[1:]
            block, direction = (1 - dy) % 4, 0 if dz > 0 else 1
            steps = pl.ds(WIDE * half, WIDE)
            if dz and half:
                continue
            for rows in [(0, 1), (NY - 1, 1)] if offset in BEYOND else [(0, NY)]:
                rows = pl.ds(*rows)
                copies.append(
                    pltpu.make_async_remote_copy(
                        src_ref=noise_z.at[direction, rows] if dz else noise.at[1, steps, :, rows],
                        dst_ref=noise_side.at[block, direction, rows]
                        if dz
                        else noise.at[block, steps, :, rows],
                        send_sem=send_sem.at[1],
                        recv_sem=noise_recv.at[half],
                        device_id=neighbour(here, counts, offset),
                        device_id_type=MESH,
                    )
                )
        return copies

    def pack_noise():
        above, below = jnp.zeros((NY, NZ), jnp.float32), jnp.zeros((NY, NZ), jnp.float32)
        for k in range(3 * STEPS):
            place = REACH * k
            mine = jnp.logical_and(lane >= place, lane < place + REACH)
            tile = noise[1, k // 3, k % 3]
            above = jnp.where(mine, spin(tile, place + REACH), above)
            below = jnp.where(mine, spin(tile, place), below)
        noise_z[0], noise_z[1] = above, below

    def send_faces(half):
        for kind in (SHORT, LONG):

            @pl.when(jnp.logical_not(at_outlet))
            def _():
                for copy in face_copies(half, [d for d in UP if d in kind]):
                    copy.start()

            @pl.when(jnp.logical_not(at_inlet))
            def _():
                for copy in face_copies(half, [d for d in DOWN if d in kind]):
                    copy.start()

            for copy in face_copies(half, [d for d in LEVEL if d in kind]):
                copy.start()
        if half == 1:

            @pl.when(at_inlet)
            def _():
                pl.semaphore_wait(ready_sem, len(DOWN))
                for late in range(2):
                    for kind in (SHORT, LONG):
                        offsets = [d for d in DOWN if d in kind and d != STRAIGHT]
                        for copy in face_copies(late, offsets):
                            copy.start()
                    for copy in face_copies(late, [STRAIGHT], late):
                        copy.start()

    def await_faces(half, kind):
        place = 0 if kind is SHORT else 1
        rows = received(LEVEL + DOWN, kind)
        if kind is LONG and half == 1:

            @pl.when(at_outlet)
            def _():
                await_rows(rows - KNOWN_ROWS, recv_sem.at[half, place])

            @pl.when(jnp.logical_not(at_outlet))
            def _():
                await_rows(rows, recv_sem.at[half, place])

        else:
            await_rows(rows, recv_sem.at[half, place])

        @pl.when(jnp.logical_not(at_inlet))
        def _():
            await_rows(received(UP, kind), recv_up.at[half, place])

    def rates():
        return [rate[k] for k in range(15)]

    def collide_plane(f, x, half):
        blocked = solid[x] > 0
        result = collide(f, blocked, rates()) + [jnp.where(blocked, 1.0, 0.0)]
        for q in range(20):
            post[half, x + WIDE, PLACE[q], 0] = result[q]
        above, below = send_z[half, 0], send_z[half, 1]
        for k in range(5):
            place = 16 * k + 4 * x
            moved = pltpu.roll(result[RISING[k]], place + 4, 1)
            above = jnp.where(jnp.logical_or(lane == place + 2, lane == place + 3), moved, above)
            moved = pltpu.roll(result[SINKING[k]], place, 1)
            below = jnp.where(jnp.logical_or(lane == place, lane == place + 1), moved, below)
        for k in range(10):
            place = 16 * (k // 2) + 4 * x + k % 2
            above = jnp.where(lane == place, pltpu.roll(result[STAYING[k]], place + 1, 1), above)
            place = place + 2
            below = jnp.where(lane == place, pltpu.roll(result[STAYING[k]], place, 1), below)
        send_z[half, 0], send_z[half, 1] = above, below

    def unpack(half):
        for form in range(2):
            pairs, lone = [], ([], [])
            for block in range(3):
                low, high = from_z[half, block, 0, form], from_z[half, block, 1, form]
                pairs.append(jnp.where(quarter >= 2, low, high))
                for k in range(2):
                    lone[k].append(jnp.where(quarter == 3, spin(low, 3 - k), spin(high, -2 - k)))

            def spread(tiles, slot):
                below, own, above = (
                    spin(tile, shift - 16 * slot) for tile, shift in zip(tiles, (-8, 8, 24))
                )
                return jnp.where(lane < 8, below, jnp.where(lane < 24, own, above))

            for k in range(5):
                tile = spread(pairs, k)
                side[PLACE[RISING[k]], form] = tile
                side[PLACE[SINKING[k]], form] = tile
            for k in range(10):
                side[PLACE[STAYING[k]], form] = spread(lone[k % 2], k // 2)

    def column(tile, plane, step_z):
        amount = (0 if step_z > 0 else NZ - 1) + 2 * NZ - (4 * plane + (3 if step_z > 0 else 0))
        return pltpu.roll(tile, lax.rem(amount, NZ), 1)

    def exchange_rows(main, edge, step_y):
        main, edge = spin(main, step_y, 0), spin(edge, step_y, 0)
        swap = row == (0 if step_y > 0 else NY - 1)
        return jnp.where(swap, edge, main), jnp.where(swap, main, edge)

    def stream_plane(plane, planes_of, sides_of, both):
        result = [[], []]
        for q in range(19):
            step_x, step_y, step_z = VELOCITY[q]
            source = plane - step_x
            forms = [0, 1] if both or step_y else [0]
            value = [planes_of(source, q, form) for form in forms]
            if step_z:
                enters = lane == (0 if step_z > 0 else NZ - 1)
                value = [
                    jnp.where(enters, column(sides_of(q, form), source, step_z), spin(value[form], step_z))
                    for form in forms
                ]
            if step_y:
                value = exchange_rows(value[0], value[1], step_y)
            result[0].append(value[0])
            if both:
                result[1].append(value[1])
        return result

    def stream_side(half):
        result = [[], []]
        for q in range(19):
            step_x, step_y, step_z = VELOCITY[q]
            value = []
            for form in range(2):
                moved = spin(side[PLACE[q], form], 4 * step_x + step_z)
                if step_z:
                    place, origin = (0, NZ - 1) if step_z > 0 else (3, 0)
                    outer = None
                    for plane in range(1, PLANES - 1):
                        source = plane - step_x
                        taken = spin(post[half, source, PLACE[q], form], 4 * plane + place - origin)
                        outer = taken if outer is None else jnp.where(lane >= 4 * plane, taken, outer)
                    moved = jnp.where(quarter == place, outer, moved)
                value.append(moved)
            if step_y:
                value = exchange_rows(value[0], value[1], step_y)
            for form in range(2):
                result[form].append(value[form])
        return result

    def make_filters():
        def component(a, carry):
            index = lax.broadcasted_iota(jnp.int32, (2 * NY, 4 * NY), 0)
            node = jnp.where(index < NY + 4, index, index - 2 * NY)
            node = jnp.where(jnp.logical_and(index >= NY, index < NY + 4), index, node)
            reach_y = lax.broadcasted_iota(jnp.int32, (2 * NY, 4 * NY), 1) - NY - node
            reach_y = jnp.where(reach_y > 2 * NY - 1, reach_y - 4 * NY, reach_y)
            filter_y[a] = tap(reach_y, width[0, a]) * tap_norm(width[0, a])
            index = lax.broadcasted_iota(jnp.int32, (2 * NZ, 2 * NZ), 1)
            part = index & 3
            node = jnp.where(index < NZ, index, jnp.where(part < 2, part + NZ, part - 4))
            index = lax.broadcasted_iota(jnp.int32, (2 * NZ, 2 * NZ), 0)
            part = index - NZ
            origin = jnp.where(part < 2 * REACH, part + NZ - REACH, 8 * NZ)
            origin = jnp.where(part < REACH, part - REACH, origin)
            reach_z = jnp.where(part < 0, index, origin) - node
            filter_z[a] = tap(reach_z, width[1, a]) * tap_norm(width[1, a])
            return carry

        lax.fori_loop(0, 3, component, 0)

    def filter_steps(half):
        await_rows(NOISE_ROWS[half], noise_recv.at[half])
        outer = jnp.logical_or(row == 0, row == NY - 1)
        for a in range(3):
            across = []
            for step in range(WIDE * half, WIDE * half + WIDE):
                place = REACH * (3 * step + a)
                blocks = []
                for b in range(4):
                    main = noise[b, step, a]
                    sides = jnp.where(
                        lane < REACH,
                        spin(noise_side[b, 0], -place),
                        spin(noise_side[b, 1], REACH - place),
                    )
                    if b == 3:
                        main, sides = jnp.where(outer, main, 0.0), jnp.where(outer, sides, 0.0)
                    blocks.append(jnp.concatenate([main, sides], 1))
                across.append(
                    jnp.dot(
                        filter_y[a],
                        jnp.concatenate(blocks, 0),
                        precision=lax.Precision.HIGHEST,
                        preferred_element_type=jnp.float32,
                    )
                )
            turbulence[a] = jnp.dot(
                jnp.concatenate(across, 0),
                filter_z[a],
                precision=lax.Precision.HIGHEST,
                preferred_element_type=jnp.float32,
            )
        for k in range(WIDE):
            rows = pl.ds(2 * NY * k, 2 * NY)
            for q, value in enumerate(inflow([turbulence[a, rows] for a in range(3)])):
                flow[k, q] = value

    def inflow_at(step, q, form, packed):
        return flow[step % WIDE, q, form * NY : (form + 1) * NY, packed * NZ : (packed + 1) * NZ]

    def collide_inlet():
        blocked = post[0, WIDE + NX, PLACE[SOLID], 0]
        result = collide([inflow_at(1, q, 0, 0) for q in range(19)], blocked > 0.5, rates())
        for q, value in enumerate(result + [blocked]):
            if PLACE[q] >= 5:
                post[1, WIDE + NX, PLACE[q], 0] = value

    send_z[...] = jnp.zeros_like(send_z)
    loads[0].wait()
    loads[1].wait()

    def first(x, carry):
        plane = pl.ds(x, 1)
        pltpu.make_async_copy(f_hbm.at[:, plane], f_in.at[:, plane], load_sem.at[x]).wait()
        collide_plane([f_in[q, x] for q in range(19)], x, 0)
        return carry

    lax.fori_loop(0, NX, first, 0, unroll=NX)
    loads[NX + 2].wait()
    loads[NX + 3].wait()
    pl.when(at_edge)(pack_noise)

    expected = jnp.where(at_inlet, len(LEVEL) + len(UP), len(NEIGHBOURS))
    pl.semaphore_wait(barrier, expected + jnp.where(at_edge, len(BEYOND), 0))

    @pl.when(at_outlet)
    def _():
        for offset in UP:
            greet(offset, ready_sem)

    for half in range(HALVES):
        send_faces(half)

        @pl.when(at_edge)
        def _():
            if half == 0:
                for part in range(HALVES):
                    for copy in noise_copies(part):
                        copy.start()
                make_filters()
            else:
                pl.when(at_outlet)(collide_inlet)
            filter_steps(half)

        await_faces(half, SHORT)
        unpack(half)
        await_faces(half, LONG)

        step = WIDE * half

        def around(plane, edge=None):
            index = plane - 1
            f = stream_plane(
                plane,
                lambda source, q, form: post[half, source, PLACE[q], form],
                lambda q, form: side[PLACE[q], form],
                True,
            )
            for form in range(2):
                f_form = f[form]
                if edge is not None:
                    f_form = [
                        jnp.where(edge, inflow_at(step, q, form, 0), f_form[q]) for q in range(19)
                    ]
                result = collide(f_form, post[half, plane, PLACE[SOLID], form] > 0.5, rates())
                for q in range(19):
                    later[index, q, form] = result[q]

        def between(plane, carry):
            around(plane)
            return carry

        around(1)
        around(WIDE, at_inlet)
        lax.fori_loop(WIDE + 1, WIDE + NX, between, 0, unroll=3)
        around(WIDE + NX, at_outlet)
        f = stream_side(half)
        edge_plane = jnp.where(at_inlet, WIDE, WIDE + NX)
        set_here = jnp.logical_and(at_edge, (lane >> 2) == edge_plane)
        for form in range(2):
            f_form = [
                jnp.where(set_here, inflow_at(step, q, form, 1), f[form][q]) for q in range(19)
            ]
            result = collide(f_form, side[PLACE[SOLID], form] > 0.5, rates())
            for q in range(19):
                later_side[q, form] = result[q]

        step = WIDE * half + 1

        def own(x, carry):
            f = stream_plane(
                x + WIDE,
                lambda source, q, form: later[source - 1, q, form],
                lambda q, form: later_side[q, form],
                False,
            )[0]
            set_here = jnp.logical_and(at_inlet, x == 0)
            f = [jnp.where(set_here, inflow_at(step, q, 0, 0), f[q]) for q in range(19)]
            if half + 1 < HALVES:
                collide_plane(f, x, half + 1)
            else:
                for q in range(19):
                    out[q, x] = f[q]
            return carry

        lax.fori_loop(0, NX, own, 0, unroll=NX)

    @pl.when(at_inlet)
    def _():
        await_rows(HALVES * OTHER_ROWS - KNOWN_ROWS, send_sem.at[0])

    @pl.when(jnp.logical_not(at_inlet))
    def _():
        await_rows(HALVES * OTHER_ROWS, send_sem.at[0])

    @pl.when(jnp.logical_not(at_outlet))
    def _():
        await_rows(HALVES * UP_ROWS, send_sem.at[2])

    @pl.when(at_edge)
    def _():
        await_rows(sum(NOISE_ROWS), send_sem.at[1])


def solution(mesh):
    counts = tuple(mesh.shape[axis] for axis in AXES)
    tile = (NY, NZ)

    def local(populations_in, relax_rates, solid_mask, noise_slabs, half_widths):
        operands = (populations_in, relax_rates, solid_mask, noise_slabs, half_widths.T)
        return pl.pallas_call(
            functools.partial(kernel, counts),
            name="lattice_steps",
            out_shape=jax.ShapeDtypeStruct(populations_in.shape, jnp.float32),
            in_specs=[pl.BlockSpec(memory_space=pltpu.HBM)] * 5,
            out_specs=pl.BlockSpec(memory_space=pltpu.VMEM),
            scratch_shapes=[
                pltpu.VMEM((19, NX) + tile, jnp.float32),
                pltpu.SMEM((15,), jnp.float32),
                pltpu.VMEM((NX,) + tile, jnp.int32),
                pltpu.VMEM((4, STEPS, 3) + tile, jnp.float32),
                pltpu.VMEM((2,) + tile, jnp.float32),
                pltpu.VMEM((4, 2) + tile, jnp.float32),
                pltpu.SMEM((2, 3), jnp.int32),
                pltpu.VMEM((HALVES, PLANES, 20, 2) + tile, jnp.float32),
                pltpu.VMEM((20, 2) + tile, jnp.float32),
                pltpu.VMEM((PLANES - 2, 19, 2) + tile, jnp.float32),
                pltpu.VMEM((19, 2) + tile, jnp.float32),
                pltpu.VMEM((HALVES, 2) + tile, jnp.float32),
                pltpu.VMEM((HALVES, 3, 2, 2) + tile, jnp.float32),
                pltpu.VMEM((3, 2 * NY, 4 * NY), jnp.float32),
                pltpu.VMEM((3, 2 * NZ, 2 * NZ), jnp.float32),
                pltpu.VMEM((3, WIDE * 2 * NY, 2 * NZ), jnp.float32),
                pltpu.VMEM((WIDE, 19, 2 * NY, 2 * NZ), jnp.float32),
                pltpu.SemaphoreType.DMA((NX + 4,)),
                pltpu.SemaphoreType.DMA((3,)),
                pltpu.SemaphoreType.DMA((HALVES, 2)),
                pltpu.SemaphoreType.DMA((HALVES, 2)),
                pltpu.SemaphoreType.DMA((HALVES,)),
                pltpu.SemaphoreType.REGULAR,
                pltpu.VMEM((HALVES * OTHER_ROWS, NZ), jnp.float32),
            ],
            compiler_params=pltpu.CompilerParams(
                collective_id=0, has_side_effects=True, vmem_limit_bytes=32 << 20
            ),
        )(*[pltpu.with_memory_space_constraint(x, pltpu.HBM) for x in operands])

    return jax.shard_map(
        local,
        mesh=mesh,
        in_specs=(
            P(None, "gx", "gy", "gz"),
            P(),
            P("gx", "gy", "gz"),
            P(None, None, "gy", "gz"),
            P(),
        ),
        out_specs=P(None, "gx", "gy", "gz"),
        check_vma=False,
    )
```

```python
import functools
import itertools

import jax
import jax.numpy as jnp
from jax import lax
from jax.experimental import pallas as pl
from jax.experimental.pallas import tpu as pltpu
from jax.sharding import PartitionSpec as P

MESH = pl.DeviceIdType.MESH
AXES = ("gx", "gy", "gz")
FILT = 8
STEPS = 4
NX, NY, NZ = 4, 8, 128
UNROLL = 6
VELOCITY = [
    (0, 0, 0),
    (1, 0, 0),
    (-1, 0, 0),
    (0, 1, 0),
    (0, -1, 0),
    (0, 0, 1),
    (0, 0, -1),
    (1, 1, 0),
    (-1, -1, 0),
    (1, -1, 0),
    (-1, 1, 0),
    (1, 0, 1),
    (-1, 0, -1),
    (1, 0, -1),
    (-1, 0, 1),
    (0, 1, 1),
    (0, -1, -1),
    (0, 1, -1),
    (0, -1, 1),
]
OPPOSITE = [0] + [q + 1 if q % 2 == 1 else q - 1 for q in range(1, 19)]
NORMS = (2394.0, 12.0, 36.0, 4.0, 4.0, 4.0, 40.0, 40.0, 40.0, 8.0, 8.0, 8.0, 252.0, 24.0, 72.0)
SOLID = 19
ORDER = sorted(range(20), key=lambda q: (tuple(-c for c in (VELOCITY + [(0, 0, 0)])[q][:2]), q))
PLACE = [ORDER.index(q) for q in range(20)]
WIDE = 2
HALVES = STEPS // WIDE
PLANES = NX + 2 * WIDE
RISING, SINKING = ([q for q in range(19) if VELOCITY[q][2] == step] for step in (1, -1))
STAYING = [q for q in range(19) if VELOCITY[q][2] == 0] + [SOLID]
NEIGHBOURS = sorted(
    (d for d in itertools.product((-1, 0, 1), repeat=3) if any(d)),
    key=lambda d: -sum(map(abs, d)),
)
LEVEL, UP, DOWN = ([d for d in NEIGHBOURS if d[0] == step] for step in (0, 1, -1))
STRAIGHT = (-1, 0, 0)
ACROSS = [d for d in itertools.product((0,), (-1, 0, 1, 2), (-1, 0, 1)) if any(d)]
BEYOND = [d for d in ACROSS if d[1] == 2]


def pieces(offset):
    dx, dy, dz = offset
    if dz:
        return [(0, NY) if not dy else (NY - WIDE, WIDE) if dy > 0 else (0, WIDE)]
    near_row, far_row = ((0, NY), None) if not dy else ((7, 1), (6, 1)) if dy > 0 else ((0, 1), (1, 1))
    if dx > 0:
        whole = [
            [[(0, 15)], []],
            [[(0, 12)], [(0, 1), (5, 3)]],
            [[(1, 4), (8, 7)], [(4, 1), (12, 3)]],
        ][dy]
        half = [[[(0, 5)], []], [[(0, 4)], [(0, 1)]], [[(1, 4)], [(4, 1)]]][dy]
        planes = [(5, 1, 1, whole), (4, 1, 0, half)]
    elif dx < 0:
        whole = [
            [[(5, 15)], []],
            [[(5, 7), (15, 4)], [(5, 3), (15, 1)]],
            [[(8, 12)], [(12, 3), (19, 1)]],
        ][dy]
        half = [[[(15, 5)], []], [[(15, 4)], [(15, 1)]], [[(16, 4)], [(19, 1)]]][dy]
        planes = [(2, 1, 6, whole), (3, 1, 7, half)]
    elif dy > 0:
        planes = [(2, NX, 2, [[(0, 12), (15, 4)], [(0, 1), (5, 3), (15, 1)]])]
    else:
        planes = [(2, NX, 2, [[(1, 4), (8, 12)], [(4, 1), (12, 3), (19, 1)]])]
    return [
        (first, number, array, arrays, there, rows)
        for first, number, there, ranges in planes
        for rows, parts in zip((near_row, far_row), ranges)
        for array, arrays in parts
    ]


def rows_of(offsets):
    return sum(
        piece[1] if len(piece) == 2 else piece[1] * piece[3] * piece[5][1]
        for offset in offsets
        for piece in pieces(offset)
    )


SHORT, LONG = ([d for d in NEIGHBOURS if (d[2] != 0) == short] for short in (True, False))
UP_ROWS = rows_of(UP)
OTHER_ROWS = rows_of(LEVEL + DOWN)


def received(offsets, kind):
    return rows_of([d for d in offsets if d in kind])


REACH = 10
KNOWN_ROWS = 15 * NY
NOISE_Y_ROWS = WIDE * 3 * (2 * NY + 2)
NOISE_ROWS = [6 * NY + 2 * 2 + NOISE_Y_ROWS, NOISE_Y_ROWS]


def neighbour(here, counts, offset):
    return tuple(
        lax.rem(place + step + count, count) if step else place
        for place, step, count in zip(here, offset, counts)
    )


def collide(f, solid, rate):
    total = {q: f[q] + f[q + 1] for q in range(1, 19, 2)}
    apart = {q: f[q] - f[q + 1] for q in range(1, 19, 2)}
    p_xy, p_xz, p_yz = total[7] + total[9], total[11] + total[13], total[15] + total[17]
    q_xy, q_xz, q_yz = total[7] - total[9], total[11] - total[13], total[15] - total[17]
    a_xy, b_xy = apart[7] + apart[9], apart[7] - apart[9]
    a_xz, b_xz = apart[11] + apart[13], apart[11] - apart[13]
    a_yz, b_yz = apart[15] + apart[17], apart[15] - apart[17]
    axis_sum = total[1] + total[3] + total[5]
    edge_sum = p_xy + p_xz + p_yz
    rho = f[0] + axis_sum + edge_sum
    far_x, far_y, far_z = a_xy + a_xz, b_xy + a_yz, b_xz + b_yz
    j_x, j_y, j_z = apart[1] + far_x, apart[3] + far_y, apart[5] + far_z
    inverse = 1.0 / rho
    u_x, u_y, u_z = j_x * inverse, j_y * inverse, j_z * inverse
    xx, yy, zz = j_x * u_x, j_y * u_y, j_z * u_z
    square = xx + yy + zz
    normal_xy, normal_z = xx - yy, 2.0 * zz - xx - yy

    def relax(which, value):
        return rate[which] * value

    axis_xy, edge_xy = total[1] - total[3], p_xz - p_yz
    axis_z = 2.0 * total[5] - total[1] - total[3]
    edge_z = p_xz + p_yz - 2.0 * p_xy
    m4 = relax(0, 8.0 * edge_sum - 11.0 * axis_sum - 30.0 * f[0] + 11.0 * rho - 19.0 * square)
    m5 = relax(1, axis_xy + edge_xy - normal_xy)
    m6 = relax(2, axis_z + edge_z - normal_z)
    m7 = relax(3, q_xy - j_x * u_y)
    m8 = relax(4, q_yz - j_y * u_z)
    m9 = relax(5, q_xz - j_x * u_z)
    m10 = relax(6, far_x - 4.0 * apart[1] + (2.0 / 3.0) * j_x)
    m11 = relax(7, far_y - 4.0 * apart[3] + (2.0 / 3.0) * j_y)
    m12 = relax(8, far_z - 4.0 * apart[5] + (2.0 / 3.0) * j_z)
    m13 = relax(9, a_xy - a_xz)
    m14 = relax(10, a_yz - b_xy)
    m15 = relax(11, b_xz - b_yz)
    m16 = relax(12, 12.0 * f[0] - 4.0 * axis_sum + edge_sum - 3.0 * rho + 5.5 * square)
    m17 = relax(13, edge_xy - 2.0 * axis_xy + 0.5 * normal_xy)
    m18 = relax(14, edge_z - 2.0 * axis_z + 0.5 * normal_z)

    axis_base = -11.0 * m4 - 4.0 * m16
    edge_base = 8.0 * m4 + m16
    v5, v6 = m5 - 2.0 * m17, m6 - 2.0 * m18
    w5, w6 = m5 + m17, m6 + m18
    e_xy, e_xz, e_yz = edge_base - 2.0 * w6, edge_base + w5 + w6, edge_base - w5 + w6
    even = {
        1: axis_base + v5 - v6,
        3: axis_base - v5 - v6,
        5: axis_base + 2.0 * v6,
        7: e_xy + m7,
        9: e_xy - m7,
        11: e_xz + m9,
        13: e_xz - m9,
        15: e_yz + m8,
        17: e_yz - m8,
    }
    s_xy, t_xy = m10 + m13, m11 - m14
    s_xz, t_xz = m10 - m13, m12 + m15
    s_yz, t_yz = m11 + m14, m12 - m15
    odd = {
        1: -4.0 * m10,
        3: -4.0 * m11,
        5: -4.0 * m12,
        7: s_xy + t_xy,
        9: s_xy - t_xy,
        11: s_xz + t_xz,
        13: s_xz - t_xz,
        15: s_yz + t_yz,
        17: s_yz - t_yz,
    }
    post = [f[0] + 30.0 * m4 - 12.0 * m16]
    for q in range(1, 19, 2):
        post.append(f[q] - even[q] - odd[q])
        post.append(f[q + 1] - even[q] + odd[q])
    return [jnp.where(solid, f[OPPOSITE[q]], post[q]) for q in range(19)]


def inflow(turbulence):
    u = [0.05 + 0.05 * turbulence[0], 0.05 * turbulence[1], 0.05 * turbulence[2]]
    speed = 1.0 - 1.5 * (u[0] * u[0] + u[1] * u[1] + u[2] * u[2])
    result = []
    for q in range(19):
        weight = (1.0 / 3.0, 1.0 / 18.0, 1.0 / 36.0)[sum(map(abs, VELOCITY[q]))]
        along = None
        for step, part in zip(VELOCITY[q], u):
            if step:
                part = part if step > 0 else -part
                along = part if along is None else along + part
        result.append(weight * (speed if along is None else speed + along * (3.0 + 4.5 * along)))
    return result


def tap(offset, half_width):
    spread = half_width.astype(jnp.float32)
    reach = offset.astype(jnp.float32)
    value = jnp.exp(reach * reach * (-jnp.pi / (2.0 * (spread * spread))))
    return jnp.where(jnp.abs(reach) <= 2.0 * spread, value, 0.0)


def tap_norm(half_width):
    offset = lax.broadcasted_iota(jnp.int32, (8, 128), 1) - FILT
    value = jnp.where(offset <= FILT, tap(offset, half_width), 0.0)
    return 1.0 / jnp.sqrt(jnp.sum(value * value, axis=1, keepdims=True))[0:1]


def kernel(
    counts,
    f_hbm,
    rate_hbm,
    solid_hbm,
    noise_hbm,
    width_hbm,
    out,
    f_in,
    rate,
    rate_tiles,
    solid,
    noise,
    noise_z,
    noise_side,
    width,
    post,
    side,
    later,
    later_side,
    send_z,
    from_z,
    filter_y,
    filter_z,
    turbulence,
    flow,
    load_sem,
    send_sem,
    recv_sem,
    recv_up,
    noise_recv,
    ready_sem,
    ruler,
):
    here = tuple(lax.axis_index(axis) for axis in AXES)
    at_inlet = here[0] == 0
    at_outlet = here[0] == counts[0] - 1
    at_edge = jnp.logical_or(at_inlet, at_outlet)
    barrier = pltpu.get_barrier_semaphore()

    def greet(offset, semaphore=barrier):
        pl.semaphore_signal(
            semaphore, inc=1, device_id=neighbour(here, counts, offset), device_id_type=MESH
        )

    for offset in DOWN + LEVEL:
        greet(offset)

    @pl.when(jnp.logical_not(at_outlet))
    def _():
        for offset in UP:
            greet(offset)

    @pl.when(at_edge)
    def _():
        for offset in BEYOND:
            greet(offset)

    loads = [pltpu.make_async_copy(rate_hbm, rate, load_sem.at[NX])]
    loads.append(pltpu.make_async_copy(solid_hbm, solid, load_sem.at[NX + 1]))
    for x in range(NX):
        plane = pl.ds(x, 1)
        loads.append(pltpu.make_async_copy(f_hbm.at[:, plane], f_in.at[:, plane], load_sem.at[x]))
    loads.append(pltpu.make_async_copy(width_hbm, width, load_sem.at[NX + 2]))
    loads.append(pltpu.make_async_copy(noise_hbm, noise.at[1], load_sem.at[NX + 3]))
    for load in loads:
        load.start()

    row = lax.broadcasted_iota(jnp.int32, (NY, NZ), 0)
    lane = lax.broadcasted_iota(jnp.int32, (NY, NZ), 1)
    quarter = lane & 3

    def spin(value, amount, axis=1):
        amount = amount % value.shape[axis]
        return pltpu.roll(value, amount, axis) if amount else value

    def await_rows(rows, semaphore):
        span = ruler.at[pl.ds(0, rows)]
        pltpu.make_async_copy(span, span, semaphore).wait()

    def face_copies(half, offsets, known=0):
        copies = []
        for offset in offsets:
            dx, dy, dz = offset
            form = 1 if dy else 0
            for piece in pieces(offset)[known:]:
                if dz:
                    rows = pl.ds(*piece)
                    source = send_z.at[half, 0 if dz > 0 else 1, rows]
                    target = from_z.at[half, 1 - dx, 0 if dz > 0 else 1, form, rows]
                else:
                    first, number, array, arrays, there, rows = piece
                    array, rows = pl.ds(array, arrays), pl.ds(*rows)
                    source = post.at[half, pl.ds(first, number), array, 0, rows]
                    target = post.at[half, pl.ds(there, number), array, form, rows]
                copies.append(
                    pltpu.make_async_remote_copy(
                        src_ref=source,
                        dst_ref=target,
                        send_sem=send_sem.at[2 if dx > 0 else 0],
                        recv_sem=(recv_up if dx > 0 else recv_sem).at[half, 0 if dz else 1],
                        device_id=neighbour(here, counts, offset),
                        device_id_type=MESH,
                    )
                )
        return copies

    def noise_copies(half):
        copies = []
        for offset in ACROSS:
            dy, dz = offset[1:]
            block, direction = (1 - dy) % 4, 0 if dz > 0 else 1
            steps = pl.ds(WIDE * half, WIDE)
            if dz and half:
                continue
            for rows in [(0, 1), (NY - 1, 1)] if offset in BEYOND else [(0, NY)]:
                rows = pl.ds(*rows)
                copies.append(
                    pltpu.make_async_remote_copy(
                        src_ref=noise_z.at[direction, rows] if dz else noise.at[1, steps, :, rows],
                        dst_ref=noise_side.at[block, direction, rows]
                        if dz
                        else noise.at[block, steps, :, rows],
                        send_sem=send_sem.at[1],
                        recv_sem=noise_recv.at[half],
                        device_id=neighbour(here, counts, offset),
                        device_id_type=MESH,
                    )
                )
        return copies

    def pack_noise():
        above, below = jnp.zeros((NY, NZ), jnp.float32), jnp.zeros((NY, NZ), jnp.float32)
        for k in range(3 * STEPS):
            place = REACH * k
            mine = jnp.logical_and(lane >= place, lane < place + REACH)
            tile = noise[1, k // 3, k % 3]
            above = jnp.where(mine, spin(tile, place + REACH), above)
            below = jnp.where(mine, spin(tile, place), below)
        noise_z[0], noise_z[1] = above, below

    def send_faces(half):
        for kind in (SHORT, LONG):

            @pl.when(jnp.logical_not(at_outlet))
            def _():
                for copy in face_copies(half, [d for d in UP if d in kind]):
                    copy.start()

            @pl.when(jnp.logical_not(at_inlet))
            def _():
                for copy in face_copies(half, [d for d in DOWN if d in kind]):
                    copy.start()

            for copy in face_copies(half, [d for d in LEVEL if d in kind]):
                copy.start()
        if half == 1:

            @pl.when(at_inlet)
            def _():
                pl.semaphore_wait(ready_sem, len(DOWN))
                for late in range(2):
                    for kind in (SHORT, LONG):
                        offsets = [d for d in DOWN if d in kind and d != STRAIGHT]
                        for copy in face_copies(late, offsets):
                            copy.start()
                    for copy in face_copies(late, [STRAIGHT], late):
                        copy.start()

    def await_faces(half, kind):
        place = 0 if kind is SHORT else 1
        rows = received(LEVEL + DOWN, kind)
        if kind is LONG and half == 1:

            @pl.when(at_outlet)
            def _():
                await_rows(rows - KNOWN_ROWS, recv_sem.at[half, place])

            @pl.when(jnp.logical_not(at_outlet))
            def _():
                await_rows(rows, recv_sem.at[half, place])

        else:
            await_rows(rows, recv_sem.at[half, place])

        @pl.when(jnp.logical_not(at_inlet))
        def _():
            await_rows(received(UP, kind), recv_up.at[half, place])

    def rates():
        return [rate_tiles[k] for k in range(15)]

    def collide_plane(f, x, half):
        blocked = solid[x] > 0
        result = collide(f, blocked, rates()) + [jnp.where(blocked, 1.0, 0.0)]
        for q in range(20):
            post[half, x + WIDE, PLACE[q], 0] = result[q]
        above, below = send_z[half, 0], send_z[half, 1]
        for k in range(5):
            place = 16 * k + 4 * x
            moved = pltpu.roll(result[RISING[k]], place + 4, 1)
            above = jnp.where(jnp.logical_or(lane == place + 2, lane == place + 3), moved, above)
            moved = pltpu.roll(result[SINKING[k]], place, 1)
            below = jnp.where(jnp.logical_or(lane == place, lane == place + 1), moved, below)
        for k in range(10):
            place = 16 * (k // 2) + 4 * x + k % 2
            above = jnp.where(lane == place, pltpu.roll(result[STAYING[k]], place + 1, 1), above)
            place = place + 2
            below = jnp.where(lane == place, pltpu.roll(result[STAYING[k]], place, 1), below)
        send_z[half, 0], send_z[half, 1] = above, below

    def unpack(half):
        for form in range(2):
            pairs, lone = [], ([], [])
            for block in range(3):
                low, high = from_z[half, block, 0, form], from_z[half, block, 1, form]
                pairs.append(jnp.where(quarter >= 2, low, high))
                for k in range(2):
                    lone[k].append(jnp.where(quarter == 3, spin(low, 3 - k), spin(high, -2 - k)))

            def spread(tiles, slot):
                below, own, above = (
                    spin(tile, shift - 16 * slot) for tile, shift in zip(tiles, (-8, 8, 24))
                )
                return jnp.where(lane < 8, below, jnp.where(lane < 24, own, above))

            for k in range(5):
                tile = spread(pairs, k)
                side[PLACE[RISING[k]], form] = tile
                side[PLACE[SINKING[k]], form] = tile
            for k in range(10):
                side[PLACE[STAYING[k]], form] = spread(lone[k % 2], k // 2)

    def column(tile, plane, step_z):
        amount = (0 if step_z > 0 else NZ - 1) + 2 * NZ - (4 * plane + (3 if step_z > 0 else 0))
        return pltpu.roll(tile, lax.rem(amount, NZ), 1)

    def exchange_rows(main, edge, step_y):
        main, edge = spin(main, step_y, 0), spin(edge, step_y, 0)
        swap = row == (0 if step_y > 0 else NY - 1)
        return jnp.where(swap, edge, main), jnp.where(swap, main, edge)

    def stream_plane(plane, planes_of, sides_of, both):
        result = [[], []]
        for q in range(19):
            step_x, step_y, step_z = VELOCITY[q]
            source = plane - step_x
            forms = [0, 1] if both or step_y else [0]
            value = [planes_of(source, q, form) for form in forms]
            if step_z:
                enters = lane == (0 if step_z > 0 else NZ - 1)
                value = [
                    jnp.where(enters, column(sides_of(q, form), source, step_z), spin(value[form], step_z))
                    for form in forms
                ]
            if step_y:
                value = exchange_rows(value[0], value[1], step_y)
            result[0].append(value[0])
            if both:
                result[1].append(value[1])
        return result

    def stream_side(half):
        result = [[], []]
        for q in range(19):
            step_x, step_y, step_z = VELOCITY[q]
            value = []
            for form in range(2):
                moved = spin(side[PLACE[q], form], 4 * step_x + step_z)
                if step_z:
                    place, origin = (0, NZ - 1) if step_z > 0 else (3, 0)
                    outer = None
                    for plane in range(1, PLANES - 1):
                        source = plane - step_x
                        taken = spin(post[half, source, PLACE[q], form], 4 * plane + place - origin)
                        outer = taken if outer is None else jnp.where(lane >= 4 * plane, taken, outer)
                    moved = jnp.where(quarter == place, outer, moved)
                value.append(moved)
            if step_y:
                value = exchange_rows(value[0], value[1], step_y)
            for form in range(2):
                result[form].append(value[form])
        return result

    def make_filters():
        def component(a, carry):
            index = lax.broadcasted_iota(jnp.int32, (2 * NY, 4 * NY), 0)
            node = jnp.where(index < NY + 4, index, index - 2 * NY)
            node = jnp.where(jnp.logical_and(index >= NY, index < NY + 4), index, node)
            reach_y = lax.broadcasted_iota(jnp.int32, (2 * NY, 4 * NY), 1) - NY - node
            reach_y = jnp.where(reach_y > 2 * NY - 1, reach_y - 4 * NY, reach_y)
            filter_y[a] = tap(reach_y, width[0, a]) * tap_norm(width[0, a])
            index = lax.broadcasted_iota(jnp.int32, (2 * NZ, 2 * NZ), 1)
            part = index & 3
            node = jnp.where(index < NZ, index, jnp.where(part < 2, part + NZ, part - 4))
            index = lax.broadcasted_iota(jnp.int32, (2 * NZ, 2 * NZ), 0)
            part = index - NZ
            origin = jnp.where(part < 2 * REACH, part + NZ - REACH, 8 * NZ)
            origin = jnp.where(part < REACH, part - REACH, origin)
            reach_z = jnp.where(part < 0, index, origin) - node
            filter_z[a] = tap(reach_z, width[1, a]) * tap_norm(width[1, a])
            return carry

        lax.fori_loop(0, 3, component, 0)

    def filter_steps(half):
        await_rows(NOISE_ROWS[half], noise_recv.at[half])
        outer = jnp.logical_or(row == 0, row == NY - 1)
        for a in range(3):
            across = []
            for step in range(WIDE * half, WIDE * half + WIDE):
                place = REACH * (3 * step + a)
                blocks = []
                for b in range(4):
                    main = noise[b, step, a]
                    sides = jnp.where(
                        lane < REACH,
                        spin(noise_side[b, 0], -place),
                        spin(noise_side[b, 1], REACH - place),
                    )
                    if b == 3:
                        main, sides = jnp.where(outer, main, 0.0), jnp.where(outer, sides, 0.0)
                    blocks.append(jnp.concatenate([main, sides], 1))
                across.append(
                    jnp.dot(
                        filter_y[a],
                        jnp.concatenate(blocks, 0),
                        precision=lax.Precision.HIGHEST,
                        preferred_element_type=jnp.float32,
                    )
                )
            turbulence[a] = jnp.dot(
                jnp.concatenate(across, 0),
                filter_z[a],
                precision=lax.Precision.HIGHEST,
                preferred_element_type=jnp.float32,
            )
        for k in range(WIDE):
            rows = pl.ds(2 * NY * k, 2 * NY)
            for q, value in enumerate(inflow([turbulence[a, rows] for a in range(3)])):
                flow[k, q] = value

    def inflow_at(step, q, form, packed):
        return flow[step % WIDE, q, form * NY : (form + 1) * NY, packed * NZ : (packed + 1) * NZ]

    def collide_inlet():
        blocked = post[0, WIDE + NX, PLACE[SOLID], 0]
        result = collide([inflow_at(1, q, 0, 0) for q in range(19)], blocked > 0.5, rates())
        for q, value in enumerate(result + [blocked]):
            if PLACE[q] >= 5:
                post[1, WIDE + NX, PLACE[q], 0] = value

    send_z[...] = jnp.zeros_like(send_z)
    loads[0].wait()
    for k in range(15):
        rate_tiles[k] = jnp.full((NY, NZ), rate[k] * (1.0 / NORMS[k]), jnp.float32)
    loads[1].wait()

    def first(x, carry):
        plane = pl.ds(x, 1)
        pltpu.make_async_copy(f_hbm.at[:, plane], f_in.at[:, plane], load_sem.at[x]).wait()
        collide_plane([f_in[q, x] for q in range(19)], x, 0)
        return carry

    lax.fori_loop(0, NX, first, 0, unroll=NX)
    loads[NX + 2].wait()
    loads[NX + 3].wait()
    pl.when(at_edge)(pack_noise)

    expected = jnp.where(at_inlet, len(LEVEL) + len(UP), len(NEIGHBOURS))
    pl.semaphore_wait(barrier, expected + jnp.where(at_edge, len(BEYOND), 0))

    @pl.when(at_outlet)
    def _():
        for offset in UP:
            greet(offset, ready_sem)

    @pl.when(at_edge)
    def _():
        for copy in noise_copies(0):
            copy.start()

    for half in range(HALVES):
        send_faces(half)

        @pl.when(at_edge)
        def _():
            if half == 0:
                for copy in noise_copies(1):
                    copy.start()
                make_filters()
            else:
                pl.when(at_outlet)(collide_inlet)
            filter_steps(half)

        await_faces(half, SHORT)
        unpack(half)
        await_faces(half, LONG)

        step = WIDE * half

        def around(plane, edge=None):
            index = plane - 1
            f = stream_plane(
                plane,
                lambda source, q, form: post[half, source, PLACE[q], form],
                lambda q, form: side[PLACE[q], form],
                True,
            )
            for form in range(2):
                f_form = f[form]
                if edge is not None:
                    f_form = [
                        jnp.where(edge, inflow_at(step, q, form, 0), f_form[q]) for q in range(19)
                    ]
                result = collide(f_form, post[half, plane, PLACE[SOLID], form] > 0.5, rates())
                for q in range(19):
                    later[index, q, form] = result[q]

        def between(plane, carry):
            around(plane)
            return carry

        around(1)
        around(WIDE, at_inlet)
        lax.fori_loop(WIDE + 1, WIDE + NX, between, 0, unroll=3)
        around(WIDE + NX, at_outlet)
        f = stream_side(half)
        edge_plane = jnp.where(at_inlet, WIDE, WIDE + NX)
        set_here = jnp.logical_and(at_edge, (lane >> 2) == edge_plane)
        for form in range(2):
            f_form = [
                jnp.where(set_here, inflow_at(step, q, form, 1), f[form][q]) for q in range(19)
            ]
            result = collide(f_form, side[PLACE[SOLID], form] > 0.5, rates())
            for q in range(19):
                later_side[q, form] = result[q]

        step = WIDE * half + 1

        def own(x, carry):
            f = stream_plane(
                x + WIDE,
                lambda source, q, form: later[source - 1, q, form],
                lambda q, form: later_side[q, form],
                False,
            )[0]
            set_here = jnp.logical_and(at_inlet, x == 0)
            f = [jnp.where(set_here, inflow_at(step, q, 0, 0), f[q]) for q in range(19)]
            if half + 1 < HALVES:
                collide_plane(f, x, half + 1)
            else:
                for q in range(19):
                    out[q, x] = f[q]
            return carry

        lax.fori_loop(0, NX, own, 0, unroll=NX)

    @pl.when(at_inlet)
    def _():
        await_rows(HALVES * OTHER_ROWS - KNOWN_ROWS, send_sem.at[0])

    @pl.when(jnp.logical_not(at_inlet))
    def _():
        await_rows(HALVES * OTHER_ROWS, send_sem.at[0])

    @pl.when(jnp.logical_not(at_outlet))
    def _():
        await_rows(HALVES * UP_ROWS, send_sem.at[2])

    @pl.when(at_edge)
    def _():
        await_rows(sum(NOISE_ROWS), send_sem.at[1])


def solution(mesh):
    counts = tuple(mesh.shape[axis] for axis in AXES)
    tile = (NY, NZ)

    def local(populations_in, relax_rates, solid_mask, noise_slabs, half_widths):
        operands = (populations_in, relax_rates, solid_mask, noise_slabs, half_widths.T)
        return pl.pallas_call(
            functools.partial(kernel, counts),
            name="lattice_steps",
            out_shape=jax.ShapeDtypeStruct(populations_in.shape, jnp.float32),
            in_specs=[pl.BlockSpec(memory_space=pltpu.HBM)] * 5,
            out_specs=pl.BlockSpec(memory_space=pltpu.VMEM),
            scratch_shapes=[
                pltpu.VMEM((19, NX) + tile, jnp.float32),
                pltpu.SMEM((15,), jnp.float32),
                pltpu.VMEM((15,) + tile, jnp.float32),
                pltpu.VMEM((NX,) + tile, jnp.int32),
                pltpu.VMEM((4, STEPS, 3) + tile, jnp.float32),
                pltpu.VMEM((2,) + tile, jnp.float32),
                pltpu.VMEM((4, 2) + tile, jnp.float32),
                pltpu.SMEM((2, 3), jnp.int32),
                pltpu.VMEM((HALVES, PLANES, 20, 2) + tile, jnp.float32),
                pltpu.VMEM((20, 2) + tile, jnp.float32),
                pltpu.VMEM((PLANES - 2, 19, 2) + tile, jnp.float32),
                pltpu.VMEM((19, 2) + tile, jnp.float32),
                pltpu.VMEM((HALVES, 2) + tile, jnp.float32),
                pltpu.VMEM((HALVES, 3, 2, 2) + tile, jnp.float32),
                pltpu.VMEM((3, 2 * NY, 4 * NY), jnp.float32),
                pltpu.VMEM((3, 2 * NZ, 2 * NZ), jnp.float32),
                pltpu.VMEM((3, WIDE * 2 * NY, 2 * NZ), jnp.float32),
                pltpu.VMEM((WIDE, 19, 2 * NY, 2 * NZ), jnp.float32),
                pltpu.SemaphoreType.DMA((NX + 4,)),
                pltpu.SemaphoreType.DMA((3,)),
                pltpu.SemaphoreType.DMA((HALVES, 2)),
                pltpu.SemaphoreType.DMA((HALVES, 2)),
                pltpu.SemaphoreType.DMA((HALVES,)),
                pltpu.SemaphoreType.REGULAR,
                pltpu.VMEM((HALVES * OTHER_ROWS, NZ), jnp.float32),
            ],
            compiler_params=pltpu.CompilerParams(
                collective_id=0, has_side_effects=True, vmem_limit_bytes=32 << 20
            ),
        )(*[pltpu.with_memory_space_constraint(x, pltpu.HBM) for x in operands])

    return jax.shard_map(
        local,
        mesh=mesh,
        in_specs=(
            P(None, "gx", "gy", "gz"),
            P(),
            P("gx", "gy", "gz"),
            P(None, None, "gy", "gz"),
            P(),
        ),
        out_specs=P(None, "gx", "gy", "gz"),
        check_vma=False,
    )
```

```python
import functools
import itertools

import jax
import jax.numpy as jnp
from jax import lax
from jax.experimental import pallas as pl
from jax.experimental.pallas import tpu as pltpu
from jax.sharding import PartitionSpec as P

MESH = pl.DeviceIdType.MESH
AXES = ("gx", "gy", "gz")
FILT = 8
STEPS = 4
NX, NY, NZ = 4, 8, 128
UNROLL = 6
VELOCITY = [
    (0, 0, 0),
    (1, 0, 0),
    (-1, 0, 0),
    (0, 1, 0),
    (0, -1, 0),
    (0, 0, 1),
    (0, 0, -1),
    (1, 1, 0),
    (-1, -1, 0),
    (1, -1, 0),
    (-1, 1, 0),
    (1, 0, 1),
    (-1, 0, -1),
    (1, 0, -1),
    (-1, 0, 1),
    (0, 1, 1),
    (0, -1, -1),
    (0, 1, -1),
    (0, -1, 1),
]
OPPOSITE = [0] + [q + 1 if q % 2 == 1 else q - 1 for q in range(1, 19)]
NORMS = (2394.0, 12.0, 36.0, 4.0, 4.0, 4.0, 40.0, 40.0, 40.0, 8.0, 8.0, 8.0, 252.0, 24.0, 72.0)
SOLID = 19
ORDER = sorted(range(20), key=lambda q: (tuple(-c for c in (VELOCITY + [(0, 0, 0)])[q][:2]), q))
PLACE = [ORDER.index(q) for q in range(20)]
WIDE = 2
HALVES = STEPS // WIDE
PLANES = NX + 2 * WIDE
RISING, SINKING = ([q for q in range(19) if VELOCITY[q][2] == step] for step in (1, -1))
STAYING = [q for q in range(19) if VELOCITY[q][2] == 0] + [SOLID]
NEIGHBOURS = sorted(
    (d for d in itertools.product((-1, 0, 1), repeat=3) if any(d)),
    key=lambda d: -sum(map(abs, d)),
)
LEVEL, UP, DOWN = ([d for d in NEIGHBOURS if d[0] == step] for step in (0, 1, -1))
STRAIGHT = (-1, 0, 0)
ACROSS = [d for d in itertools.product((0,), (-1, 0, 1, 2), (-1, 0, 1)) if any(d)]
BEYOND = [d for d in ACROSS if d[1] == 2]


def pieces(offset):
    dx, dy, dz = offset
    if dz:
        return [(0, NY) if not dy else (NY - WIDE, WIDE) if dy > 0 else (0, WIDE)]
    near_row, far_row = ((0, NY), None) if not dy else ((7, 1), (6, 1)) if dy > 0 else ((0, 1), (1, 1))
    if dx > 0:
        whole = [
            [[(0, 15)], []],
            [[(0, 12)], [(0, 1), (5, 3)]],
            [[(1, 4), (8, 7)], [(4, 1), (12, 3)]],
        ][dy]
        half = [[[(0, 5)], []], [[(0, 4)], [(0, 1)]], [[(1, 4)], [(4, 1)]]][dy]
        planes = [(5, 1, 1, whole), (4, 1, 0, half)]
    elif dx < 0:
        whole = [
            [[(5, 15)], []],
            [[(5, 7), (15, 4)], [(5, 3), (15, 1)]],
            [[(8, 12)], [(12, 3), (19, 1)]],
        ][dy]
        half = [[[(15, 5)], []], [[(15, 4)], [(15, 1)]], [[(16, 4)], [(19, 1)]]][dy]
        planes = [(2, 1, 6, whole), (3, 1, 7, half)]
    elif dy > 0:
        planes = [(2, NX, 2, [[(0, 12), (15, 4)], [(0, 1), (5, 3), (15, 1)]])]
    else:
        planes = [(2, NX, 2, [[(1, 4), (8, 12)], [(4, 1), (12, 3), (19, 1)]])]
    return [
        (first, number, array, arrays, there, rows)
        for first, number, there, ranges in planes
        for rows, parts in zip((near_row, far_row), ranges)
        for array, arrays in parts
    ]


def rows_of(offsets):
    return sum(
        piece[1] if len(piece) == 2 else piece[1] * piece[3] * piece[5][1]
        for offset in offsets
        for piece in pieces(offset)
    )


SHORT, LONG = ([d for d in NEIGHBOURS if (d[2] != 0) == short] for short in (True, False))
UP_ROWS = rows_of(UP)
OTHER_ROWS = rows_of(LEVEL + DOWN)


def received(offsets, kind):
    return rows_of([d for d in offsets if d in kind])


REACH = 10
KNOWN_ROWS = 15 * NY
NOISE_Y_ROWS = WIDE * 3 * (2 * NY + 2)
NOISE_ROWS = [6 * NY + 2 * 2 + NOISE_Y_ROWS, NOISE_Y_ROWS]


def neighbour(here, counts, offset):
    return tuple(
        lax.rem(place + step + count, count) if step else place
        for place, step, count in zip(here, offset, counts)
    )


def collide(f, solid, rate):
    total = {q: f[q] + f[q + 1] for q in range(1, 19, 2)}
    apart = {q: f[q] - f[q + 1] for q in range(1, 19, 2)}
    p_xy, p_xz, p_yz = total[7] + total[9], total[11] + total[13], total[15] + total[17]
    q_xy, q_xz, q_yz = total[7] - total[9], total[11] - total[13], total[15] - total[17]
    a_xy, b_xy = apart[7] + apart[9], apart[7] - apart[9]
    a_xz, b_xz = apart[11] + apart[13], apart[11] - apart[13]
    a_yz, b_yz = apart[15] + apart[17], apart[15] - apart[17]
    axis_sum = total[1] + total[3] + total[5]
    edge_sum = p_xy + p_xz + p_yz
    rho = f[0] + axis_sum + edge_sum
    far_x, far_y, far_z = a_xy + a_xz, b_xy + a_yz, b_xz + b_yz
    j_x, j_y, j_z = apart[1] + far_x, apart[3] + far_y, apart[5] + far_z
    inverse = 1.0 / rho
    u_x, u_y, u_z = j_x * inverse, j_y * inverse, j_z * inverse
    xx, yy, zz = j_x * u_x, j_y * u_y, j_z * u_z
    square = xx + yy + zz
    normal_xy, normal_z = xx - yy, 2.0 * zz - xx - yy

    def relax(which, value):
        return rate[which] * value

    axis_xy, edge_xy = total[1] - total[3], p_xz - p_yz
    axis_z = 2.0 * total[5] - total[1] - total[3]
    edge_z = p_xz + p_yz - 2.0 * p_xy
    m4 = relax(0, 8.0 * edge_sum - 11.0 * axis_sum - 30.0 * f[0] + 11.0 * rho - 19.0 * square)
    m5 = relax(1, axis_xy + edge_xy - normal_xy)
    m6 = relax(2, axis_z + edge_z - normal_z)
    m7 = relax(3, q_xy - j_x * u_y)
    m8 = relax(4, q_yz - j_y * u_z)
    m9 = relax(5, q_xz - j_x * u_z)
    m10 = relax(6, far_x - 4.0 * apart[1] + (2.0 / 3.0) * j_x)
    m11 = relax(7, far_y - 4.0 * apart[3] + (2.0 / 3.0) * j_y)
    m12 = relax(8, far_z - 4.0 * apart[5] + (2.0 / 3.0) * j_z)
    m13 = relax(9, a_xy - a_xz)
    m14 = relax(10, a_yz - b_xy)
    m15 = relax(11, b_xz - b_yz)
    m16 = relax(12, 12.0 * f[0] - 4.0 * axis_sum + edge_sum - 3.0 * rho + 5.5 * square)
    m17 = relax(13, edge_xy - 2.0 * axis_xy + 0.5 * normal_xy)
    m18 = relax(14, edge_z - 2.0 * axis_z + 0.5 * normal_z)

    axis_base = -11.0 * m4 - 4.0 * m16
    edge_base = 8.0 * m4 + m16
    v5, v6 = m5 - 2.0 * m17, m6 - 2.0 * m18
    w5, w6 = m5 + m17, m6 + m18
    e_xy, e_xz, e_yz = edge_base - 2.0 * w6, edge_base + w5 + w6, edge_base - w5 + w6
    even = {
        1: axis_base + v5 - v6,
        3: axis_base - v5 - v6,
        5: axis_base + 2.0 * v6,
        7: e_xy + m7,
        9: e_xy - m7,
        11: e_xz + m9,
        13: e_xz - m9,
        15: e_yz + m8,
        17: e_yz - m8,
    }
    s_xy, t_xy = m10 + m13, m11 - m14
    s_xz, t_xz = m10 - m13, m12 + m15
    s_yz, t_yz = m11 + m14, m12 - m15
    odd = {
        1: -4.0 * m10,
        3: -4.0 * m11,
        5: -4.0 * m12,
        7: s_xy + t_xy,
        9: s_xy - t_xy,
        11: s_xz + t_xz,
        13: s_xz - t_xz,
        15: s_yz + t_yz,
        17: s_yz - t_yz,
    }
    post = [f[0] + 30.0 * m4 - 12.0 * m16]
    for q in range(1, 19, 2):
        post.append(f[q] - even[q] - odd[q])
        post.append(f[q + 1] - even[q] + odd[q])
    return [jnp.where(solid, f[OPPOSITE[q]], post[q]) for q in range(19)]


def inflow(turbulence):
    u = [0.05 + 0.05 * turbulence[0], 0.05 * turbulence[1], 0.05 * turbulence[2]]
    speed = 1.0 - 1.5 * (u[0] * u[0] + u[1] * u[1] + u[2] * u[2])
    result = []
    for q in range(19):
        weight = (1.0 / 3.0, 1.0 / 18.0, 1.0 / 36.0)[sum(map(abs, VELOCITY[q]))]
        along = None
        for step, part in zip(VELOCITY[q], u):
            if step:
                part = part if step > 0 else -part
                along = part if along is None else along + part
        result.append(weight * (speed if along is None else speed + along * (3.0 + 4.5 * along)))
    return result


def tap(offset, half_width):
    spread = half_width.astype(jnp.float32)
    reach = offset.astype(jnp.float32)
    value = jnp.exp(reach * reach * (-jnp.pi / (2.0 * (spread * spread))))
    return jnp.where(jnp.abs(reach) <= 2.0 * spread, value, 0.0)


def tap_norm(half_width):
    offset = lax.broadcasted_iota(jnp.int32, (8, 128), 1) - FILT
    value = jnp.where(offset <= FILT, tap(offset, half_width), 0.0)
    return 1.0 / jnp.sqrt(jnp.sum(value * value, axis=1, keepdims=True))[0:1]


def kernel(
    counts,
    f_hbm,
    rate_hbm,
    solid_hbm,
    noise_hbm,
    width_hbm,
    out,
    f_in,
    rate,
    rate_tiles,
    solid,
    noise,
    noise_z,
    noise_side,
    width,
    post,
    side,
    later,
    later_side,
    send_z,
    from_z,
    filter_y,
    filter_z,
    turbulence,
    flow,
    load_sem,
    send_sem,
    recv_sem,
    recv_up,
    noise_recv,
    ready_sem,
    ruler,
):
    here = tuple(lax.axis_index(axis) for axis in AXES)
    at_inlet = here[0] == 0
    at_outlet = here[0] == counts[0] - 1
    at_edge = jnp.logical_or(at_inlet, at_outlet)
    barrier = pltpu.get_barrier_semaphore()

    def greet(offset, semaphore=barrier):
        pl.semaphore_signal(
            semaphore, inc=1, device_id=neighbour(here, counts, offset), device_id_type=MESH
        )

    for offset in DOWN + LEVEL:
        greet(offset)

    @pl.when(jnp.logical_not(at_outlet))
    def _():
        for offset in UP:
            greet(offset)

    @pl.when(at_edge)
    def _():
        for offset in BEYOND:
            greet(offset)

    loads = [pltpu.make_async_copy(rate_hbm, rate, load_sem.at[NX])]
    loads.append(pltpu.make_async_copy(solid_hbm, solid, load_sem.at[NX + 1]))
    for x in range(NX):
        plane = pl.ds(x, 1)
        loads.append(pltpu.make_async_copy(f_hbm.at[:, plane], f_in.at[:, plane], load_sem.at[x]))
    loads.append(pltpu.make_async_copy(width_hbm, width, load_sem.at[NX + 2]))
    loads.append(pltpu.make_async_copy(noise_hbm, noise.at[1], load_sem.at[NX + 3]))
    for load in loads:
        load.start()

    row = lax.broadcasted_iota(jnp.int32, (NY, NZ), 0)
    lane = lax.broadcasted_iota(jnp.int32, (NY, NZ), 1)
    quarter = lane & 3

    def spin(value, amount, axis=1):
        amount = amount % value.shape[axis]
        return pltpu.roll(value, amount, axis) if amount else value

    def await_rows(rows, semaphore):
        span = ruler.at[pl.ds(0, rows)]
        pltpu.make_async_copy(span, span, semaphore).wait()

    def face_copies(half, offsets, known=0):
        copies = []
        for offset in offsets:
            dx, dy, dz = offset
            form = 1 if dy else 0
            for piece in pieces(offset)[known:]:
                if dz:
                    rows = pl.ds(*piece)
                    source = send_z.at[half, 0 if dz > 0 else 1, rows]
                    target = from_z.at[half, 1 - dx, 0 if dz > 0 else 1, form, rows]
                else:
                    first, number, array, arrays, there, rows = piece
                    array, rows = pl.ds(array, arrays), pl.ds(*rows)
                    source = post.at[half, pl.ds(first, number), array, 0, rows]
                    target = post.at[half, pl.ds(there, number), array, form, rows]
                copies.append(
                    pltpu.make_async_remote_copy(
                        src_ref=source,
                        dst_ref=target,
                        send_sem=send_sem.at[2 if dx > 0 else 0],
                        recv_sem=(recv_up if dx > 0 else recv_sem).at[half, 0 if dz else 2 if dx < 0 else 1],
                        device_id=neighbour(here, counts, offset),
                        device_id_type=MESH,
                    )
                )
        return copies

    def noise_copies(half):
        copies = []
        for offset in ACROSS:
            dy, dz = offset[1:]
            block, direction = (1 - dy) % 4, 0 if dz > 0 else 1
            steps = pl.ds(WIDE * half, WIDE)
            if dz and half:
                continue
            for rows in [(0, 1), (NY - 1, 1)] if offset in BEYOND else [(0, NY)]:
                rows = pl.ds(*rows)
                copies.append(
                    pltpu.make_async_remote_copy(
                        src_ref=noise_z.at[direction, rows] if dz else noise.at[1, steps, :, rows],
                        dst_ref=noise_side.at[block, direction, rows]
                        if dz
                        else noise.at[block, steps, :, rows],
                        send_sem=send_sem.at[1],
                        recv_sem=noise_recv.at[half],
                        device_id=neighbour(here, counts, offset),
                        device_id_type=MESH,
                    )
                )
        return copies

    def pack_noise():
        above, below = jnp.zeros((NY, NZ), jnp.float32), jnp.zeros((NY, NZ), jnp.float32)
        for k in range(3 * STEPS):
            place = REACH * k
            mine = jnp.logical_and(lane >= place, lane < place + REACH)
            tile = noise[1, k // 3, k % 3]
            above = jnp.where(mine, spin(tile, place + REACH), above)
            below = jnp.where(mine, spin(tile, place), below)
        noise_z[0], noise_z[1] = above, below

    def send_faces(half):
        for kind in (SHORT, LONG):

            @pl.when(jnp.logical_not(at_outlet))
            def _():
                for copy in face_copies(half, [d for d in UP if d in kind]):
                    copy.start()

            @pl.when(jnp.logical_not(at_inlet))
            def _():
                for copy in face_copies(half, [d for d in DOWN if d in kind]):
                    copy.start()

            for copy in face_copies(half, [d for d in LEVEL if d in kind]):
                copy.start()
        if half == 1:

            @pl.when(at_inlet)
            def _():
                pl.semaphore_wait(ready_sem, len(DOWN))
                for late in range(2):
                    for kind in (SHORT, LONG):
                        offsets = [d for d in DOWN if d in kind and d != STRAIGHT]
                        for copy in face_copies(late, offsets):
                            copy.start()
                    for copy in face_copies(late, [STRAIGHT], late):
                        copy.start()

    def await_faces(half, kind):
        place = 0 if kind is SHORT else 1
        offsets = LEVEL + DOWN if kind is SHORT else LEVEL
        await_rows(received(offsets, kind), recv_sem.at[half, place])

        @pl.when(jnp.logical_not(at_inlet))
        def _():
            await_rows(received(UP, kind), recv_up.at[half, place])

    def await_faces_from_above(half):
        rows = received(DOWN, LONG)
        if half == 0:
            await_rows(rows, recv_sem.at[half, 2])
        else:

            @pl.when(at_outlet)
            def _():
                await_rows(rows - KNOWN_ROWS, recv_sem.at[half, 2])

            @pl.when(jnp.logical_not(at_outlet))
            def _():
                await_rows(rows, recv_sem.at[half, 2])

    def rates():
        return [rate_tiles[k] for k in range(15)]

    def collide_plane(f, x, half):
        blocked = solid[x] > 0
        result = collide(f, blocked, rates()) + [jnp.where(blocked, 1.0, 0.0)]
        for q in range(20):
            post[half, x + WIDE, PLACE[q], 0] = result[q]
        above, below = send_z[half, 0], send_z[half, 1]
        for k in range(5):
            place = 16 * k + 4 * x
            moved = pltpu.roll(result[RISING[k]], place + 4, 1)
            above = jnp.where(jnp.logical_or(lane == place + 2, lane == place + 3), moved, above)
            moved = pltpu.roll(result[SINKING[k]], place, 1)
            below = jnp.where(jnp.logical_or(lane == place, lane == place + 1), moved, below)
        for k in range(10):
            place = 16 * (k // 2) + 4 * x + k % 2
            above = jnp.where(lane == place, pltpu.roll(result[STAYING[k]], place + 1, 1), above)
            place = place + 2
            below = jnp.where(lane == place, pltpu.roll(result[STAYING[k]], place, 1), below)
        send_z[half, 0], send_z[half, 1] = above, below

    def unpack(half):
        for form in range(2):
            pairs, lone = [], ([], [])
            for block in range(3):
                low, high = from_z[half, block, 0, form], from_z[half, block, 1, form]
                pairs.append(jnp.where(quarter >= 2, low, high))
                for k in range(2):
                    lone[k].append(jnp.where(quarter == 3, spin(low, 3 - k), spin(high, -2 - k)))

            def spread(tiles, slot):
                below, own, above = (
                    spin(tile, shift - 16 * slot) for tile, shift in zip(tiles, (-8, 8, 24))
                )
                return jnp.where(lane < 8, below, jnp.where(lane < 24, own, above))

            for k in range(5):
                tile = spread(pairs, k)
                side[PLACE[RISING[k]], form] = tile
                side[PLACE[SINKING[k]], form] = tile
            for k in range(10):
                side[PLACE[STAYING[k]], form] = spread(lone[k % 2], k // 2)

    def column(tile, plane, step_z):
        amount = (0 if step_z > 0 else NZ - 1) + 2 * NZ - (4 * plane + (3 if step_z > 0 else 0))
        return pltpu.roll(tile, lax.rem(amount, NZ), 1)

    def exchange_rows(main, edge, step_y):
        main, edge = spin(main, step_y, 0), spin(edge, step_y, 0)
        swap = row == (0 if step_y > 0 else NY - 1)
        return jnp.where(swap, edge, main), jnp.where(swap, main, edge)

    def stream_plane(plane, planes_of, sides_of, both):
        result = [[], []]
        for q in range(19):
            step_x, step_y, step_z = VELOCITY[q]
            source = plane - step_x
            forms = [0, 1] if both or step_y else [0]
            value = [planes_of(source, q, form) for form in forms]
            if step_z:
                enters = lane == (0 if step_z > 0 else NZ - 1)
                value = [
                    jnp.where(enters, column(sides_of(q, form), source, step_z), spin(value[form], step_z))
                    for form in forms
                ]
            if step_y:
                value = exchange_rows(value[0], value[1], step_y)
            result[0].append(value[0])
            if both:
                result[1].append(value[1])
        return result

    def stream_side(half):
        result = [[], []]
        for q in range(19):
            step_x, step_y, step_z = VELOCITY[q]
            value = []
            for form in range(2):
                moved = spin(side[PLACE[q], form], 4 * step_x + step_z)
                if step_z:
                    place, origin = (0, NZ - 1) if step_z > 0 else (3, 0)
                    outer = None
                    for plane in range(1, PLANES - 1):
                        source = plane - step_x
                        taken = spin(post[half, source, PLACE[q], form], 4 * plane + place - origin)
                        outer = taken if outer is None else jnp.where(lane >= 4 * plane, taken, outer)
                    moved = jnp.where(quarter == place, outer, moved)
                value.append(moved)
            if step_y:
                value = exchange_rows(value[0], value[1], step_y)
            for form in range(2):
                result[form].append(value[form])
        return result

    def make_filters():
        def component(a, carry):
            index = lax.broadcasted_iota(jnp.int32, (2 * NY, 4 * NY), 0)
            node = jnp.where(index < NY + 4, index, index - 2 * NY)
            node = jnp.where(jnp.logical_and(index >= NY, index < NY + 4), index, node)
            reach_y = lax.broadcasted_iota(jnp.int32, (2 * NY, 4 * NY), 1) - NY - node
            reach_y = jnp.where(reach_y > 2 * NY - 1, reach_y - 4 * NY, reach_y)
            filter_y[a] = tap(reach_y, width[0, a]) * tap_norm(width[0, a])
            index = lax.broadcasted_iota(jnp.int32, (2 * NZ, 2 * NZ), 1)
            part = index & 3
            node = jnp.where(index < NZ, index, jnp.where(part < 2, part + NZ, part - 4))
            index = lax.broadcasted_iota(jnp.int32, (2 * NZ, 2 * NZ), 0)
            part = index - NZ
            origin = jnp.where(part < 2 * REACH, part + NZ - REACH, 8 * NZ)
            origin = jnp.where(part < REACH, part - REACH, origin)
            reach_z = jnp.where(part < 0, index, origin) - node
            filter_z[a] = tap(reach_z, width[1, a]) * tap_norm(width[1, a])
            return carry

        lax.fori_loop(0, 3, component, 0)

    def filter_steps(half):
        await_rows(NOISE_ROWS[half], noise_recv.at[half])
        outer = jnp.logical_or(row == 0, row == NY - 1)
        for a in range(3):
            across = []
            for step in range(WIDE * half, WIDE * half + WIDE):
                place = REACH * (3 * step + a)
                blocks = []
                for b in range(4):
                    main = noise[b, step, a]
                    sides = jnp.where(
                        lane < REACH,
                        spin(noise_side[b, 0], -place),
                        spin(noise_side[b, 1], REACH - place),
                    )
                    if b == 3:
                        main, sides = jnp.where(outer, main, 0.0), jnp.where(outer, sides, 0.0)
                    blocks.append(jnp.concatenate([main, sides], 1))
                across.append(
                    jnp.dot(
                        filter_y[a],
                        jnp.concatenate(blocks, 0),
                        precision=lax.Precision.HIGHEST,
                        preferred_element_type=jnp.float32,
                    )
                )
            turbulence[a] = jnp.dot(
                jnp.concatenate(across, 0),
                filter_z[a],
                precision=lax.Precision.HIGHEST,
                preferred_element_type=jnp.float32,
            )
        for k in range(WIDE):
            rows = pl.ds(2 * NY * k, 2 * NY)
            for q, value in enumerate(inflow([turbulence[a, rows] for a in range(3)])):
                flow[k, q] = value

    def inflow_at(step, q, form, packed):
        return flow[step % WIDE, q, form * NY : (form + 1) * NY, packed * NZ : (packed + 1) * NZ]

    def collide_inlet():
        blocked = post[0, WIDE + NX, PLACE[SOLID], 0]
        result = collide([inflow_at(1, q, 0, 0) for q in range(19)], blocked > 0.5, rates())
        for q, value in enumerate(result + [blocked]):
            if PLACE[q] >= 5:
                post[1, WIDE + NX, PLACE[q], 0] = value

    send_z[...] = jnp.zeros_like(send_z)
    loads[0].wait()
    for k in range(15):
        rate_tiles[k] = jnp.full((NY, NZ), rate[k] * (1.0 / NORMS[k]), jnp.float32)
    loads[1].wait()

    def first(x, carry):
        plane = pl.ds(x, 1)
        pltpu.make_async_copy(f_hbm.at[:, plane], f_in.at[:, plane], load_sem.at[x]).wait()
        collide_plane([f_in[q, x] for q in range(19)], x, 0)
        return carry

    lax.fori_loop(0, NX, first, 0, unroll=NX)
    loads[NX + 2].wait()
    loads[NX + 3].wait()
    pl.when(at_edge)(pack_noise)

    expected = jnp.where(at_inlet, len(LEVEL) + len(UP), len(NEIGHBOURS))
    pl.semaphore_wait(barrier, expected + jnp.where(at_edge, len(BEYOND), 0))

    @pl.when(at_outlet)
    def _():
        for offset in UP:
            greet(offset, ready_sem)

    @pl.when(at_edge)
    def _():
        for copy in noise_copies(0):
            copy.start()

    for half in range(HALVES):
        send_faces(half)

        @pl.when(at_edge)
        def _():
            if half == 0:
                for copy in noise_copies(1):
                    copy.start()
                make_filters()
            else:
                pl.when(at_outlet)(collide_inlet)
            filter_steps(half)

        await_faces(half, SHORT)
        unpack(half)
        await_faces(half, LONG)

        step = WIDE * half

        def around(plane, edge=None):
            index = plane - 1
            f = stream_plane(
                plane,
                lambda source, q, form: post[half, source, PLACE[q], form],
                lambda q, form: side[PLACE[q], form],
                True,
            )
            for form in range(2):
                f_form = f[form]
                if edge is not None:
                    f_form = [
                        jnp.where(edge, inflow_at(step, q, form, 0), f_form[q]) for q in range(19)
                    ]
                result = collide(f_form, post[half, plane, PLACE[SOLID], form] > 0.5, rates())
                for q in range(19):
                    later[index, q, form] = result[q]

        def between(plane, carry):
            around(plane)
            return carry

        around(1)
        around(WIDE, at_inlet)
        lax.fori_loop(WIDE + 1, WIDE + NX - 1, between, 0, unroll=2)
        await_faces_from_above(half)
        around(WIDE + NX - 1)
        around(WIDE + NX, at_outlet)
        f = stream_side(half)
        edge_plane = jnp.where(at_inlet, WIDE, WIDE + NX)
        set_here = jnp.logical_and(at_edge, (lane >> 2) == edge_plane)
        for form in range(2):
            f_form = [
                jnp.where(set_here, inflow_at(step, q, form, 1), f[form][q]) for q in range(19)
            ]
            result = collide(f_form, side[PLACE[SOLID], form] > 0.5, rates())
            for q in range(19):
                later_side[q, form] = result[q]

        step = WIDE * half + 1

        def own(x, carry):
            f = stream_plane(
                x + WIDE,
                lambda source, q, form: later[source - 1, q, form],
                lambda q, form: later_side[q, form],
                False,
            )[0]
            set_here = jnp.logical_and(at_inlet, x == 0)
            f = [jnp.where(set_here, inflow_at(step, q, 0, 0), f[q]) for q in range(19)]
            if half + 1 < HALVES:
                collide_plane(f, x, half + 1)
            else:
                for q in range(19):
                    out[q, x] = f[q]
            return carry

        lax.fori_loop(0, NX, own, 0, unroll=NX)

    @pl.when(at_inlet)
    def _():
        await_rows(HALVES * OTHER_ROWS - KNOWN_ROWS, send_sem.at[0])

    @pl.when(jnp.logical_not(at_inlet))
    def _():
        await_rows(HALVES * OTHER_ROWS, send_sem.at[0])

    @pl.when(jnp.logical_not(at_outlet))
    def _():
        await_rows(HALVES * UP_ROWS, send_sem.at[2])

    @pl.when(at_edge)
    def _():
        await_rows(sum(NOISE_ROWS), send_sem.at[1])


def solution(mesh):
    counts = tuple(mesh.shape[axis] for axis in AXES)
    tile = (NY, NZ)

    def local(populations_in, relax_rates, solid_mask, noise_slabs, half_widths):
        operands = (populations_in, relax_rates, solid_mask, noise_slabs, half_widths.T)
        return pl.pallas_call(
            functools.partial(kernel, counts),
            name="lattice_steps",
            out_shape=jax.ShapeDtypeStruct(populations_in.shape, jnp.float32),
            in_specs=[pl.BlockSpec(memory_space=pltpu.HBM)] * 5,
            out_specs=pl.BlockSpec(memory_space=pltpu.VMEM),
            scratch_shapes=[
                pltpu.VMEM((19, NX) + tile, jnp.float32),
                pltpu.SMEM((15,), jnp.float32),
                pltpu.VMEM((15,) + tile, jnp.float32),
                pltpu.VMEM((NX,) + tile, jnp.int32),
                pltpu.VMEM((4, STEPS, 3) + tile, jnp.float32),
                pltpu.VMEM((2,) + tile, jnp.float32),
                pltpu.VMEM((4, 2) + tile, jnp.float32),
                pltpu.SMEM((2, 3), jnp.int32),
                pltpu.VMEM((HALVES, PLANES, 20, 2) + tile, jnp.float32),
                pltpu.VMEM((20, 2) + tile, jnp.float32),
                pltpu.VMEM((PLANES - 2, 19, 2) + tile, jnp.float32),
                pltpu.VMEM((19, 2) + tile, jnp.float32),
                pltpu.VMEM((HALVES, 2) + tile, jnp.float32),
                pltpu.VMEM((HALVES, 3, 2, 2) + tile, jnp.float32),
                pltpu.VMEM((3, 2 * NY, 4 * NY), jnp.float32),
                pltpu.VMEM((3, 2 * NZ, 2 * NZ), jnp.float32),
                pltpu.VMEM((3, WIDE * 2 * NY, 2 * NZ), jnp.float32),
                pltpu.VMEM((WIDE, 19, 2 * NY, 2 * NZ), jnp.float32),
                pltpu.SemaphoreType.DMA((NX + 4,)),
                pltpu.SemaphoreType.DMA((3,)),
                pltpu.SemaphoreType.DMA((HALVES, 3)),
                pltpu.SemaphoreType.DMA((HALVES, 2)),
                pltpu.SemaphoreType.DMA((HALVES,)),
                pltpu.SemaphoreType.REGULAR,
                pltpu.VMEM((HALVES * OTHER_ROWS, NZ), jnp.float32),
            ],
            compiler_params=pltpu.CompilerParams(
                collective_id=0, has_side_effects=True, vmem_limit_bytes=32 << 20
            ),
        )(*[pltpu.with_memory_space_constraint(x, pltpu.HBM) for x in operands])

    return jax.shard_map(
        local,
        mesh=mesh,
        in_specs=(
            P(None, "gx", "gy", "gz"),
            P(),
            P("gx", "gy", "gz"),
            P(None, None, "gy", "gz"),
            P(),
        ),
        out_specs=P(None, "gx", "gy", "gz"),
        check_vma=False,
    )
```
